128 devices in a mesh: rec: 8 (over z, core), seq: 16 (over y, x).
Axes of the slice: x: 4, y: 4, z: 4, core: 2. Of those that a mesh axis runs over, the one named last changes fastest.
Arguments:
- tokens: bfloat16 [8, 4096, 768], P('rec', 'seq'), may hold values from -6 to 6
- cotangent: bfloat16 [8, 4096, 768], P('rec', 'seq'), may hold values from -6 to 6
- log_decay: float32 [8, 24, 4096], P('rec', None, 'seq'), may hold values from -0.8 to 0
- w_in: bfloat16 [768, 1536], replicated, may hold values from -0.21875 to 0.21875
- w_bc: bfloat16 [768, 256], replicated, may hold values from -0.009765625 to 0.009765625
- w_out: bfloat16 [1536, 768], replicated, may hold values from -0.15625 to 0.15625
Outputs:
- d_tokens: bfloat16 [8, 4096, 768], P('rec', 'seq')
- grad_in: float32 [768, 1536], P(('rec', 'seq'))
- grad_bc: float32 [768, 256], P(('rec', 'seq'))
- grad_out: float32 [1536, 768], P(('rec', 'seq'))
The draws below stay inside these ranges and needn't reach their ends.
All inputs are finite; a program needn't handle non-finite values.
Results may differ from the reference program's by a relative error of at most 0.0085.
Values sent between devices are 32-bit elements; how exact they have to be, the bound alone decides.
No kernel may reach another device: no remote copies, remote signals or barrier semaphores. Data moves between devices by JAX's collectives and lax.ppermute only.
A program may use at most 256 MiB of HBM per device.

```python
import jax
import jax.numpy as jnp
from jax import lax

D = 768
HEADS = 24
HEAD_DIM = 64
NSTATE = 128
BLOCK = 128
TOKENS_PER_SHARD = 256
LENGTH = 4096
RECS = 8
N_SEQ = 16


def draw_log_decay(key, part):
    keys = jax.random.split(key, 6)
    share = 0.3
    quick = jax.random.uniform(keys[0], (RECS, HEADS, 1)) < share
    fast_decay_rate = -jax.random.uniform(keys[1], (RECS, HEADS, 1), minval=0.02, maxval=0.035)
    slow_rate = -jax.random.uniform(keys[2], (RECS, HEADS, 1), minval=1e-05, maxval=0.0001)
    starting_index = jnp.where(quick, fast_decay_rate, slow_rate)
    approximate_guess = jnp.exp(jax.random.uniform(keys[3], (RECS, HEADS, LENGTH), minval=-0.7, maxval=0.7))
    element_indices = jax.random.randint(keys[4], (RECS, 3, 1), 0, LENGTH)
    segment_locations = jnp.arange(LENGTH)[None, None, :]
    sample_group_items = jnp.any(segment_locations == element_indices, axis=1)
    amplitude_level = -jax.random.uniform(keys[5], (RECS, 1, LENGTH), minval=0.22, maxval=0.69)
    return (starting_index * approximate_guess + jnp.where(sample_group_items[:, None, :], amplitude_level, 0.0)).astype(jnp.float32)


def block_scale(rng, shape, cuts, smallest, high):
    def one(dim, blocks):
        steps = jax.random.uniform(jax.random.fold_in(jax.random.fold_in(rng, 6), dim), (blocks,), jnp.float32, smallest / len(cuts), high / len(cuts))
        return jnp.repeat(jnp.exp(steps), shape[dim] // blocks).reshape((-1,) + (1,) * (len(shape) - dim - 1))

    loudness = one(*cuts[0])
    for cut in cuts[1:]:
        loudness = loudness * one(*cut)
    return loudness


def gaussian(rng, shape, spread, reach, pieces=(), kind=jnp.bfloat16):
    gain = block_scale(rng, shape, pieces, -0.22, 0.18) if pieces else 1.0
    values = jax.random.normal(rng, shape, jnp.float32) * spread * gain
    return jnp.minimum(jnp.maximum(values, -reach), reach).astype(kind)


def setup_inputs(seed: int = 0) -> dict:
    arg_keys = jax.random.split(jax.random.key(seed), 7)
    return {
        "tokens": gaussian(arg_keys[0], (RECS, LENGTH, D), 1.0, 6.0, ((0, 8), (1, 16))),
        "cotangent": gaussian(arg_keys[1], (RECS, LENGTH, D), 1.0, 6.0, ((0, 8), (1, 16))),
        "log_decay": draw_log_decay(jax.random.fold_in(arg_keys[6], 71), 0),
        "w_in": gaussian(arg_keys[3], (D, HEADS * HEAD_DIM), D ** -0.5, 0.21875),
        "w_bc": gaussian(arg_keys[4], (D, 2 * NSTATE), (D * TOKENS_PER_SHARD * N_SEQ // 8) ** -0.5, 0.009765625),
        "w_out": gaussian(arg_keys[5], (HEADS * HEAD_DIM, D), (HEADS * HEAD_DIM) ** -0.5, 0.15625),
    }


def ssd_block(state, segment_list):
    xs_b, b_b, c_b, la_b = segment_list
    width = la_b.shape[1]
    cum = jnp.cumsum(la_b, axis=1)
    diff = cum[:, :, None] - cum[:, None, :]
    lower = jnp.tril(jnp.ones((width, width), dtype=bool))
    decay = jnp.where(lower, jnp.exp(jnp.where(lower, diff, 0.0)), 0.0)
    scores = jnp.dot(c_b, b_b.T, precision=lax.Precision.HIGHEST)
    y_inner = jnp.einsum('hts,shp->thp', decay * scores[None], xs_b, precision=lax.Precision.HIGHEST)
    y_carry = jnp.einsum('tn,hnp->thp', c_b, state, precision=lax.Precision.HIGHEST) * jnp.exp(cum).T[:, :, None]
    tail = jnp.exp(cum[:, -1:] - cum)
    new_state = jnp.exp(cum[:, -1])[:, None, None] * state + jnp.einsum('sn,shp->hnp', b_b, xs_b * tail.T[:, :, None], precision=lax.Precision.HIGHEST)
    return (new_state, y_inner + y_carry)

def ssd_pass(xs3, bmat, cmat, decay_log, state):
    count = xs3.shape[0] // BLOCK
    blocks = (xs3.reshape(count, BLOCK, xs3.shape[1], xs3.shape[2]), bmat.reshape(count, BLOCK, bmat.shape[1]), cmat.reshape(count, BLOCK, cmat.shape[1]), decay_log.reshape(decay_log.shape[0], count, BLOCK).transpose(1, 0, 2))
    final, ys = lax.scan(ssd_block, state, blocks)
    return (ys.reshape(xs3.shape), final)

def one_record(items, w_in, w_bc, w_out):
    tok, grad_y, decay_log = items
    xs = jnp.dot(tok, w_in, preferred_element_type=jnp.float32).astype(jnp.bfloat16)
    bc = jnp.dot(tok, w_bc, preferred_element_type=jnp.float32).astype(jnp.bfloat16)
    xs3 = xs.astype(jnp.float32).reshape(LENGTH, HEADS, HEAD_DIM)
    bmat = bc[:, :NSTATE].astype(jnp.float32)
    cmat = bc[:, NSTATE:].astype(jnp.float32)
    dy3 = jnp.dot(grad_y, w_out.T, preferred_element_type=jnp.float32).reshape(LENGTH, HEADS, HEAD_DIM)
    zero_state = jnp.zeros((HEADS, NSTATE, HEAD_DIM), jnp.float32)

    def mixer(xs_a, b_a, c_a):
        y_fwd, _ = ssd_pass(xs_a, b_a, c_a, decay_log, zero_state)
        y_rev, _ = ssd_pass(xs_a[::-1], b_a[::-1], c_a[::-1], decay_log[:, ::-1], zero_state)
        return y_fwd + y_rev[::-1]
    yfull, pullback = jax.vjp(mixer, xs3, bmat, cmat)
    dxs_f, d_b, d_c = pullback(dy3)
    y16 = yfull.reshape(LENGTH, HEADS * HEAD_DIM).astype(jnp.bfloat16)
    dxs = dxs_f.reshape(LENGTH, HEADS * HEAD_DIM).astype(jnp.bfloat16)
    dbc = jnp.concatenate([d_b, d_c], axis=1).astype(jnp.bfloat16)
    d_tok = (jnp.dot(dxs, w_in.T, preferred_element_type=jnp.float32) + jnp.dot(dbc, w_bc.T, preferred_element_type=jnp.float32)).astype(jnp.bfloat16)
    raw_in = jnp.dot(tok.T, dxs, preferred_element_type=jnp.float32)
    raw_bc = jnp.dot(tok.T, dbc, preferred_element_type=jnp.float32)
    raw_out = jnp.dot(y16.T, grad_y, preferred_element_type=jnp.float32)
    return (d_tok, raw_in, raw_bc, raw_out)

def reference(tokens, cotangent, log_decay, w_in, w_bc, w_out):
    d_tok, raw_in, raw_bc, raw_out = lax.map(lambda items: one_record(items, w_in, w_bc, w_out), (tokens, cotangent, log_decay))
    raw_in = lax.optimization_barrier(jnp.sum(raw_in, axis=0))
    raw_bc = lax.optimization_barrier(jnp.sum(raw_bc, axis=0))
    raw_out = lax.optimization_barrier(jnp.sum(raw_out, axis=0))
    entries = raw_in.size + raw_bc.size + raw_out.size
    mean_sq = (jnp.sum(raw_in * raw_in) + jnp.sum(raw_bc * raw_bc) + jnp.sum(raw_out * raw_out)) / entries
    factor = jnp.minimum(1.0, 1.0 / jnp.sqrt(mean_sq + 1e-06))
    return (d_tok, factor * raw_in, factor * raw_bc, factor * raw_out)
```

```python
import jax
import jax.numpy as jnp
from jax import lax
from jax.experimental import pallas as pl
from jax.experimental.pallas import tpu as pltpu
from jax.sharding import PartitionSpec as P

F32 = jnp.float32
BF16 = jnp.bfloat16
NX = 4
NY = 4
NZ = 4
SEG = 256
HALF = SEG // 2
DM = 768
NS = 128
NH = 6
HD = 64
HC = NH * HD
ROWS = DM // 2


def shift(axis, step, wrap=True):
    if axis == "c":
        return "rec", [(r, r ^ 1) for r in range(2 * NZ)]
    count, stride, total, name = {
        "x": (NX, 1, NX * NY, "seq"),
        "y": (NY, NX, NX * NY, "seq"),
        "z": (NZ, 2, 2 * NZ, "rec"),
    }[axis]
    pairs = []
    for i in range(total):
        at = (i // stride) % count
        to = at + step
        if not wrap and not 0 <= to < count:
            continue
        pairs.append((i, i + (to % count - at) * stride))
    return name, pairs


def move(value, axis, step, wrap=True):
    name, pairs = shift(axis, step, wrap)
    return lax.ppermute(value, name, pairs)


def dot(a, b, ca, cb):
    return lax.dot_general(a, b, (((ca,), (cb,)), ((), ())), preferred_element_type=F32)


def place(p, x):
    return lax.rem(p - x + NX, NX)


def vm(n):
    return [pl.BlockSpec(memory_space=pltpu.VMEM)] * n


SMEM = pl.BlockSpec(memory_space=pltpu.SMEM)
PARAMS = pltpu.CompilerParams(vmem_limit_bytes=56 * 2**20)


def tok_kernel(
    at, a0, b0, a1, b1, a2, b2, a3, b3, w_in, w_bc, ci, ce,
    tokb, xs, xfr, bc, pre, t_f, t_r, ends,
):
    x = at[0]
    for k, (a, b) in enumerate(((a0, b0), (a1, b1), (a2, b2), (a3, b3))):
        tokb[k, :HALF] = a[...].astype(BF16)
        tokb[k, HALF:] = b[...].astype(BF16)

    def segment(k, _):
        t = tokb[k]
        xv = dot(t, w_in[...], 1, 0).astype(BF16)
        bv = dot(t, w_bc[...], 1, 0).astype(BF16)
        xs[k] = xv
        bc[k] = bv
        xf = xv.astype(F32)
        last = ci[k, SEG - 1 : SEG, :]
        xfr[k, :, :HC] = (xf * jnp.exp(last - ci[k])).astype(BF16)
        xfr[k, :, HC:] = (xf * jnp.exp(ce[k])).astype(BF16)
        ends[k] = dot(bv[:, :NS], xfr[k], 0, 0)
        return 0

    lax.fori_loop(0, NX, segment, 0)
    acc = jnp.zeros((NS, HC), F32)
    for p in range(NX):
        k = place(p, x)
        pre[0, k] = acc
        acc = acc * jnp.exp(ci[k, SEG - 1 : SEG, :]) + ends[k, :, :HC]
    t_f[...] = acc
    acc = jnp.zeros((NS, HC), F32)
    for p in reversed(range(NX)):
        k = place(p, x)
        pre[1, k] = acc
        acc = acc * jnp.exp(ci[k, SEG - 1 : SEG, :]) + ends[k, :, HC:]
    t_r[...] = acc


def cot_kernel(
    at, a0, b0, a1, b1, a2, b2, a3, b3, w_out, ci, ce, bc,
    cotb, dy, dyfr, pre, t_f, t_r, ends,
):
    x = at[0]
    for k, (a, b) in enumerate(((a0, b0), (a1, b1), (a2, b2), (a3, b3))):
        cotb[k, :HALF] = a[...].astype(BF16)
        cotb[k, HALF:] = b[...].astype(BF16)

    def segment(k, _):
        d = dot(cotb[k], w_out[...], 1, 1)
        dy[k] = d.astype(BF16)
        last = ci[k, SEG - 1 : SEG, :]
        dyfr[k, :, :HC] = (d * jnp.exp(ci[k])).astype(BF16)
        dyfr[k, :, HC:] = (d * jnp.exp(last - ce[k])).astype(BF16)
        ends[k] = dot(bc[k, :, NS:], dyfr[k], 0, 0)
        return 0

    lax.fori_loop(0, NX, segment, 0)
    acc = jnp.zeros((NS, HC), F32)
    for p in reversed(range(NX)):
        k = place(p, x)
        pre[0, k] = acc
        acc = acc * jnp.exp(ci[k, SEG - 1 : SEG, :]) + ends[k, :, :HC]
    t_f[...] = acc
    acc = jnp.zeros((NS, HC), F32)
    for p in range(NX):
        k = place(p, x)
        pre[1, k] = acc
        acc = acc * jnp.exp(ci[k, SEG - 1 : SEG, :]) + ends[k, :, HC:]
    t_r[...] = acc


def enter(pre, which, q, ci, x, order, out, cols):
    log = jnp.zeros((1, HC), F32)
    for p in order:
        k = place(p, x)
        out[k, :, cols] = (pre[which, k] + q[...] * jnp.exp(log)).astype(BF16)
        log = log + ci[k, SEG - 1 : SEG, :]


def inner_kernel(
    at, xs, bc, dy, dyfr, cotb, ci, ce, cirow, cerow, pre, q_f, q_r,
    keep, send, dxi, dci, dbi, sr, yb, g,
):
    x, core = at[0], at[1]
    enter(pre, 0, q_f, ci, x, range(NX), sr, pl.ds(0, HC))
    enter(pre, 1, q_r, ci, x, reversed(range(NX)), sr, pl.ds(HC, HC))

    def segment(k, _):
        b, c = bc[k, :, :NS], bc[k, :, NS:]
        t = lax.broadcasted_iota(jnp.int32, (SEG, SEG), 0)
        s = lax.broadcasted_iota(jnp.int32, (SEG, SEG), 1)
        low, same = t > s, t == s
        scores = dot(c, b, 1, 1)
        scores = jnp.where(same, 2.0 * scores, scores)
        lane = lax.broadcasted_iota(jnp.int32, (SEG, 2 * HD), 1)
        carry = dot(c, sr[k], 1, 0)
        total = jnp.zeros((SEG, SEG), F32)
        for pair in range(NH // 2):
            cols = slice(pair * 2 * HD, (pair + 1) * 2 * HD)
            xp, dp = xs[k, :, cols], dy[k, :, cols]
            ws, xm, dm = [], [], []
            for i in range(2):
                h = 2 * pair + i
                at_t = slice(h * HD, h * HD + 1)
                diff = jnp.where(
                    low,
                    ci[k, :, at_t] - cirow[k, h : h + 1, :],
                    cerow[k, h : h + 1, :] - ce[k, :, at_t],
                )
                decay = jnp.exp(diff)
                mine = (lane < HD) if i == 0 else (lane >= HD)
                xm.append(jnp.where(mine, xp, jnp.zeros_like(xp)))
                dm.append(jnp.where(mine, dp, jnp.zeros_like(dp)))
                ws.append((decay * scores).astype(BF16))
                total = total + decay * dot(dm[i], xp, 1, 1)
            y = dot(ws[0], xm[0], 1, 0) + dot(ws[1], xm[1], 1, 0)
            last = ci[k, SEG - 1 : SEG, cols]
            y = y + carry[:, cols] * jnp.exp(ci[k, :, cols])
            y = y + carry[:, slice(HC + cols.start, HC + cols.stop)] * jnp.exp(last - ce[k, :, cols])
            yb[pl.ds(k * SEG, SEG), cols] = y.astype(BF16)
            dxi[k, :, cols] = dot(ws[0], dm[0], 0, 0) + dot(ws[1], dm[1], 0, 0)
        total = jnp.where(same, 2.0 * total, total).astype(BF16)
        dci[k] = dot(total, b, 1, 0) + dot(dyfr[k], sr[k], 1, 1)
        dbi[k] = dot(total, c, 0, 0)
        return 0

    lax.fori_loop(0, NX, segment, 0)
    raw = dot(yb[...], cotb[...].reshape(NX * SEG, DM), 0, 0)
    for j in range(2):
        for q in range(4):
            z, c = 2 * j + q // 2, q % 2
            g[c, 96 * z : 96 * z + 96, :] = raw[96 * q : 96 * q + 96, HC * j : HC * j + HC]
    keep[...] = g[core]
    send[...] = g[1 - core]


def outer_kernel(
    at, tokb, xfr, bc, ci, ce, pre, q_f, q_r, dxi, dci, dbi, w_in, w_bc,
    keep, send, d0, d1a, d1b, d2a, d2b, d3a, d3b, ds, dz, g,
):
    x, core = at[0], at[1]
    enter(pre, 0, q_f, ci, x, reversed(range(NX)), ds, pl.ds(0, HC))
    enter(pre, 1, q_r, ci, x, range(NX), ds, pl.ds(HC, HC))

    def segment(k, _):
        b = bc[k, :, :NS]
        last = ci[k, SEG - 1 : SEG, :]
        back = dot(b, ds[k], 1, 0)
        dx = dxi[k] + back[:, :HC] * jnp.exp(last - ci[k]) + back[:, HC:] * jnp.exp(ce[k])
        dz[k, :, :HC] = dx.astype(BF16)
        dz[k, :, HC : HC + NS] = (dbi[k] + dot(xfr[k], ds[k], 1, 1)).astype(BF16)
        dz[k, :, HC + NS :] = dci[k].astype(BF16)
        return 0

    lax.fori_loop(0, NX, segment, 0)

    def tokens_of(k):
        return dot(dz[k, :, :HC], w_in[...], 1, 1) + dot(dz[k, :, HC:], w_bc[...], 1, 1)

    for k, (lo, hi) in ((2, (d2a, d2b)), (1, (d1a, d1b)), (3, (d3a, d3b))):
        d = tokens_of(k)
        lo[...] = d[:HALF]
        hi[...] = d[HALF:]
    d0[...] = tokens_of(0)
    width = HC + 2 * NS
    raw = dot(tokb[...].reshape(NX * SEG, DM), dz[...].reshape(NX * SEG, width), 0, 0)
    for j in range(2 * NZ):
        z, c = j // 2, j % 2
        g[c, 96 * z : 96 * z + 96, :] = raw[96 * j : 96 * j + 96, :]
    keep[...] = g[core]
    send[...] = g[1 - core]


def call(kernel, outs, scratch, args, flops):
    moved = sum(a.size * a.dtype.itemsize for a in args)
    return pl.pallas_call(
        kernel,
        out_shape=[jax.ShapeDtypeStruct(*o) for o in outs],
        in_specs=[SMEM] + vm(len(args) - 1),
        out_specs=vm(len(outs)),
        scratch_shapes=[pltpu.VMEM(*s) for s in scratch],
        compiler_params=PARAMS,
        cost_estimate=pl.CostEstimate(flops=flops, bytes_accessed=moved, transcendentals=0),
    )(*args)


def along_y(t_up, t_down, lrow, l_up, l_down):
    f = move(t_up, "y", 1, False)
    r = move(t_down, "y", -1, False)
    two_f = t_up + jnp.exp(lrow) * f
    two_r = t_down + jnp.exp(lrow) * r
    far_f = move(two_f, "y", 2, False)
    far_r = move(two_r, "y", -2, False)
    return f + jnp.exp(l_up) * far_f, r + jnp.exp(l_down) * far_r


def pick(value, index):
    return lax.dynamic_index_in_dim(value, index, 0, keepdims=False)


def scatter_sum(part, first, second, at):
    if first == "y":
        part = jnp.swapaxes(part, 0, 1)
    for axis in (first, second):
        own = pick(part, at[axis])
        for step in (1, 3, 2):
            own = own + move(pick(part, (at[axis] + step) % 4), axis, step)
        part = own
    return part


def body(tokens, cotangent, log_decay, w_in, w_bc, w_out):
    seq, rec = lax.axis_index("seq"), lax.axis_index("rec")
    x, y = seq % NX, seq // NX
    core, z = rec % 2, rec // 2
    at = jnp.stack([x, core]).astype(jnp.int32)

    def gather(v):
        a, b = v[:HALF].astype(F32), v[HALF:].astype(F32)
        a3, b3 = move(a, "x", 1), move(b, "x", 1)
        a1, b1 = move(a, "x", -1), move(b, "x", -1)
        a2, b2 = move(a3, "x", 1), move(b1, "x", -1)
        return [a, b, a1, b1, a2, b2, a3, b3]

    la0 = log_decay[0]
    las = jnp.stack([la0, move(la0, "x", -1), move(la0, "x", 2), move(la0, "x", 1)])
    toks = gather(tokens[0])
    cots = gather(cotangent[0])
    la = lax.dynamic_slice(las, (0, x * NH, 0), (NX, NH, SEG))
    tri = jnp.triu(jnp.ones((SEG, SEG), F32))
    spread = jnp.repeat(jnp.eye(NH, dtype=F32), HD, axis=1)
    best = lax.Precision.HIGHEST
    cirow = jnp.einsum("khs,st->kht", la, tri, precision=best)
    cerow = cirow - la
    ci = jnp.einsum("kht,hj->ktj", cirow, spread, precision=best)
    ce = jnp.einsum("kht,hj->ktj", cerow, spread, precision=best)
    lrow = jnp.broadcast_to(jnp.sum(ci[:, -1, :], axis=0)[None], (8, HC))
    l_up, l_down = move(lrow, "y", 1)[:1], move(lrow, "y", -1)[:1]
    lrow = lrow[:1]
    wi = lax.dynamic_slice(w_in, (0, x * HC), (DM, HC))
    wo = lax.dynamic_slice(w_out, (x * HC, 0), (HC, DM))

    state = ((NS, HC), F32)
    edges = ((2, NX, NS, HC), F32)
    tokb, xs, xfr, bc, pre_s, t_f, t_r = call(
        tok_kernel,
        [((NX, SEG, DM), BF16), ((NX, SEG, HC), BF16), ((NX, SEG, 2 * HC), BF16), ((NX, SEG, 2 * NS), BF16),
         edges, state, state],
        [((NX, NS, 2 * HC), F32)],
        [at, *toks, wi, w_bc, ci, ce],
        2 * 1024 * (DM * (HC + 2 * NS) + NS * 2 * HC),
    )
    q_f, q_r = along_y(t_f, t_r, lrow, l_up, l_down)
    cotb, dy, dyfr, pre_d, u_f, u_r = call(
        cot_kernel,
        [((NX, SEG, DM), BF16), ((NX, SEG, HC), BF16), ((NX, SEG, 2 * HC), BF16), edges, state, state],
        [((NX, NS, 2 * HC), F32)],
        [at, *cots, wo, ci, ce, bc],
        2 * 1024 * (DM * HC + NS * 2 * HC),
    )
    p_r, p_f = along_y(u_r, u_f, lrow, l_up, l_down)
    keep_o, send_o, dxi, dci, dbi = call(
        inner_kernel,
        [((ROWS, HC), F32), ((ROWS, HC), F32), ((NX, SEG, HC), F32), ((NX, SEG, NS), F32), ((NX, SEG, NS), F32)],
        [((NX, NS, 2 * HC), BF16), ((NX * SEG, HC), BF16), ((2, ROWS, HC), F32)],
        [at, xs, bc, dy, dyfr, cotb, ci, ce, cirow, cerow, pre_s, q_f, q_r],
        2 * 1024 * (HC * DM + 5 * SEG * HC + 6 * NS * HC),
    )
    width = HC + 2 * NS
    half = ((HALF, DM), F32)
    keep_i, send_i, d0, d1a, d1b, d2a, d2b, d3a, d3b = call(
        outer_kernel,
        [((ROWS, width), F32), ((ROWS, width), F32), ((SEG, DM), F32), half, half, half, half, half, half],
        [((NX, NS, 2 * HC), BF16), ((NX, SEG, width), BF16), ((2, ROWS, width), F32)],
        [at, tokb, xfr, bc, ci, ce, pre_d, p_f, p_r, dxi, dci, dbi, wi, w_bc],
        2 * 1024 * (2 * width * DM + 4 * NS * HC),
    )
    from_a = d1a + move(d2a, "x", 1)
    from_b = d3b + move(d2b, "x", -1)
    top = d0[:HALF] + move(from_a, "x", 1) + move(d3a, "x", -1)
    bottom = d0[HALF:] + move(d1b, "x", 1) + move(from_b, "x", -1)
    d_tok = jnp.concatenate([top, bottom], axis=0).astype(BF16)

    place_of = {"z": z, "y": y}
    raw_o = (keep_o + move(send_o, "c", 1)).reshape(NZ, NY, 24, HC)
    raw_i = (keep_i + move(send_i, "c", 1)).reshape(NZ, NY, 24, width)
    raw_o = scatter_sum(raw_o, "z", "y", place_of)
    raw_i = jnp.concatenate(
        [
            scatter_sum(raw_i[..., :256], "z", "y", place_of),
            scatter_sum(raw_i[..., 256:], "y", "z", place_of),
        ],
        axis=-1,
    )
    blocks = raw_i.reshape(NX, 6, width)
    pieces = jnp.stack(
        [pick(blocks, x)] + [move(pick(blocks, (x + k) % NX), "x", k) for k in range(1, NX)]
    )
    sum_bc = jnp.sum(pieces[..., HC:], axis=0)
    all_in = jnp.concatenate([pick(pieces, (x - p) % NX)[:, :HC] for p in range(NX)], axis=1)
    left = z < 2
    upper, lower = raw_o[:12], raw_o[12:]
    one, two = [], []
    for r in range(2 * NZ):
        for s in range(NX * NY):
            zz, cc, yy, xx = r // 2, r % 2, s // NX, s % NX
            to = 32 * xx + 2 * ((zz % 2) * 8 + cc * 4 + yy)
            first = 0 if zz < 2 else 1
            one.append((r * 16 + s, to + first))
            two.append((r * 16 + s, to + 1 - first))
    got_one = lax.ppermute(jnp.where(left, upper, lower), ("rec", "seq"), one)
    got_two = lax.ppermute(jnp.where(left, lower, upper), ("rec", "seq"), two)
    even = x % 2 == 0
    all_out = jnp.concatenate(
        [jnp.where(even, got_one, got_two), jnp.where(even, got_two, got_one)], axis=1
    )
    square = jnp.sum(all_in * all_in) + jnp.sum(sum_bc * sum_bc) + jnp.sum(raw_o * raw_o)
    square = jnp.full((8, 128), square)
    square = square + move(square, "c", 1)
    for axis in ("z", "y", "x"):
        square = square + (move(square, axis, 1) + move(square, axis, 3) + move(square, axis, 2))
    entries = DM * 1536 + DM * 256 + 1536 * DM
    factor = jnp.minimum(1.0, 1.0 / jnp.sqrt(square[:1, :1] / entries + 1e-06))
    return d_tok[None], factor * all_in, factor * sum_bc, factor * all_out


def solution(mesh):
    in_specs = (P("rec", "seq", None), P("rec", "seq", None), P("rec", None, "seq"), P(), P(), P())
    out_specs = (
        P("rec", "seq", None),
        P(("rec", "seq"), None),
        P(("rec", "seq"), None),
        P(("rec", "seq"), None),
    )
    return jax.shard_map(body, mesh=mesh, in_specs=in_specs, out_specs=out_specs, check_vma=False)
```

```python
import functools

import jax
import jax.numpy as jnp
from jax import lax
from jax.experimental import pallas as pl
from jax.experimental.pallas import tpu as pltpu
from jax.sharding import PartitionSpec as P

F32 = jnp.float32
BF16 = jnp.bfloat16
NX = 4
NY = 4
NZ = 4
SEG = 256
HALF = SEG // 2
DM = 768
NS = 128
NH = 6
HD = 64
HC = NH * HD
ROWS = DM // 2
WIDE = HC + 2 * NS
TALL = NS + 8


def shift(axis, step, wrap=True):
    if axis == "c":
        return "rec", [(r, r ^ 1) for r in range(2 * NZ)]
    count, stride, total, name = {
        "x": (NX, 1, NX * NY, "seq"),
        "y": (NY, NX, NX * NY, "seq"),
        "z": (NZ, 2, 2 * NZ, "rec"),
    }[axis]
    pairs = []
    for i in range(total):
        at = (i // stride) % count
        to = at + step
        if not wrap and not 0 <= to < count:
            continue
        pairs.append((i, i + (to % count - at) * stride))
    return name, pairs


def move(value, axis, step, wrap=True):
    name, pairs = shift(axis, step, wrap)
    return lax.ppermute(value, name, pairs)


def dot(a, b, ca, cb):
    return lax.dot_general(a, b, (((ca,), (cb,)), ((), ())), preferred_element_type=F32)


def place(p, x):
    return lax.rem(p - x + NX, NX)


def vm(n):
    return [pl.BlockSpec(memory_space=pltpu.VMEM)] * n


SMEM = pl.BlockSpec(memory_space=pltpu.SMEM)
PARAMS = pltpu.CompilerParams(vmem_limit_bytes=30 * 2**20)


def send_rows(up, down, log, y, s_p, s_m, s_2):
    s_p[:NS] = jnp.where(y == NY - 1, down, up)
    s_m[:NS] = jnp.where(y == 0, up, down)
    s_2[:NS] = jnp.where(y < 2, up, down)
    log = jnp.broadcast_to(log, (8, HC))
    for s in (s_p, s_m, s_2):
        s[NS:] = log


def from_rows(r_p, r_m, r_2, y):
    def on(yes):
        return jnp.where(yes, 1.0, 0.0).astype(F32)

    l_p, l_m, l_2 = (r[NS : NS + 1, :] for r in (r_p, r_m, r_2))
    v_p, v_m, v_2 = (r[:NS, :] for r in (r_p, r_m, r_2))
    up = v_p * on(y >= 1) + v_2 * (on(y >= 2) * jnp.exp(l_p)) + v_m * (on(y == 3) * jnp.exp(l_p + l_2))
    down = v_m * on(y <= 2) + v_2 * (on(y <= 1) * jnp.exp(l_m)) + v_p * (on(y == 0) * jnp.exp(l_m + l_2))
    return up, down


def row_scan(order, ends, cols, ci, x, pre, which):
    acc = jnp.zeros((NS, HC), F32)
    for p in order:
        k = place(p, x)
        pre[which, k] = acc
        acc = acc * jnp.exp(ci[k, SEG - 1 : SEG, :]) + ends[k, :, cols]
    return acc


def row_log(ci):
    return sum(ci[k, SEG - 1 : SEG, :] for k in range(NX))


FIRST, SECOND = slice(0, HC), slice(HC, 2 * HC)


def tok_kernel(
    at, t0, t1, t2, t3, w_in, w_bc, ci, ce, tokb, xs, xfr, bc, pre, s_p, s_m, s_2, ends
):
    x, y = at[0], at[2]
    for k, t in enumerate((t0, t1, t2, t3)):
        tokb[k] = t[...].astype(BF16)

    def segment(k, _):
        t = tokb[k]
        xv = dot(t, w_in[...], 1, 0).astype(BF16)
        bv = dot(t, w_bc[...], 1, 0).astype(BF16)
        xs[k] = xv
        bc[k] = bv
        xf = xv.astype(F32)
        last = ci[k, SEG - 1 : SEG, :]
        xfr[k, :, :HC] = (xf * jnp.exp(last - ci[k])).astype(BF16)
        xfr[k, :, HC:] = (xf * jnp.exp(ce[k])).astype(BF16)
        ends[k] = dot(bv[:, :NS], xfr[k], 0, 0)
        return 0

    lax.fori_loop(0, NX, segment, 0)
    up = row_scan(range(NX), ends, FIRST, ci, x, pre, 0)
    down = row_scan(reversed(range(NX)), ends, SECOND, ci, x, pre, 1)
    send_rows(up, down, row_log(ci), y, s_p, s_m, s_2)


def cot_part(cots, first, w_out, ci, ce, bc, cotb, dy, dyfr, ends):
    for i, t in enumerate(cots):
        cotb[i] = t[...].astype(BF16)

    def segment(i, _):
        k = first + i
        d = dot(cotb[i], w_out[...], 1, 1)
        dy[i] = d.astype(BF16)
        last = ci[k, SEG - 1 : SEG, :]
        dyfr[i, :, :HC] = (d * jnp.exp(ci[k])).astype(BF16)
        dyfr[i, :, HC:] = (d * jnp.exp(last - ce[k])).astype(BF16)
        ends[k] = dot(bc[k, :, NS:], dyfr[i], 0, 0)
        return 0

    lax.fori_loop(0, len(cots), segment, 0)


def cot_kernel_a(at, c0, c1, w_out, ci, ce, bc, cotb, dy, dyfr, ends_a, ends):
    cot_part((c0, c1), 0, w_out, ci, ce, bc, cotb, dy, dyfr, ends)
    ends_a[...] = ends[:2]


def cot_kernel_b(
    at, c2, c3, w_out, ci, ce, bc, ends_a, cotb, dy, dyfr, pre, s_p, s_m, s_2, ends
):
    x, y = at[0], at[2]
    ends[:2] = ends_a[...]
    cot_part((c2, c3), 2, w_out, ci, ce, bc, cotb, dy, dyfr, ends)
    down = row_scan(reversed(range(NX)), ends, FIRST, ci, x, pre, 0)
    up = row_scan(range(NX), ends, SECOND, ci, x, pre, 1)
    send_rows(up, down, row_log(ci), y, s_p, s_m, s_2)


def enter(pre, which, q, ci, x, order, out, cols):
    log = jnp.zeros((1, HC), F32)
    for p in order:
        k = place(p, x)
        out[k, :, cols] = (pre[which, k] + q * jnp.exp(log)).astype(BF16)
        log = log + ci[k, SEG - 1 : SEG, :]


def inner_kernel(
    at, xs, bc, dy_a, dy_b, dyfr_a, dyfr_b, cotb_a, cotb_b, ci, ce, cirow, cerow, pre, r_p, r_m, r_2,
    keep, send, dxi, dci, dbi, sr, yb, g,
):
    x, core, y_at = at[0], at[1], at[2]
    up, down = from_rows(r_p, r_m, r_2, y_at)
    enter(pre, 0, up, ci, x, range(NX), sr, pl.ds(0, HC))
    enter(pre, 1, down, ci, x, reversed(range(NX)), sr, pl.ds(HC, HC))

    def run(first, dy, dyfr):
        def segment(i, _):
            k = first + i
            b, c = bc[k, :, :NS], bc[k, :, NS:]
            t = lax.broadcasted_iota(jnp.int32, (SEG, SEG), 0)
            s = lax.broadcasted_iota(jnp.int32, (SEG, SEG), 1)
            low, same = t > s, t == s
            scores = dot(c, b, 1, 1)
            scores = jnp.where(same, 2.0 * scores, scores)
            lane = lax.broadcasted_iota(jnp.int32, (SEG, 2 * HD), 1)
            carry = dot(c, sr[k], 1, 0)
            total = jnp.zeros((SEG, SEG), F32)
            for pair in range(NH // 2):
                cols = slice(pair * 2 * HD, (pair + 1) * 2 * HD)
                xp, dp = xs[k, :, cols], dy[i, :, cols]
                ws, xm, dm = [], [], []
                for j in range(2):
                    h = 2 * pair + j
                    at_t = slice(h * HD, h * HD + 1)
                    diff = jnp.where(
                        low,
                        ci[k, :, at_t] - cirow[k, h : h + 1, :],
                        cerow[k, h : h + 1, :] - ce[k, :, at_t],
                    )
                    decay = jnp.exp(diff)
                    mine = (lane < HD) if j == 0 else (lane >= HD)
                    xm.append(jnp.where(mine, xp, jnp.zeros_like(xp)))
                    dm.append(jnp.where(mine, dp, jnp.zeros_like(dp)))
                    ws.append((decay * scores).astype(BF16))
                    total = total + decay * dot(dm[j], xp, 1, 1)
                y = dot(ws[0], xm[0], 1, 0) + dot(ws[1], xm[1], 1, 0)
                last = ci[k, SEG - 1 : SEG, cols]
                y = y + carry[:, cols] * jnp.exp(ci[k, :, cols])
                y = y + carry[:, slice(HC + cols.start, HC + cols.stop)] * jnp.exp(last - ce[k, :, cols])
                yb[pl.ds(k * SEG, SEG), cols] = y.astype(BF16)
                dxi[k, :, cols] = dot(ws[0], dm[0], 0, 0) + dot(ws[1], dm[1], 0, 0)
            total = jnp.where(same, 2.0 * total, total).astype(BF16)
            dci[k] = dot(total, b, 1, 0) + dot(dyfr[i], sr[k], 1, 1)
            dbi[k] = dot(total, c, 0, 0)
            return 0

        lax.fori_loop(0, 2, segment, 0)

    run(0, dy_a, dyfr_a)
    run(2, dy_b, dyfr_b)
    half = 2 * SEG
    raw = dot(yb[:half, :], cotb_a[...].reshape(half, DM), 0, 0)
    raw = raw + dot(yb[half:, :], cotb_b[...].reshape(half, DM), 0, 0)
    for j in range(2):
        for q in range(4):
            z, c = 2 * j + q // 2, q % 2
            g[c, 96 * z : 96 * z + 96, :] = raw[96 * q : 96 * q + 96, HC * j : HC * j + HC]
    keep[...] = g[core]
    send[...] = g[1 - core]


def outer_kernel(
    at, tokb, xfr, bc, ci, ce, pre, r_p, r_m, r_2, dxi, dci, dbi, keep, send, dz, ds, g
):
    x, core, y_at = at[0], at[1], at[2]
    up, down = from_rows(r_p, r_m, r_2, y_at)
    enter(pre, 0, down, ci, x, reversed(range(NX)), ds, pl.ds(0, HC))
    enter(pre, 1, up, ci, x, range(NX), ds, pl.ds(HC, HC))

    def segment(k, _):
        b = bc[k, :, :NS]
        last = ci[k, SEG - 1 : SEG, :]
        back = dot(b, ds[k], 1, 0)
        dx = dxi[k] + back[:, :HC] * jnp.exp(last - ci[k]) + back[:, HC:] * jnp.exp(ce[k])
        dz[k, :, :HC] = dx.astype(BF16)
        dz[k, :, HC : HC + NS] = (dbi[k] + dot(xfr[k], ds[k], 1, 1)).astype(BF16)
        dz[k, :, HC + NS :] = dci[k].astype(BF16)
        return 0

    lax.fori_loop(0, NX, segment, 0)
    raw = dot(tokb[...].reshape(NX * SEG, DM), dz[...].reshape(NX * SEG, WIDE), 0, 0)
    for j in range(2 * NZ * NY):
        z, c, y = j // 8, j // 4 % 2, j % 4
        row = (4 * y + z) * 24
        g[c, row : row + 24, :] = raw[24 * j : 24 * j + 24, :]
    keep[...] = g[core]
    send[...] = g[1 - core]


def tokens_kernel(at, dz, w_in, w_bc, d0, d1, d2a, d2b, d3):
    def tokens_of(k):
        return dot(dz[k, :, :HC], w_in[...], 1, 1) + dot(dz[k, :, HC:], w_bc[...], 1, 1)

    d = tokens_of(2)
    d2a[...] = d[:HALF]
    d2b[...] = d[HALF:]
    d1[...] = tokens_of(1)
    d3[...] = tokens_of(3)
    d0[...] = tokens_of(0)


def pass_kernel(at, d1, d3, r_a, r_b, s1, s3):
    s1[:HALF] = d1[:HALF] + r_a[...]
    s1[HALF:] = d1[HALF:]
    s3[:HALF] = d3[:HALF]
    s3[HALF:] = d3[HALF:] + r_b[...]


def deal_kernel(which, at, *refs):
    terms, outs, total = refs[:-5], refs[-5:-1], refs[-1]
    acc = terms[0][...]
    for term in terms[1:]:
        acc = acc + term[...]
    total[...] = acc.reshape(total.shape)
    for k, out in enumerate(outs):
        out[...] = total[lax.rem(at[which] + k, 4)]


def out_kernel(at, a, b, c, d, one, two, square):
    rows = a[...] + b[...] + c[...] + d[...]
    left = at[3] < 2
    one[...] = jnp.where(left, rows[:12], rows[12:])
    two[...] = jnp.where(left, rows[12:], rows[:12])
    square[...] = jnp.broadcast_to(jnp.sum(rows * rows).reshape(1, 1), (8, 128))


def cut_kernel(at, a, b, c, d, square, p0, p1, p2, p3):
    rows = a[...] + b[...] + c[...] + d[...]
    mine = rows[:, :HC]
    local = jnp.sum(mine * mine).reshape(1, 1) + square[:1, :1]
    for k, out in enumerate((p0, p1, p2, p3)):
        to = lax.rem(at[0] + k, NX)
        part = mine[:6]
        for p in range(1, NX):
            part = jnp.where(to == p, mine[6 * p : 6 * p + 6], part)
        out[:6] = part
        out[6:8] = jnp.zeros((2, HC), F32)
        out[8:32, : 2 * NS] = rows[:, HC:]
        out[8:32, 2 * NS :] = jnp.zeros((24, HC - 2 * NS), F32)
        out[32:] = jnp.broadcast_to(local, (8, HC))


def square_kernel(at, a, b, c, d, square):
    refs = (a, b, c, d)
    bc = sum(r[8:32, : 2 * NS] for r in refs)
    total = sum(r[32:, :128] for r in refs)
    square[...] = total + jnp.sum(bc * bc).reshape(1, 1)


def last_kernel(at, a, b, c, d, one, two, square, all_in, all_bc, all_out, parts):
    x = at[0]
    entries = DM * 1536 + DM * 256 + 1536 * DM
    factor = jnp.minimum(1.0, 1.0 / jnp.sqrt(square[:1, :1] / entries + 1e-06))
    for k, r in enumerate((a, b, c, d)):
        parts[k] = r[...]
    for p in range(NX):
        all_in[:, HC * p : HC * p + HC] = factor * parts[lax.rem(x - p + NX, NX), :6, :]
    rows = sum(r[8:32, : 2 * NS] for r in (a, b, c, d))
    mine = rows[:6]
    for p in range(1, NX):
        mine = jnp.where(x == p, rows[6 * p : 6 * p + 6], mine)
    all_bc[...] = factor * mine
    even = lax.rem(x, 2) == 0
    all_out[:, :HC] = factor * jnp.where(even, one[...], two[...])
    all_out[:, HC:] = factor * jnp.where(even, two[...], one[...])


def call(kernel, outs, scratch, args, flops=0):
    moved = sum(a.size * a.dtype.itemsize for a in args)
    return pl.pallas_call(
        kernel,
        out_shape=[jax.ShapeDtypeStruct(*o) for o in outs],
        in_specs=[SMEM] + vm(len(args) - 1),
        out_specs=vm(len(outs)),
        scratch_shapes=[pltpu.VMEM(*s) for s in scratch],
        compiler_params=PARAMS,
        cost_estimate=pl.CostEstimate(flops=flops, bytes_accessed=moved, transcendentals=0),
    )(*args)


def rows_exchange(s_p, s_m, s_2):
    return [move(s_p, "y", 1), move(s_m, "y", -1), move(s_2, "y", 2)]


def deal(at, which, terms, rows, cols):
    axis = {2: "y", 3: "z"}[which]
    p0, p1, p2, p3 = call(
        functools.partial(deal_kernel, which), [((rows, cols), F32)] * 4, [((4, rows, cols), F32)], [at, *terms]
    )
    return [p0, move(p1, axis, 1), move(p2, axis, 2), move(p3, axis, 3)]


def body(tokens, cotangent, log_decay, w_in, w_bc, w_out):
    seq, rec = lax.axis_index("seq"), lax.axis_index("rec")
    x = seq % NX
    at = jnp.stack([x, rec % 2, seq // NX, rec // 2]).astype(jnp.int32)
    tie = lax.optimization_barrier

    t0, c0 = tokens[0].astype(F32), cotangent[0].astype(F32)
    t3, t1 = move(t0, "x", 1), move(t0, "x", -1)
    la0 = log_decay[0]
    las = jnp.stack([la0, move(la0, "x", -1), move(la0, "x", 2), move(la0, "x", 1)])
    la = lax.dynamic_slice(las, (0, x * NH, 0), (NX, NH, SEG))
    tri = jnp.triu(jnp.ones((SEG, SEG), F32))
    spread = jnp.repeat(jnp.eye(NH, dtype=F32), HD, axis=1)
    best = lax.Precision.HIGHEST
    cirow = jnp.einsum("khs,st->kht", la, tri, precision=best)
    cerow = cirow - la
    ci = jnp.einsum("kht,hj->ktj", cirow, spread, precision=best)
    ce = jnp.einsum("kht,hj->ktj", cerow, spread, precision=best)
    wi = lax.dynamic_slice(w_in, (0, x * HC), (DM, HC))
    wo = lax.dynamic_slice(w_out, (x * HC, 0), (HC, DM))
    t3, ci, ce, cirow, cerow, wi, wo = tie((t3, ci, ce, cirow, cerow, wi, wo))
    t2 = move(t3, "x", 1)
    c0_l, t1 = tie((c0, t1))
    c1 = move(c0_l, "x", -1)
    c0_r, t2 = tie((c0, t2))
    c3 = move(c0_r, "x", 1)
    c2 = move(c1, "x", -1)

    tall = ((TALL, HC), F32)
    edges = ((2, NX, NS, HC), F32)
    ends = ((NX, NS, 2 * HC), F32)
    tokb, xs, xfr, bc, pre_s, *s_rows = call(
        tok_kernel,
        [((NX, SEG, DM), BF16), ((NX, SEG, HC), BF16), ((NX, SEG, 2 * HC), BF16), ((NX, SEG, 2 * NS), BF16),
         edges, tall, tall, tall],
        [ends],
        [at, t0, t1, t2, t3, wi, w_bc, ci, ce],
        2 * 1024 * (DM * (HC + 2 * NS) + NS * 2 * HC),
    )
    q_rows = rows_exchange(*s_rows)
    two = [((2, SEG, DM), BF16), ((2, SEG, HC), BF16), ((2, SEG, 2 * HC), BF16)]
    flops = 1024 * (DM * HC + NS * 2 * HC)
    cotb_a, dy_a, dyfr_a, ends_a = call(
        cot_kernel_a, [*two, ((2, NS, 2 * HC), F32)], [ends], [at, c0, c1, wo, ci, ce, bc], flops
    )
    cotb_b, dy_b, dyfr_b, pre_d, *s_rows = call(
        cot_kernel_b, [*two, edges, tall, tall, tall], [ends], [at, c2, c3, wo, ci, ce, bc, ends_a], flops
    )
    p_rows = rows_exchange(*s_rows)
    keep_o, send_o, dxi, dci, dbi = call(
        inner_kernel,
        [((ROWS, HC), F32), ((ROWS, HC), F32), ((NX, SEG, HC), F32), ((NX, SEG, NS), F32), ((NX, SEG, NS), F32)],
        [((NX, NS, 2 * HC), BF16), ((NX * SEG, HC), BF16), ((2, ROWS, HC), F32)],
        [at, xs, bc, dy_a, dy_b, dyfr_a, dyfr_b, cotb_a, cotb_b, ci, ce, cirow, cerow, pre_s, *q_rows],
        2 * 1024 * (HC * DM + 5 * SEG * HC + 6 * NS * HC),
    )
    terms = deal(at, 3, [keep_o, move(send_o, "c", 1)], 96, HC)
    terms = deal(at, 2, terms, 24, HC)
    one, two_, square_o = call(out_kernel, [((12, HC), F32), ((12, HC), F32), ((8, 128), F32)], [], [at, *terms])
    keep_i, send_i, dz = call(
        outer_kernel,
        [((ROWS, WIDE), F32), ((ROWS, WIDE), F32), ((NX, SEG, WIDE), BF16)],
        [((NX, NS, 2 * HC), BF16), ((2, ROWS, WIDE), F32)],
        [at, tokb, xfr, bc, ci, ce, pre_d, *p_rows, dxi, dci, dbi],
        2 * 1024 * (WIDE * DM + 4 * NS * HC),
    )
    got_i = move(send_i, "c", 1)
    whole, half = ((SEG, DM), F32), ((HALF, DM), F32)
    d0, d1, d2a, d2b, d3 = call(
        tokens_kernel, [whole, whole, half, half, whole], [], [at, dz, wi, w_bc], 2 * 1024 * WIDE * DM
    )
    terms = deal(at, 2, [keep_i, got_i], 96, WIDE)
    r_a, r_b = move(d2a, "x", 1), move(d2b, "x", -1)
    terms = deal(at, 3, terms, 24, WIDE)
    s1, s3 = call(pass_kernel, [whole, whole], [], [at, d1, d3, r_a, r_b])
    m1, m3 = move(s1, "x", 1), move(s3, "x", -1)
    d_tok = (d0 + m1 + m3).astype(BF16)
    p0, p1, p2, p3 = call(cut_kernel, [((40, HC), F32)] * 4, [], [at, *terms, square_o])
    pieces = [p0, move(p1, "x", 1), move(p2, "x", 2), move(p3, "x", 3)]
    pairs = [], []
    for r in range(2 * NZ):
        for s in range(NX * NY):
            zz, cc, yy, xx = r // 2, r % 2, s // NX, s % NX
            to = 32 * xx + 2 * ((zz % 2) * 8 + cc * 4 + yy)
            first = 0 if zz < 2 else 1
            pairs[0].append((r * 16 + s, to + first))
            pairs[1].append((r * 16 + s, to + 1 - first))
    got_one = lax.ppermute(one, ("rec", "seq"), pairs[0])
    got_two = lax.ppermute(two_, ("rec", "seq"), pairs[1])
    (square,) = call(square_kernel, [((8, 128), F32)], [], [at, *pieces])
    for axis in ("y", "z"):
        square = square + (move(square, axis, 1) + move(square, axis, 3) + move(square, axis, 2))
    square = square + move(square, "c", 1)
    all_in, all_bc, all_out = call(
        last_kernel,
        [((6, NX * HC), F32), ((6, 2 * NS), F32), ((12, DM), F32)],
        [((NX, 40, HC), F32)],
        [at, *pieces, got_one, got_two, square],
    )
    return d_tok[None], all_in, all_bc, all_out


def solution(mesh):
    in_specs = (P("rec", "seq", None), P("rec", "seq", None), P("rec", None, "seq"), P(), P(), P())
    out_specs = (
        P("rec", "seq", None),
        P(("rec", "seq"), None),
        P(("rec", "seq"), None),
        P(("rec", "seq"), None),
    )
    return jax.shard_map(body, mesh=mesh, in_specs=in_specs, out_specs=out_specs, check_vma=False)
```

```python
import functools

import jax
import jax.numpy as jnp
from jax import lax
from jax.experimental import pallas as pl
from jax.experimental.pallas import tpu as pltpu
from jax.sharding import PartitionSpec as P

F32 = jnp.float32
BF16 = jnp.bfloat16
NX = 4
NY = 4
NZ = 4
SEG = 256
HALF = SEG // 2
DM = 768
NS = 128
NH = 6
HD = 64
HC = NH * HD
ROWS = DM // 2
WIDE = HC + 2 * NS
ALL = WIDE + HC
TALL = NS + 8


def shift(axis, step, wrap=True):
    if axis == "c":
        return "rec", [(r, r ^ 1) for r in range(2 * NZ)]
    count, stride, total, name = {
        "x": (NX, 1, NX * NY, "seq"),
        "y": (NY, NX, NX * NY, "seq"),
        "z": (NZ, 2, 2 * NZ, "rec"),
    }[axis]
    pairs = []
    for i in range(total):
        at = (i // stride) % count
        to = at + step
        if not wrap and not 0 <= to < count:
            continue
        pairs.append((i, i + (to % count - at) * stride))
    return name, pairs


def move(value, axis, step, wrap=True):
    name, pairs = shift(axis, step, wrap)
    return lax.ppermute(value, name, pairs)


def dot(a, b, ca, cb):
    return lax.dot_general(a, b, (((ca,), (cb,)), ((), ())), preferred_element_type=F32)


def exact(a, b, ca, cb):
    return lax.dot_general(
        a, b, (((ca,), (cb,)), ((), ())), precision=lax.Precision.HIGHEST, preferred_element_type=F32
    )


def place(p, x):
    return lax.rem(p - x + NX, NX)


def vm(n):
    return [pl.BlockSpec(memory_space=pltpu.VMEM)] * n


SMEM = pl.BlockSpec(memory_space=pltpu.SMEM)
PARAMS = pltpu.CompilerParams(vmem_limit_bytes=30 * 2**20)


def send_rows(up, down, log, y, s_p, s_m, s_2):
    s_p[:NS] = jnp.where(y == NY - 1, down, up)
    s_m[:NS] = jnp.where(y == 0, up, down)
    s_2[:NS] = jnp.where(y < 2, up, down)
    log = jnp.broadcast_to(log, (8, HC))
    for s in (s_p, s_m, s_2):
        s[NS:] = log


def from_rows(r_p, r_m, r_2, y):
    def on(yes):
        return jnp.where(yes, 1.0, 0.0).astype(F32)

    l_p, l_m, l_2 = (r[NS : NS + 1, :] for r in (r_p, r_m, r_2))
    v_p, v_m, v_2 = (r[:NS, :] for r in (r_p, r_m, r_2))
    up = v_p * on(y >= 1) + v_2 * (on(y >= 2) * jnp.exp(l_p)) + v_m * (on(y == 3) * jnp.exp(l_p + l_2))
    down = v_m * on(y <= 2) + v_2 * (on(y <= 1) * jnp.exp(l_m)) + v_p * (on(y == 0) * jnp.exp(l_m + l_2))
    return up, down


def row_scan(order, ends, cols, ci, x, pre, which):
    acc = jnp.zeros((NS, HC), F32)
    for p in order:
        k = place(p, x)
        pre[which, k] = acc
        acc = acc * jnp.exp(ci[k, SEG - 1 : SEG, :]) + ends[k, :, cols]
    return acc


def row_log(ci):
    return sum(ci[k, SEG - 1 : SEG, :] for k in range(NX))


FIRST, SECOND = slice(0, HC), slice(HC, 2 * HC)


def pack_kernel(tok, cot, log, out, cot_out):
    cot_out[...] = cot[...].astype(F32)
    out[:SEG] = tok[...].astype(F32)
    for part in range(3):
        out[SEG:, SEG * part : SEG * part + SEG] = log[8 * part : 8 * part + 8]


def decays(x, toks, cirow, cerow, ci, ce, la):
    s = lax.broadcasted_iota(jnp.int32, (SEG, SEG), 0)
    t = lax.broadcasted_iota(jnp.int32, (SEG, SEG), 1)
    tri = jnp.where(s <= t, 1.0, 0.0).astype(F32)
    head = lax.broadcasted_iota(jnp.int32, (8, HC), 0) * HD
    lane = lax.broadcasted_iota(jnp.int32, (8, HC), 1)
    spread = jnp.where((lane >= head) & (lane < head + HD), 1.0, 0.0).astype(F32)
    la[...] = jnp.zeros((8, SEG), F32)
    for k, tok in enumerate(toks):
        for j in range(NH):
            mine = jnp.zeros((1, SEG), F32)
            for p in range(NX):
                row, part = (NH * p + j) % 8, (NH * p + j) // 8
                its = tok[SEG + row : SEG + row + 1, SEG * part : SEG * part + SEG]
                mine = jnp.where(x == p, its, mine)
            la[j : j + 1] = mine
        through = exact(la[...], tri, 1, 0)
        before = through - la[...]
        cirow[k] = through
        cerow[k] = before
        ci[k] = exact(through, spread, 0, 0)
        ce[k] = exact(before, spread, 0, 0)


def tok_kernel(
    at, t0, t1, t2, t3, w_in, w_bc,
    cirow, cerow, ci, ce, tokb, xs, xfr, bc, pre, s_p, s_m, s_2, ends, la,
):
    x, y = at[0], at[2]
    decays(x, (t0, t1, t2, t3), cirow, cerow, ci, ce, la)
    for k, t in enumerate((t0, t1, t2, t3)):
        tokb[k] = t[:SEG].astype(BF16)

    def segment(k, _):
        t = tokb[k]
        xv = dot(t, w_in[...], 1, 0).astype(BF16)
        bv = dot(t, w_bc[...], 1, 0).astype(BF16)
        xs[k] = xv
        bc[k] = bv
        xf = xv.astype(F32)
        last = ci[k, SEG - 1 : SEG, :]
        xfr[k, :, :HC] = (xf * jnp.exp(last - ci[k])).astype(BF16)
        xfr[k, :, HC:] = (xf * jnp.exp(ce[k])).astype(BF16)
        ends[k] = dot(bv[:, :NS], xfr[k], 0, 0)
        return 0

    lax.fori_loop(0, NX, segment, 0)
    up = row_scan(range(NX), ends, FIRST, ci, x, pre, 0)
    down = row_scan(reversed(range(NX)), ends, SECOND, ci, x, pre, 1)
    send_rows(up, down, row_log(ci), y, s_p, s_m, s_2)


def cot_part(cots, first, w_out, ci, ce, bc, cotb, dy, dyfr, ends):
    for i, t in enumerate(cots):
        cotb[i] = t[...].astype(BF16)

    def segment(i, _):
        k = first + i
        d = dot(cotb[i], w_out[...], 1, 1)
        dy[i] = d.astype(BF16)
        last = ci[k, SEG - 1 : SEG, :]
        dyfr[i, :, :HC] = (d * jnp.exp(ci[k])).astype(BF16)
        dyfr[i, :, HC:] = (d * jnp.exp(last - ce[k])).astype(BF16)
        ends[k] = dot(bc[k, :, NS:], dyfr[i], 0, 0)
        return 0

    lax.fori_loop(0, len(cots), segment, 0)


def cot_kernel_a(at, c0, c1, w_out, ci, ce, bc, cotb, dy, dyfr, ends_a, ends):
    cot_part((c0, c1), 0, w_out, ci, ce, bc, cotb, dy, dyfr, ends)
    ends_a[...] = ends[:2]


def cot_kernel_b(
    at, c2, c3, w_out, ci, ce, bc, ends_a, cotb, dy, dyfr, pre, s_p, s_m, s_2, ends
):
    x, y = at[0], at[2]
    ends[:2] = ends_a[...]
    cot_part((c2, c3), 2, w_out, ci, ce, bc, cotb, dy, dyfr, ends)
    down = row_scan(reversed(range(NX)), ends, FIRST, ci, x, pre, 0)
    up = row_scan(range(NX), ends, SECOND, ci, x, pre, 1)
    send_rows(up, down, row_log(ci), y, s_p, s_m, s_2)


def enter(pre, which, q, ci, x, order, out, cols):
    log = jnp.zeros((1, HC), F32)
    for p in order:
        k = place(p, x)
        out[k, :, cols] = (pre[which, k] + q * jnp.exp(log)).astype(BF16)
        log = log + ci[k, SEG - 1 : SEG, :]


def blocks():
    return [(j, j // 4 % 2, (4 * (j % 4) + j // 8) * 24) for j in range(2 * NZ * NY)]


def inner_kernel(
    at, xs, bc, dy_a, dy_b, dyfr_a, dyfr_b, cotb_a, cotb_b, ci, ce, cirow, cerow, pre, r_p, r_m, r_2,
    g, dxi, dci, dbi, sr, yb,
):
    x, y_at = at[0], at[2]
    up, down = from_rows(r_p, r_m, r_2, y_at)
    enter(pre, 0, up, ci, x, range(NX), sr, pl.ds(0, HC))
    enter(pre, 1, down, ci, x, reversed(range(NX)), sr, pl.ds(HC, HC))

    def run(first, dy, dyfr):
        def segment(i, _):
            k = first + i
            b, c = bc[k, :, :NS], bc[k, :, NS:]
            t = lax.broadcasted_iota(jnp.int32, (SEG, SEG), 0)
            s = lax.broadcasted_iota(jnp.int32, (SEG, SEG), 1)
            low, same = t > s, t == s
            scores = dot(c, b, 1, 1)
            scores = jnp.where(same, 2.0 * scores, scores)
            lane = lax.broadcasted_iota(jnp.int32, (SEG, 2 * HD), 1)
            carry = dot(c, sr[k], 1, 0)
            total = jnp.zeros((SEG, SEG), F32)
            for pair in range(NH // 2):
                cols = slice(pair * 2 * HD, (pair + 1) * 2 * HD)
                xp, dp = xs[k, :, cols], dy[i, :, cols]
                ws, xm, dm = [], [], []
                for j in range(2):
                    h = 2 * pair + j
                    at_t = slice(h * HD, h * HD + 1)
                    diff = jnp.where(
                        low,
                        ci[k, :, at_t] - cirow[k, h : h + 1, :],
                        cerow[k, h : h + 1, :] - ce[k, :, at_t],
                    )
                    decay = jnp.exp(diff)
                    mine = (lane < HD) if j == 0 else (lane >= HD)
                    xm.append(jnp.where(mine, xp, jnp.zeros_like(xp)))
                    dm.append(jnp.where(mine, dp, jnp.zeros_like(dp)))
                    ws.append((decay * scores).astype(BF16))
                    total = total + decay * dot(dm[j], xp, 1, 1)
                y = dot(ws[0], xm[0], 1, 0) + dot(ws[1], xm[1], 1, 0)
                last = ci[k, SEG - 1 : SEG, cols]
                y = y + carry[:, cols] * jnp.exp(ci[k, :, cols])
                y = y + carry[:, slice(HC + cols.start, HC + cols.stop)] * jnp.exp(last - ce[k, :, cols])
                yb[pl.ds(k * SEG, SEG), cols] = y.astype(BF16)
                dxi[k, :, cols] = dot(ws[0], dm[0], 0, 0) + dot(ws[1], dm[1], 0, 0)
            total = jnp.where(same, 2.0 * total, total).astype(BF16)
            dci[k] = dot(total, b, 1, 0) + dot(dyfr[i], sr[k], 1, 1)
            dbi[k] = dot(total, c, 0, 0)
            return 0

        lax.fori_loop(0, 2, segment, 0)

    run(0, dy_a, dyfr_a)
    run(2, dy_b, dyfr_b)
    half = 2 * SEG
    raw = dot(yb[:half, :], cotb_a[...].reshape(half, DM), 0, 0)
    raw = raw + dot(yb[half:, :], cotb_b[...].reshape(half, DM), 0, 0)
    for j, c, row in blocks():
        g[c, row : row + 12, :] = raw[12 * j : 12 * j + 12, :HC]
        g[c, row + 12 : row + 24, :] = raw[12 * j : 12 * j + 12, HC:]


def outer_kernel(
    at, tokb, xfr, bc, ci, ce, pre, r_p, r_m, r_2, dxi, dci, dbi, g_out, keep, send, dz, ds, g
):
    x, core, y_at = at[0], at[1], at[2]
    up, down = from_rows(r_p, r_m, r_2, y_at)
    enter(pre, 0, down, ci, x, reversed(range(NX)), ds, pl.ds(0, HC))
    enter(pre, 1, up, ci, x, range(NX), ds, pl.ds(HC, HC))

    def segment(k, _):
        b = bc[k, :, :NS]
        last = ci[k, SEG - 1 : SEG, :]
        back = dot(b, ds[k], 1, 0)
        dx = dxi[k] + back[:, :HC] * jnp.exp(last - ci[k]) + back[:, HC:] * jnp.exp(ce[k])
        dz[k, :, :HC] = dx.astype(BF16)
        dz[k, :, HC : HC + NS] = (dbi[k] + dot(xfr[k], ds[k], 1, 1)).astype(BF16)
        dz[k, :, HC + NS :] = dci[k].astype(BF16)
        return 0

    lax.fori_loop(0, NX, segment, 0)
    raw = dot(tokb[...].reshape(NX * SEG, DM), dz[...].reshape(NX * SEG, WIDE), 0, 0)
    for j, c, row in blocks():
        g[c, row : row + 24, :] = raw[24 * j : 24 * j + 24, :]
    for out, c in ((keep, core), (send, 1 - core)):
        out[:, :WIDE] = g[c]
        out[:, WIDE:] = g_out[c]


def tokens_kernel(at, dz, w_in, w_bc, d0, d1, d2a, d2b, d3):
    def tokens_of(k):
        return dot(dz[k, :, :HC], w_in[...], 1, 1) + dot(dz[k, :, HC:], w_bc[...], 1, 1)

    d = tokens_of(2)
    d2a[...] = d[:HALF]
    d2b[...] = d[HALF:]
    d1[...] = tokens_of(1)
    d3[...] = tokens_of(3)
    d0[...] = tokens_of(0)


def pass_kernel(at, d1, d3, r_a, r_b, s1, s3):
    s1[:HALF] = d1[:HALF] + r_a[...]
    s1[HALF:] = d1[HALF:]
    s3[:HALF] = d3[:HALF]
    s3[HALF:] = d3[HALF:] + r_b[...]


def deal_kernel(which, at, *refs):
    terms, outs, total = refs[:-5], refs[-5:-1], refs[-1]
    acc = terms[0][...]
    for term in terms[1:]:
        acc = acc + term[...]
    total[...] = acc.reshape(total.shape)
    for k, out in enumerate(outs):
        out[...] = total[lax.rem(at[which] + k, 4)]


def cut_kernel(at, a, b, c, d, p0, p1, p2, p3, rows_out):
    rows = a[...] + b[...] + c[...] + d[...]
    mine, of_out = rows[:, :HC], rows[:, WIDE:]
    rows_out[...] = of_out
    local = (jnp.sum(mine * mine) + jnp.sum(of_out * of_out)).reshape(1, 1)
    for k, out in enumerate((p0, p1, p2, p3)):
        to = lax.rem(at[0] + k, NX)
        part = mine[:6]
        for p in range(1, NX):
            part = jnp.where(to == p, mine[6 * p : 6 * p + 6], part)
        out[:6] = part
        out[6:8] = jnp.zeros((2, HC), F32)
        out[8:32, : 2 * NS] = rows[:, HC:WIDE]
        out[8:32, 2 * NS :] = jnp.zeros((24, HC - 2 * NS), F32)
        out[32:] = jnp.broadcast_to(local, (8, HC))


def square_kernel(at, a, b, c, d, square):
    refs = (a, b, c, d)
    bc = sum(r[8:32, : 2 * NS] for r in refs)
    total = sum(r[32:, :128] for r in refs)
    square[...] = total + jnp.sum(bc * bc).reshape(1, 1)


def last_kernel(at, a, b, c, d, rows_out, square, all_in, all_bc, all_out, parts):
    x = at[0]
    entries = DM * 1536 + DM * 256 + 1536 * DM
    factor = jnp.minimum(1.0, 1.0 / jnp.sqrt(square[:1, :1] / entries + 1e-06))
    for k, r in enumerate((a, b, c, d)):
        parts[k] = r[...]
    for p in range(NX):
        all_in[:, HC * p : HC * p + HC] = factor * parts[lax.rem(x - p + NX, NX), :6, :]
    rows = sum(r[8:32, : 2 * NS] for r in (a, b, c, d))
    mine = rows[:6]
    for p in range(1, NX):
        mine = jnp.where(x == p, rows[6 * p : 6 * p + 6], mine)
    all_bc[...] = factor * mine
    all_out[:, :HC] = factor * rows_out[:12]
    all_out[:, HC:] = factor * rows_out[12:]


def call(kernel, outs, scratch, args, flops=0):
    moved = sum(a.size * a.dtype.itemsize for a in args)
    return pl.pallas_call(
        kernel,
        out_shape=[jax.ShapeDtypeStruct(*o) for o in outs],
        in_specs=[SMEM] + vm(len(args) - 1),
        out_specs=vm(len(outs)),
        scratch_shapes=[pltpu.VMEM(*s) for s in scratch],
        compiler_params=PARAMS,
        cost_estimate=pl.CostEstimate(flops=flops, bytes_accessed=moved, transcendentals=0),
    )(*args)


def rows_exchange(s_p, s_m, s_2):
    return [move(s_p, "y", 1), move(s_m, "y", -1), move(s_2, "y", 2)]


def deal(at, which, terms, rows, cols):
    axis = {2: "y", 3: "z"}[which]
    p0, p1, p2, p3 = call(
        functools.partial(deal_kernel, which), [((rows, cols), F32)] * 4, [((4, rows, cols), F32)], [at, *terms]
    )
    return [p0, move(p1, axis, 1), move(p2, axis, 2), move(p3, axis, 3)]


def body(tokens, cotangent, log_decay, w_in, w_bc, w_out):
    seq, rec = lax.axis_index("seq"), lax.axis_index("rec")
    x = seq % NX
    at = jnp.stack([x, rec % 2, seq // NX, rec // 2]).astype(jnp.int32)
    tie = lax.optimization_barrier

    t0, c0 = pl.pallas_call(
        pack_kernel,
        out_shape=[jax.ShapeDtypeStruct((SEG + 8, DM), F32), jax.ShapeDtypeStruct((SEG, DM), F32)],
        in_specs=vm(3),
        out_specs=vm(2),
        compiler_params=PARAMS,
    )(tokens[0], cotangent[0], log_decay[0])
    t3, t1 = move(t0, "x", 1), move(t0, "x", -1)
    wi = lax.dynamic_slice(w_in, (0, x * HC), (DM, HC))
    wo = lax.dynamic_slice(w_out, (x * HC, 0), (HC, DM))
    t2 = move(t3, "x", 1)
    c0_l, t1 = tie((c0, t1))
    c1 = move(c0_l, "x", -1)
    c0_r, t2 = tie((c0, t2))
    c3 = move(c0_r, "x", 1)
    c2 = move(c1, "x", -1)

    tall = ((TALL, HC), F32)
    edges = ((2, NX, NS, HC), F32)
    ends = ((NX, NS, 2 * HC), F32)
    cirow, cerow, ci, ce, tokb, xs, xfr, bc, pre_s, *s_rows = call(
        tok_kernel,
        [((NX, 8, SEG), F32), ((NX, 8, SEG), F32), ((NX, SEG, HC), F32), ((NX, SEG, HC), F32),
         ((NX, SEG, DM), BF16), ((NX, SEG, HC), BF16), ((NX, SEG, 2 * HC), BF16), ((NX, SEG, 2 * NS), BF16),
         edges, tall, tall, tall],
        [ends, ((8, SEG), F32)],
        [at, t0, t1, t2, t3, wi, w_bc],
        2 * 1024 * (DM * (HC + 2 * NS) + NS * 2 * HC),
    )
    q_rows = rows_exchange(*s_rows)
    two = [((2, SEG, DM), BF16), ((2, SEG, HC), BF16), ((2, SEG, 2 * HC), BF16)]
    flops = 1024 * (DM * HC + NS * 2 * HC)
    cotb_a, dy_a, dyfr_a, ends_a = call(
        cot_kernel_a, [*two, ((2, NS, 2 * HC), F32)], [ends], [at, c0, c1, wo, ci, ce, bc], flops
    )
    cotb_b, dy_b, dyfr_b, pre_d, *s_rows = call(
        cot_kernel_b, [*two, edges, tall, tall, tall], [ends], [at, c2, c3, wo, ci, ce, bc, ends_a], flops
    )
    p_rows = rows_exchange(*s_rows)
    g_out, dxi, dci, dbi = call(
        inner_kernel,
        [((2, ROWS, HC), F32), ((NX, SEG, HC), F32), ((NX, SEG, NS), F32), ((NX, SEG, NS), F32)],
        [((NX, NS, 2 * HC), BF16), ((NX * SEG, HC), BF16)],
        [at, xs, bc, dy_a, dy_b, dyfr_a, dyfr_b, cotb_a, cotb_b, ci, ce, cirow, cerow, pre_s, *q_rows],
        2 * 1024 * (HC * DM + 5 * SEG * HC + 6 * NS * HC),
    )
    keep, send, dz = call(
        outer_kernel,
        [((ROWS, ALL), F32), ((ROWS, ALL), F32), ((NX, SEG, WIDE), BF16)],
        [((NX, NS, 2 * HC), BF16), ((2, ROWS, WIDE), F32)],
        [at, tokb, xfr, bc, ci, ce, pre_d, *p_rows, dxi, dci, dbi, g_out],
        2 * 1024 * (WIDE * DM + 4 * NS * HC),
    )
    got = move(send, "c", 1)
    whole, half = ((SEG, DM), F32), ((HALF, DM), F32)
    d0, d1, d2a, d2b, d3 = call(
        tokens_kernel, [whole, whole, half, half, whole], [], [at, dz, wi, w_bc], 2 * 1024 * WIDE * DM
    )
    terms = deal(at, 2, [keep, got], 96, ALL)
    r_a, r_b = move(d2a, "x", 1), move(d2b, "x", -1)
    s1, s3 = call(pass_kernel, [whole, whole], [], [at, d1, d3, r_a, r_b])
    m1, m3 = move(s1, "x", 1), move(s3, "x", -1)
    d_tok = (d0 + m1 + m3).astype(BF16)
    terms = deal(at, 3, terms, 24, ALL)
    p0, p1, p2, p3, rows_out = call(
        cut_kernel, [((40, HC), F32)] * 4 + [((24, HC), F32)], [], [at, *terms]
    )
    pieces = [p0, move(p1, "x", 1), move(p2, "x", 2), move(p3, "x", 3)]
    lanes = NX * NY
    pairs = [(r * lanes + i, 2 * NZ * NY * (i % NX) + r * NY + i // NX) for r in range(2 * NZ) for i in range(lanes)]
    rows_out = lax.ppermute(rows_out, ("rec", "seq"), pairs)
    (square,) = call(square_kernel, [((8, 128), F32)], [], [at, *pieces])
    for axis in ("y", "z"):
        square = square + (move(square, axis, 1) + move(square, axis, 3) + move(square, axis, 2))
    square = square + move(square, "c", 1)
    all_in, all_bc, all_out = call(
        last_kernel,
        [((6, NX * HC), F32), ((6, 2 * NS), F32), ((12, DM), F32)],
        [((NX, 40, HC), F32)],
        [at, *pieces, rows_out, square],
    )
    return d_tok[None], all_in, all_bc, all_out


def solution(mesh):
    in_specs = (P("rec", "seq", None), P("rec", "seq", None), P("rec", None, "seq"), P(), P(), P())
    out_specs = (
        P("rec", "seq", None),
        P(("rec", "seq"), None),
        P(("rec", "seq"), None),
        P(("rec", "seq"), None),
    )
    return jax.shard_map(body, mesh=mesh, in_specs=in_specs, out_specs=out_specs, check_vma=False)
```

```python
import functools

import jax
import jax.numpy as jnp
from jax import lax
from jax.experimental import pallas as pl
from jax.experimental.pallas import tpu as pltpu
from jax.sharding import PartitionSpec as P

F32 = jnp.float32
BF16 = jnp.bfloat16
NX = 4
NY = 4
NZ = 4
SEG = 256
HALF = SEG // 2
DM = 768
NS = 128
NH = 6
HD = 64
HC = NH * HD
ROWS = DM // 2
WIDE = HC + 2 * NS
ALL = WIDE + HC
TALL = NS + 8


def shift(axis, step, wrap=True):
    if axis == "c":
        return "rec", [(r, r ^ 1) for r in range(2 * NZ)]
    count, stride, total, name = {
        "x": (NX, 1, NX * NY, "seq"),
        "y": (NY, NX, NX * NY, "seq"),
        "z": (NZ, 2, 2 * NZ, "rec"),
    }[axis]
    pairs = []
    for i in range(total):
        at = (i // stride) % count
        to = at + step
        if not wrap and not 0 <= to < count:
            continue
        pairs.append((i, i + (to % count - at) * stride))
    return name, pairs


def move(value, axis, step, wrap=True):
    name, pairs = shift(axis, step, wrap)
    return lax.ppermute(value, name, pairs)


def dot(a, b, ca, cb):
    return lax.dot_general(a, b, (((ca,), (cb,)), ((), ())), preferred_element_type=F32)


def exact(a, b, ca, cb):
    return lax.dot_general(
        a, b, (((ca,), (cb,)), ((), ())), precision=lax.Precision.HIGHEST, preferred_element_type=F32
    )


def place(p, x):
    k = lax.rem(p - x + NX, NX)
    return k ^ (k >> 1)


def vm(n):
    return [pl.BlockSpec(memory_space=pltpu.VMEM)] * n


SMEM = pl.BlockSpec(memory_space=pltpu.SMEM)
PARAMS = pltpu.CompilerParams(vmem_limit_bytes=20 * 2**20)


def send_rows(up, down, log, y, s_p, s_m, s_2):
    s_p[:NS] = jnp.where(y == NY - 1, down, up)
    s_m[:NS] = jnp.where(y == 0, up, down)
    s_2[:NS] = jnp.where(y < 2, up, down)
    log = jnp.broadcast_to(log, (8, HC))
    for s in (s_p, s_m, s_2):
        s[NS:] = log


def from_rows(r_p, r_m, r_2, y):
    def on(yes):
        return jnp.where(yes, 1.0, 0.0).astype(F32)

    l_p, l_m, l_2 = (r[NS : NS + 1, :] for r in (r_p, r_m, r_2))
    v_p, v_m, v_2 = (r[:NS, :] for r in (r_p, r_m, r_2))
    up = v_p * on(y >= 1) + v_2 * (on(y >= 2) * jnp.exp(l_p)) + v_m * (on(y == 3) * jnp.exp(l_p + l_2))
    down = v_m * on(y <= 2) + v_2 * (on(y <= 1) * jnp.exp(l_m)) + v_p * (on(y == 0) * jnp.exp(l_m + l_2))
    return up, down


def row_scan(order, ends, cols, ci, x, pre, which):
    acc = jnp.zeros((NS, HC), F32)
    for p in order:
        k = place(p, x)
        pre[which, k] = acc
        acc = acc * jnp.exp(ci[k, SEG - 1 : SEG, :]) + ends[k, :, cols]
    return acc


def row_log(ci):
    return sum(ci[k, SEG - 1 : SEG, :] for k in range(NX))


FIRST, SECOND = slice(0, HC), slice(HC, 2 * HC)


def pack_kernel(tok, log, out):
    out[:SEG] = tok[...].astype(F32)
    for part in range(3):
        out[SEG:, SEG * part : SEG * part + SEG] = log[8 * part : 8 * part + 8]


def decays(x, toks, first, cirow, cerow, ci, ce, la):
    s = lax.broadcasted_iota(jnp.int32, (SEG, SEG), 0)
    t = lax.broadcasted_iota(jnp.int32, (SEG, SEG), 1)
    tri = jnp.where(s <= t, 1.0, 0.0).astype(F32)
    head = lax.broadcasted_iota(jnp.int32, (8, HC), 0) * HD
    lane = lax.broadcasted_iota(jnp.int32, (8, HC), 1)
    spread = jnp.where((lane >= head) & (lane < head + HD), 1.0, 0.0).astype(F32)
    la[...] = jnp.zeros((8, SEG), F32)
    for k, tok in enumerate(toks, first):
        for j in range(NH):
            mine = jnp.zeros((1, SEG), F32)
            for p in range(NX):
                row, part = (NH * p + j) % 8, (NH * p + j) // 8
                its = tok[SEG + row : SEG + row + 1, SEG * part : SEG * part + SEG]
                mine = jnp.where(x == p, its, mine)
            la[j : j + 1] = mine
        through = exact(la[...], tri, 1, 0)
        before = through - la[...]
        cirow[k] = through
        cerow[k] = before
        ci[k] = exact(through, spread, 0, 0)
        ce[k] = exact(before, spread, 0, 0)


def tok_part(at, toks, first, w_in, w_bc, cirow, cerow, ci, ce, tokb, xs, xfr, bc, ends, la):
    decays(at[0], toks, first, cirow, cerow, ci, ce, la)
    for k, t in enumerate(toks, first):
        tokb[k] = t[:SEG].astype(BF16)

    def segment(i, _):
        k = first + i
        t = tokb[k]
        xv = dot(t, w_in[...], 1, 0).astype(BF16)
        bv = dot(t, w_bc[...], 1, 0).astype(BF16)
        xs[k] = xv
        bc[k] = bv
        xf = xv.astype(F32)
        last = ci[k, SEG - 1 : SEG, :]
        xfr[k, :, :HC] = (xf * jnp.exp(last - ci[k])).astype(BF16)
        xfr[k, :, HC:] = (xf * jnp.exp(ce[k])).astype(BF16)
        ends[k] = dot(bv[:, :NS], xfr[k], 0, 0)
        return 0

    lax.fori_loop(0, len(toks), segment, 0)


def tok_kernel_a(at, t0, t1, t3, w_in, w_bc, *refs):
    tok_part(at, (t0, t1, t3), 0, w_in, w_bc, *refs)


def tok_kernel_b(at, t2, w_in, w_bc, *refs):
    given, full, (pre, s_p, s_m, s_2, ends, la) = refs[:9], refs[9:17], refs[17:]
    full = (*full, ends)
    for a, b in zip(given, full, strict=True):
        b[: NX - 1] = a[...]
    tok_part(at, (t2,), NX - 1, w_in, w_bc, *full, la)
    x, y, ci = at[0], at[2], full[2]
    up = row_scan(range(NX), ends, FIRST, ci, x, pre, 0)
    down = row_scan(reversed(range(NX)), ends, SECOND, ci, x, pre, 1)
    send_rows(up, down, row_log(ci), y, s_p, s_m, s_2)


def cot_part(cots, first, w_out, ci, ce, bc, cotb, dy, dyfr, ends):
    for i, t in enumerate(cots):
        cotb[i] = t[...].astype(BF16)

    def segment(i, _):
        k = first + i
        d = dot(cotb[i], w_out[...], 1, 1)
        dy[i] = d.astype(BF16)
        last = ci[k, SEG - 1 : SEG, :]
        dyfr[i, :, :HC] = (d * jnp.exp(ci[k])).astype(BF16)
        dyfr[i, :, HC:] = (d * jnp.exp(last - ce[k])).astype(BF16)
        ends[k] = dot(bc[k, :, NS:], dyfr[i], 0, 0)
        return 0

    lax.fori_loop(0, len(cots), segment, 0)


def cot_kernel_a(at, c0, c1, w_out, ci, ce, bc, cotb, dy, dyfr, ends_a, ends):
    cot_part((c0, c1), 0, w_out, ci, ce, bc, cotb, dy, dyfr, ends)
    ends_a[...] = ends[:2]


def cot_kernel_b(
    at, c2, c3, w_out, ci, ce, bc, ends_a, cotb, dy, dyfr, pre, s_p, s_m, s_2, ends
):
    x, y = at[0], at[2]
    ends[:2] = ends_a[...]
    cot_part((c2, c3), 2, w_out, ci, ce, bc, cotb, dy, dyfr, ends)
    down = row_scan(reversed(range(NX)), ends, FIRST, ci, x, pre, 0)
    up = row_scan(range(NX), ends, SECOND, ci, x, pre, 1)
    send_rows(up, down, row_log(ci), y, s_p, s_m, s_2)


def enter(pre, which, q, ci, x, order, out, cols):
    log = jnp.zeros((1, HC), F32)
    for p in order:
        k = place(p, x)
        out[k, :, cols] = (pre[which, k] + q * jnp.exp(log)).astype(BF16)
        log = log + ci[k, SEG - 1 : SEG, :]


def blocks():
    return [(j, j // 4 % 2, (4 * (j % 4) + j // 8) * 24) for j in range(2 * NZ * NY)]


def inner_kernel(
    at, xs, bc, dy_a, dy_b, dyfr_a, dyfr_b, cotb_a, cotb_b, ci, ce, cirow, cerow, pre, r_p, r_m, r_2,
    g, dxi, dci, dbi, sr, yb,
):
    x, y_at = at[0], at[2]
    up, down = from_rows(r_p, r_m, r_2, y_at)
    enter(pre, 0, up, ci, x, range(NX), sr, pl.ds(0, HC))
    enter(pre, 1, down, ci, x, reversed(range(NX)), sr, pl.ds(HC, HC))

    def run(first, dy, dyfr):
        def segment(i, _):
            k = first + i
            b, c = bc[k, :, :NS], bc[k, :, NS:]
            t = lax.broadcasted_iota(jnp.int32, (SEG, SEG), 0)
            s = lax.broadcasted_iota(jnp.int32, (SEG, SEG), 1)
            low, same = t > s, t == s
            scores = dot(c, b, 1, 1)
            scores = jnp.where(same, 2.0 * scores, scores)
            lane = lax.broadcasted_iota(jnp.int32, (SEG, 2 * HD), 1)
            carry = dot(c, sr[k], 1, 0)
            total = jnp.zeros((SEG, SEG), F32)
            for pair in range(NH // 2):
                cols = slice(pair * 2 * HD, (pair + 1) * 2 * HD)
                xp, dp = xs[k, :, cols], dy[i, :, cols]
                ws, xm, dm = [], [], []
                for j in range(2):
                    h = 2 * pair + j
                    at_t = slice(h * HD, h * HD + 1)
                    diff = jnp.where(
                        low,
                        ci[k, :, at_t] - cirow[k, h : h + 1, :],
                        cerow[k, h : h + 1, :] - ce[k, :, at_t],
                    )
                    decay = jnp.exp(diff)
                    mine = (lane < HD) if j == 0 else (lane >= HD)
                    xm.append(jnp.where(mine, xp, jnp.zeros_like(xp)))
                    dm.append(jnp.where(mine, dp, jnp.zeros_like(dp)))
                    ws.append((decay * scores).astype(BF16))
                    total = total + decay * dot(dm[j], xp, 1, 1)
                y = dot(ws[0], xm[0], 1, 0) + dot(ws[1], xm[1], 1, 0)
                last = ci[k, SEG - 1 : SEG, cols]
                y = y + carry[:, cols] * jnp.exp(ci[k, :, cols])
                y = y + carry[:, slice(HC + cols.start, HC + cols.stop)] * jnp.exp(last - ce[k, :, cols])
                yb[pl.ds(k * SEG, SEG), cols] = y.astype(BF16)
                dxi[k, :, cols] = dot(ws[0], dm[0], 0, 0) + dot(ws[1], dm[1], 0, 0)
            total = jnp.where(same, 2.0 * total, total).astype(BF16)
            dci[k] = dot(total, b, 1, 0) + dot(dyfr[i], sr[k], 1, 1)
            dbi[k] = dot(total, c, 0, 0)
            return 0

        lax.fori_loop(0, 2, segment, 0)

    run(0, dy_a, dyfr_a)
    run(2, dy_b, dyfr_b)
    half = 2 * SEG
    raw = dot(yb[:half, :], cotb_a[...].reshape(half, DM), 0, 0)
    raw = raw + dot(yb[half:, :], cotb_b[...].reshape(half, DM), 0, 0)
    for j, c, row in blocks():
        g[c, row : row + 12, :] = raw[12 * j : 12 * j + 12, :HC]
        g[c, row + 12 : row + 24, :] = raw[12 * j : 12 * j + 12, HC:]


def outer_kernel(
    at, tokb, xfr, bc, ci, ce, pre, r_p, r_m, r_2, dxi, dci, dbi, g_out, keep, send, dz, ds, g
):
    x, core, y_at = at[0], at[1], at[2]
    up, down = from_rows(r_p, r_m, r_2, y_at)
    enter(pre, 0, down, ci, x, reversed(range(NX)), ds, pl.ds(0, HC))
    enter(pre, 1, up, ci, x, range(NX), ds, pl.ds(HC, HC))

    def segment(k, _):
        b = bc[k, :, :NS]
        last = ci[k, SEG - 1 : SEG, :]
        back = dot(b, ds[k], 1, 0)
        dx = dxi[k] + back[:, :HC] * jnp.exp(last - ci[k]) + back[:, HC:] * jnp.exp(ce[k])
        dz[k, :, :HC] = dx.astype(BF16)
        dz[k, :, HC : HC + NS] = (dbi[k] + dot(xfr[k], ds[k], 1, 1)).astype(BF16)
        dz[k, :, HC + NS :] = dci[k].astype(BF16)
        return 0

    lax.fori_loop(0, NX, segment, 0)
    raw = dot(tokb[...].reshape(NX * SEG, DM), dz[...].reshape(NX * SEG, WIDE), 0, 0)
    for j, c, row in blocks():
        g[c, row : row + 24, :] = raw[24 * j : 24 * j + 24, :]
    for out, c in ((keep, core), (send, 1 - core)):
        out[:, :WIDE] = g[c]
        out[:, WIDE:] = g_out[c]


def tokens_kernel(at, dz, w_in, w_bc, d0, d1, d2a, d2b, d3):
    def tokens_of(k):
        return dot(dz[k, :, :HC], w_in[...], 1, 1) + dot(dz[k, :, HC:], w_bc[...], 1, 1)

    d = tokens_of(3)
    d2a[...] = d[:HALF]
    d2b[...] = d[HALF:]
    d1[...] = tokens_of(1)
    d3[...] = tokens_of(2)
    d0[...] = tokens_of(0)


def pass_kernel(at, d1, d3, r_a, r_b, s1, s3):
    s1[:HALF] = d1[:HALF] + r_a[...]
    s1[HALF:] = d1[HALF:]
    s3[:HALF] = d3[:HALF]
    s3[HALF:] = d3[HALF:] + r_b[...]


def deal_kernel(which, at, *refs):
    terms, outs, total = refs[:-5], refs[-5:-1], refs[-1]
    acc = terms[0][...]
    for term in terms[1:]:
        acc = acc + term[...]
    total[...] = acc.reshape(total.shape)
    for k, out in enumerate(outs):
        out[...] = total[lax.rem(at[which] + k, 4)]


def cut_kernel(at, a, b, c, d, p0, p1, p2, p3, rows_out):
    rows = a[...] + b[...] + c[...] + d[...]
    mine, of_out = rows[:, :HC], rows[:, WIDE:]
    rows_out[...] = of_out
    local = (jnp.sum(mine * mine) + jnp.sum(of_out * of_out)).reshape(1, 1)
    for k, out in enumerate((p0, p1, p2, p3)):
        to = lax.rem(at[0] + k, NX)
        part = mine[:6]
        for p in range(1, NX):
            part = jnp.where(to == p, mine[6 * p : 6 * p + 6], part)
        out[:6] = part
        out[6:8] = jnp.zeros((2, HC), F32)
        out[8:32, : 2 * NS] = rows[:, HC:WIDE]
        out[8:32, 2 * NS :] = jnp.zeros((24, HC - 2 * NS), F32)
        out[32:] = jnp.broadcast_to(local, (8, HC))


def square_kernel(at, a, b, c, d, square):
    refs = (a, b, c, d)
    bc = sum(r[8:32, : 2 * NS] for r in refs)
    total = sum(r[32:, :128] for r in refs)
    square[...] = total + jnp.sum(bc * bc).reshape(1, 1)


def last_kernel(at, a, b, c, d, rows_out, square, all_in, all_bc, all_out, parts):
    x = at[0]
    entries = DM * 1536 + DM * 256 + 1536 * DM
    factor = jnp.minimum(1.0, 1.0 / jnp.sqrt(square[:1, :1] / entries + 1e-06))
    for k, r in enumerate((a, b, c, d)):
        parts[k] = r[...]
    for p in range(NX):
        all_in[:, HC * p : HC * p + HC] = factor * parts[lax.rem(x - p + NX, NX), :6, :]
    rows = sum(r[8:32, : 2 * NS] for r in (a, b, c, d))
    mine = rows[:6]
    for p in range(1, NX):
        mine = jnp.where(x == p, rows[6 * p : 6 * p + 6], mine)
    all_bc[...] = factor * mine
    all_out[:, :HC] = factor * rows_out[:12]
    all_out[:, HC:] = factor * rows_out[12:]


def call(kernel, outs, scratch, args, flops=0):
    moved = sum(a.size * a.dtype.itemsize for a in args)
    return pl.pallas_call(
        kernel,
        out_shape=[jax.ShapeDtypeStruct(*o) for o in outs],
        in_specs=[SMEM] + vm(len(args) - 1),
        out_specs=vm(len(outs)),
        scratch_shapes=[pltpu.VMEM(*s) for s in scratch],
        compiler_params=PARAMS,
        cost_estimate=pl.CostEstimate(flops=flops, bytes_accessed=moved, transcendentals=0),
    )(*args)


def rows_exchange(s_p, s_m, s_2):
    return [move(s_p, "y", 1), move(s_m, "y", -1), move(s_2, "y", 2)]


def deal(at, which, terms, rows, cols):
    axis = {2: "y", 3: "z"}[which]
    p0, p1, p2, p3 = call(
        functools.partial(deal_kernel, which), [((rows, cols), F32)] * 4, [((4, rows, cols), F32)], [at, *terms]
    )
    return [p0, move(p1, axis, 1), move(p2, axis, 2), move(p3, axis, 3)]


def body(tokens, cotangent, log_decay, w_in, w_bc, w_out):
    seq, rec = lax.axis_index("seq"), lax.axis_index("rec")
    x = seq % NX
    at = jnp.stack([x, rec % 2, seq // NX, rec // 2]).astype(jnp.int32)
    tie = lax.optimization_barrier

    (t0,) = pl.pallas_call(
        pack_kernel,
        out_shape=[jax.ShapeDtypeStruct((SEG + 8, DM), F32)],
        in_specs=vm(2),
        out_specs=vm(1),
        compiler_params=PARAMS,
    )(tokens[0], log_decay[0])
    c0 = cotangent[0].astype(F32)
    wi = lax.dynamic_slice(w_in, (0, x * HC), (DM, HC))
    wo = lax.dynamic_slice(w_out, (x * HC, 0), (HC, DM))
    t3, t1 = move(t0, "x", 1), move(t0, "x", -1)
    t3, t1, c0 = tie((t3, t1, c0))
    t2 = move(t3, "x", 1)
    c1 = move(c0, "x", -1)
    t1, wi, wo = tie((t1, wi, wo))

    tall = ((TALL, HC), F32)
    edges = ((2, NX, NS, HC), F32)

    def of_tokens(n):
        return [
            ((n, 8, SEG), F32), ((n, 8, SEG), F32), ((n, SEG, HC), F32), ((n, SEG, HC), F32),
            ((n, SEG, DM), BF16), ((n, SEG, HC), BF16), ((n, SEG, 2 * HC), BF16), ((n, SEG, 2 * NS), BF16),
        ]

    def ends(n):
        return ((n, NS, 2 * HC), F32)

    flops = 2 * SEG * (DM * (HC + 2 * NS) + NS * 2 * HC)
    row = ((8, SEG), F32)
    three = call(
        tok_kernel_a, [*of_tokens(3), ends(3)], [row], [at, t0, t1, t3, wi, w_bc], 3 * flops
    )
    c0_r, t2, c1, *three = tie((c0, t2, c1, *three))
    c3, c2 = move(c0_r, "x", 1), move(c1, "x", -1)
    cirow, cerow, ci, ce, tokb, xs, xfr, bc, pre_s, *s_rows = call(
        tok_kernel_b, [*of_tokens(4), edges, tall, tall, tall], [ends(4), row], [at, t2, wi, w_bc, *three], flops
    )
    q_rows = rows_exchange(*s_rows)
    two = [((2, SEG, DM), BF16), ((2, SEG, HC), BF16), ((2, SEG, 2 * HC), BF16)]
    flops = 1024 * (DM * HC + NS * 2 * HC)
    cotb_a, dy_a, dyfr_a, ends_a = call(
        cot_kernel_a, [*two, ends(2)], [ends(4)], [at, c0, c1, wo, ci, ce, bc], flops
    )
    cotb_b, dy_b, dyfr_b, pre_d, *s_rows = call(
        cot_kernel_b, [*two, edges, tall, tall, tall], [ends(4)], [at, c3, c2, wo, ci, ce, bc, ends_a], flops
    )
    p_rows = rows_exchange(*s_rows)
    g_out, dxi, dci, dbi = call(
        inner_kernel,
        [((2, ROWS, HC), F32), ((NX, SEG, HC), F32), ((NX, SEG, NS), F32), ((NX, SEG, NS), F32)],
        [((NX, NS, 2 * HC), BF16), ((NX * SEG, HC), BF16)],
        [at, xs, bc, dy_a, dy_b, dyfr_a, dyfr_b, cotb_a, cotb_b, ci, ce, cirow, cerow, pre_s, *q_rows],
        2 * 1024 * (HC * DM + 5 * SEG * HC + 6 * NS * HC),
    )
    keep, send, dz = call(
        outer_kernel,
        [((ROWS, ALL), F32), ((ROWS, ALL), F32), ((NX, SEG, WIDE), BF16)],
        [((NX, NS, 2 * HC), BF16), ((2, ROWS, WIDE), F32)],
        [at, tokb, xfr, bc, ci, ce, pre_d, *p_rows, dxi, dci, dbi, g_out],
        2 * 1024 * (WIDE * DM + 4 * NS * HC),
    )
    got = move(send, "c", 1)
    whole, half = ((SEG, DM), F32), ((HALF, DM), F32)
    d0, d1, d2a, d2b, d3 = call(
        tokens_kernel, [whole, whole, half, half, whole], [], [at, dz, wi, w_bc], 2 * 1024 * WIDE * DM
    )
    terms = deal(at, 2, [keep, got], 96, ALL)
    r_a, r_b = move(d2a, "x", 1), move(d2b, "x", -1)
    s1, s3 = call(pass_kernel, [whole, whole], [], [at, d1, d3, r_a, r_b])
    m1, m3 = move(s1, "x", 1), move(s3, "x", -1)
    d_tok = (d0 + m1 + m3).astype(BF16)
    terms = deal(at, 3, terms, 24, ALL)
    p0, p1, p2, p3, rows_out = call(
        cut_kernel, [((40, HC), F32)] * 4 + [((24, HC), F32)], [], [at, *terms]
    )
    pieces = [p0, move(p1, "x", 1), move(p2, "x", 2), move(p3, "x", 3)]
    lanes = NX * NY
    pairs = [(r * lanes + i, 2 * NZ * NY * (i % NX) + r * NY + i // NX) for r in range(2 * NZ) for i in range(lanes)]
    rows_out = lax.ppermute(rows_out, ("rec", "seq"), pairs)
    (square,) = call(square_kernel, [((8, 128), F32)], [], [at, *pieces])
    for axis in ("y", "z"):
        square = square + (move(square, axis, 1) + move(square, axis, 3) + move(square, axis, 2))
    square = square + move(square, "c", 1)
    all_in, all_bc, all_out = call(
        last_kernel,
        [((6, NX * HC), F32), ((6, 2 * NS), F32), ((12, DM), F32)],
        [((NX, 40, HC), F32)],
        [at, *pieces, rows_out, square],
    )
    return d_tok[None], all_in, all_bc, all_out


def solution(mesh):
    in_specs = (P("rec", "seq", None), P("rec", "seq", None), P("rec", None, "seq"), P(), P(), P())
    out_specs = (
        P("rec", "seq", None),
        P(("rec", "seq"), None),
        P(("rec", "seq"), None),
        P(("rec", "seq"), None),
    )
    return jax.shard_map(body, mesh=mesh, in_specs=in_specs, out_specs=out_specs, check_vma=False)
```

```python
import functools

import jax
import jax.numpy as jnp
from jax import lax
from jax.experimental import pallas as pl
from jax.experimental.pallas import tpu as pltpu
from jax.sharding import PartitionSpec as P

F32 = jnp.float32
BF16 = jnp.bfloat16
NX = 4
NY = 4
NZ = 4
SEG = 256
HALF = SEG // 2
DM = 768
NS = 128
NH = 6
HD = 64
HC = NH * HD
ROWS = DM // 2
WIDE = HC + 2 * NS
ALL = WIDE + HC
TALL = NS + 8


def shift(axis, step, wrap=True):
    if axis == "c":
        return "rec", [(r, r ^ 1) for r in range(2 * NZ)]
    count, stride, total, name = {
        "x": (NX, 1, NX * NY, "seq"),
        "y": (NY, NX, NX * NY, "seq"),
        "z": (NZ, 2, 2 * NZ, "rec"),
    }[axis]
    pairs = []
    for i in range(total):
        at = (i // stride) % count
        to = at + step
        if not wrap and not 0 <= to < count:
            continue
        pairs.append((i, i + (to % count - at) * stride))
    return name, pairs


def move(value, axis, step, wrap=True):
    name, pairs = shift(axis, step, wrap)
    return lax.ppermute(value, name, pairs)


def dot(a, b, ca, cb):
    return lax.dot_general(a, b, (((ca,), (cb,)), ((), ())), preferred_element_type=F32)


def exact(a, b, ca, cb):
    return lax.dot_general(
        a, b, (((ca,), (cb,)), ((), ())), precision=lax.Precision.HIGHEST, preferred_element_type=F32
    )


def place(p, x):
    k = lax.rem(p - x + NX, NX)
    return k ^ (k >> 1)


def vm(n):
    return [pl.BlockSpec(memory_space=pltpu.VMEM)] * n


SMEM = pl.BlockSpec(memory_space=pltpu.SMEM)
PARAMS = pltpu.CompilerParams(vmem_limit_bytes=20 * 2**20)


def send_rows(up, down, log, y, s_p, s_m, s_2):
    s_p[:NS] = jnp.where(y == NY - 1, down, up)
    s_m[:NS] = jnp.where(y == 0, up, down)
    s_2[:NS] = jnp.where(y < 2, up, down)
    log = jnp.broadcast_to(log, (8, HC))
    for s in (s_p, s_m, s_2):
        s[NS:] = log


def from_rows(r_p, r_m, r_2, y):
    def on(yes):
        return jnp.where(yes, 1.0, 0.0).astype(F32)

    l_p, l_m, l_2 = (r[NS : NS + 1, :] for r in (r_p, r_m, r_2))
    v_p, v_m, v_2 = (r[:NS, :] for r in (r_p, r_m, r_2))
    up = v_p * on(y >= 1) + v_2 * (on(y >= 2) * jnp.exp(l_p)) + v_m * (on(y == 3) * jnp.exp(l_p + l_2))
    down = v_m * on(y <= 2) + v_2 * (on(y <= 1) * jnp.exp(l_m)) + v_p * (on(y == 0) * jnp.exp(l_m + l_2))
    return up, down


def row_scan(order, ends, cols, ci, x, pre, which):
    acc = jnp.zeros((NS, HC), F32)
    for p in order:
        k = place(p, x)
        pre[which, k] = acc
        acc = acc * jnp.exp(ci[k, SEG - 1 : SEG, :]) + ends[k, :, cols]
    return acc


def row_log(ci):
    return sum(ci[k, SEG - 1 : SEG, :] for k in range(NX))


FIRST, SECOND = slice(0, HC), slice(HC, 2 * HC)


def pack_kernel(tok, log, out):
    out[:SEG] = tok[...].astype(F32)
    for part in range(3):
        out[SEG:, SEG * part : SEG * part + SEG] = log[8 * part : 8 * part + 8]


def decays(x, toks, own, first, cirow, cerow, ci, ce, la):
    s = lax.broadcasted_iota(jnp.int32, (SEG, SEG), 0)
    t = lax.broadcasted_iota(jnp.int32, (SEG, SEG), 1)
    tri = jnp.where(s <= t, 1.0, 0.0).astype(F32)
    head = lax.broadcasted_iota(jnp.int32, (8, HC), 0) * HD
    lane = lax.broadcasted_iota(jnp.int32, (8, HC), 1)
    spread = jnp.where((lane >= head) & (lane < head + HD), 1.0, 0.0).astype(F32)
    la[...] = jnp.zeros((8, SEG), F32)
    for k, tok in enumerate(toks, first):
        for j in range(NH):
            mine = jnp.zeros((1, SEG), F32)
            for p in range(NX):
                h = NH * p + j
                if tok.shape[0] > SEG:
                    row, part = SEG + h % 8, h // 8
                    its = tok[row : row + 1, SEG * part : SEG * part + SEG]
                else:
                    its = own[h : h + 1]
                mine = jnp.where(x == p, its, mine)
            la[j : j + 1] = mine
        through = exact(la[...], tri, 1, 0)
        before = through - la[...]
        cirow[k] = through
        cerow[k] = before
        ci[k] = exact(through, spread, 0, 0)
        ce[k] = exact(before, spread, 0, 0)


def tok_part(at, toks, own, first, w_in, w_bc, cirow, cerow, ci, ce, tokb, xs, xfr, bc, ends, la):
    decays(at[0], toks, own, first, cirow, cerow, ci, ce, la)
    for k, t in enumerate(toks, first):
        tokb[k] = t[:SEG].astype(BF16)

    def segment(i, _):
        k = first + i
        t = tokb[k]
        xv = dot(t, w_in[...], 1, 0).astype(BF16)
        bv = dot(t, w_bc[...], 1, 0).astype(BF16)
        xs[k] = xv
        bc[k] = bv
        xf = xv.astype(F32)
        last = ci[k, SEG - 1 : SEG, :]
        xfr[k, :, :HC] = (xf * jnp.exp(last - ci[k])).astype(BF16)
        xfr[k, :, HC:] = (xf * jnp.exp(ce[k])).astype(BF16)
        ends[k] = dot(bv[:, :NS], xfr[k], 0, 0)
        return 0

    lax.fori_loop(0, len(toks), segment, 0)


def tok_kernel_a(at, t0, own, t1, t3, w_in, w_bc, *refs):
    tok_part(at, (t0, t1, t3), own, 0, w_in, w_bc, *refs)


def tok_kernel_b(at, t2, w_in, w_bc, *refs):
    given, full, (pre, s_p, s_m, s_2, ends, la) = refs[:9], refs[9:17], refs[17:]
    full = (*full, ends)
    for a, b in zip(given, full, strict=True):
        b[: NX - 1] = a[...]
    tok_part(at, (t2,), None, NX - 1, w_in, w_bc, *full, la)
    x, y, ci = at[0], at[2], full[2]
    up = row_scan(range(NX), ends, FIRST, ci, x, pre, 0)
    down = row_scan(reversed(range(NX)), ends, SECOND, ci, x, pre, 1)
    send_rows(up, down, row_log(ci), y, s_p, s_m, s_2)


def decay_kernel(first, count, at, cirow, cerow, ci, ce, xs, bc, mat, mat_t, y):
    def segment(i, _):
        k = first + i
        b, c = bc[k, :, :NS], bc[k, :, NS:]
        t = lax.broadcasted_iota(jnp.int32, (SEG, SEG), 0)
        s = lax.broadcasted_iota(jnp.int32, (SEG, SEG), 1)
        low, same = t > s, t == s
        scores = dot(c, b, 1, 1)
        lane = lax.broadcasted_iota(jnp.int32, (SEG, 2 * HD), 1)
        for pair in range(NH // 2):
            cols = slice(pair * 2 * HD, (pair + 1) * 2 * HD)
            xp = xs[k, :, cols]
            rows = jnp.zeros((SEG, 2 * HD), F32)
            for j in range(2):
                h = 2 * pair + j
                at_t = slice(h * HD, h * HD + 1)
                diff = jnp.where(
                    low,
                    ci[k, :, at_t] - cirow[k, h : h + 1, :],
                    cerow[k, h : h + 1, :] - ce[k, :, at_t],
                )
                decay = jnp.where(same, 2.0, jnp.exp(diff))
                mat[i, h] = decay.astype(BF16)
                w = (decay * scores).astype(BF16)
                mat_t[i, h] = w.T
                xm = jnp.where((lane < HD) if j == 0 else (lane >= HD), xp, jnp.zeros_like(xp))
                rows = rows + dot(w, xm, 1, 0)
            y[i, :, cols] = rows
        return 0

    lax.fori_loop(0, count, segment, 0)


def cot_part(cots, first, w_out, ci, ce, bc, cotb, dy, dyfr, ends):
    for i, t in enumerate(cots):
        cotb[i] = t[...].astype(BF16)

    def segment(i, _):
        k = first + i
        d = dot(cotb[i], w_out[...], 1, 1)
        dy[i] = d.astype(BF16)
        last = ci[k, SEG - 1 : SEG, :]
        dyfr[i, :, :HC] = (d * jnp.exp(ci[k])).astype(BF16)
        dyfr[i, :, HC:] = (d * jnp.exp(last - ce[k])).astype(BF16)
        ends[k] = dot(bc[k, :, NS:], dyfr[i], 0, 0)
        return 0

    lax.fori_loop(0, len(cots), segment, 0)


def cot_kernel_a(at, c0, c1, w_out, ci, ce, bc, cotb, dy, dyfr, ends_a, ends):
    cot_part((c0, c1), 0, w_out, ci, ce, bc, cotb, dy, dyfr, ends)
    ends_a[...] = ends[:2]


def cot_kernel_b(
    at, c2, c3, w_out, ci, ce, bc, ends_a, cotb, dy, dyfr, pre, s_p, s_m, s_2, ends
):
    x, y = at[0], at[2]
    ends[:2] = ends_a[...]
    cot_part((c2, c3), 2, w_out, ci, ce, bc, cotb, dy, dyfr, ends)
    down = row_scan(reversed(range(NX)), ends, FIRST, ci, x, pre, 0)
    up = row_scan(range(NX), ends, SECOND, ci, x, pre, 1)
    send_rows(up, down, row_log(ci), y, s_p, s_m, s_2)


def enter(pre, which, q, ci, x, order, out, cols):
    log = jnp.zeros((1, HC), F32)
    for p in order:
        k = place(p, x)
        out[k, :, cols] = (pre[which, k] + q * jnp.exp(log)).astype(BF16)
        log = log + ci[k, SEG - 1 : SEG, :]


def blocks():
    return [(j, j // 4 % 2, (4 * (j % 4) + j // 8) * 24) for j in range(2 * NZ * NY)]


def inner_kernel(
    at, xs, bc, dy_a, dy_b, dyfr_a, dyfr_b, cotb_a, cotb_b, ci, ce, pre, r_p, r_m, r_2,
    mat_a, mat_t_a, y_a, mat_b, mat_t_b, y_b,
    g, dxi, dci, dbi, sr, yb,
):
    x, y_at = at[0], at[2]
    up, down = from_rows(r_p, r_m, r_2, y_at)
    enter(pre, 0, up, ci, x, range(NX), sr, pl.ds(0, HC))
    enter(pre, 1, down, ci, x, reversed(range(NX)), sr, pl.ds(HC, HC))

    def run(first, count, mat, mat_t, y_in, m0, dy, dyfr, d0):
        def segment(n, _):
            k, m, i = first + n, m0 + n, d0 + n
            b, c = bc[k, :, :NS], bc[k, :, NS:]
            lane = lax.broadcasted_iota(jnp.int32, (SEG, 2 * HD), 1)
            carry = dot(c, sr[k], 1, 0)
            total = jnp.zeros((SEG, SEG), F32)
            for pair in range(NH // 2):
                cols = slice(pair * 2 * HD, (pair + 1) * 2 * HD)
                xp, dp = xs[k, :, cols], dy[i, :, cols]
                dx = jnp.zeros((SEG, 2 * HD), F32)
                for j in range(2):
                    h = 2 * pair + j
                    dm = jnp.where((lane < HD) if j == 0 else (lane >= HD), dp, jnp.zeros_like(dp))
                    total = total + mat[m, h].astype(F32) * dot(dm, xp, 1, 1)
                    dx = dx + dot(mat_t[m, h], dm, 1, 0)
                last = ci[k, SEG - 1 : SEG, cols]
                y = y_in[m, :, cols] + carry[:, cols] * jnp.exp(ci[k, :, cols])
                y = y + carry[:, slice(HC + cols.start, HC + cols.stop)] * jnp.exp(last - ce[k, :, cols])
                yb[pl.ds(k * SEG, SEG), cols] = y.astype(BF16)
                dxi[k, :, cols] = dx
            total = total.astype(BF16)
            dci[k] = dot(total, b, 1, 0) + dot(dyfr[i], sr[k], 1, 1)
            dbi[k] = dot(total, c, 0, 0)
            return 0

        lax.fori_loop(0, count, segment, 0)

    run(0, 2, mat_a, mat_t_a, y_a, 0, dy_a, dyfr_a, 0)
    run(2, 1, mat_a, mat_t_a, y_a, 2, dy_b, dyfr_b, 0)
    run(3, 1, mat_b, mat_t_b, y_b, 0, dy_b, dyfr_b, 1)
    half = 2 * SEG
    raw = dot(yb[:half, :], cotb_a[...].reshape(half, DM), 0, 0)
    raw = raw + dot(yb[half:, :], cotb_b[...].reshape(half, DM), 0, 0)
    for j, c, row in blocks():
        g[c, row : row + 12, :] = raw[12 * j : 12 * j + 12, :HC]
        g[c, row + 12 : row + 24, :] = raw[12 * j : 12 * j + 12, HC:]


def outer_kernel(
    at, tokb, xfr, bc, ci, ce, pre, r_p, r_m, r_2, dxi, dci, dbi, g_out, keep, send, dz, ds, g
):
    x, core, y_at = at[0], at[1], at[2]
    up, down = from_rows(r_p, r_m, r_2, y_at)
    enter(pre, 0, down, ci, x, reversed(range(NX)), ds, pl.ds(0, HC))
    enter(pre, 1, up, ci, x, range(NX), ds, pl.ds(HC, HC))

    def segment(k, _):
        b = bc[k, :, :NS]
        last = ci[k, SEG - 1 : SEG, :]
        back = dot(b, ds[k], 1, 0)
        dx = dxi[k] + back[:, :HC] * jnp.exp(last - ci[k]) + back[:, HC:] * jnp.exp(ce[k])
        dz[k, :, :HC] = dx.astype(BF16)
        dz[k, :, HC : HC + NS] = (dbi[k] + dot(xfr[k], ds[k], 1, 1)).astype(BF16)
        dz[k, :, HC + NS :] = dci[k].astype(BF16)
        return 0

    lax.fori_loop(0, NX, segment, 0)
    raw = dot(tokb[...].reshape(NX * SEG, DM), dz[...].reshape(NX * SEG, WIDE), 0, 0)
    for j, c, row in blocks():
        g[c, row : row + 24, :] = raw[24 * j : 24 * j + 24, :]
    for out, c in ((keep, core), (send, 1 - core)):
        out[:, :WIDE] = g[c]
        out[:, WIDE:] = g_out[c]


def tokens_kernel(at, dz, w_in, w_bc, d0, d1, d2a, d2b, d3):
    def tokens_of(k):
        return dot(dz[k, :, :HC], w_in[...], 1, 1) + dot(dz[k, :, HC:], w_bc[...], 1, 1)

    d = tokens_of(3)
    d2a[...] = d[:HALF]
    d2b[...] = d[HALF:]
    d1[...] = tokens_of(1)
    d3[...] = tokens_of(2)
    d0[...] = tokens_of(0)


def pass_kernel(at, d1, d3, r_a, r_b, s1, s3):
    s1[:HALF] = d1[:HALF] + r_a[...]
    s1[HALF:] = d1[HALF:]
    s3[:HALF] = d3[:HALF]
    s3[HALF:] = d3[HALF:] + r_b[...]


def deal_kernel(which, at, *refs):
    terms, outs, total = refs[:-5], refs[-5:-1], refs[-1]
    acc = terms[0][...]
    for term in terms[1:]:
        acc = acc + term[...]
    total[...] = acc.reshape(total.shape)
    for k, out in enumerate(outs):
        out[...] = total[lax.rem(at[which] + k, 4)]


def cut_kernel(at, a, b, c, d, p0, p1, p2, p3, rows_out):
    rows = a[...] + b[...] + c[...] + d[...]
    mine, of_out = rows[:, :HC], rows[:, WIDE:]
    rows_out[...] = of_out
    local = (jnp.sum(mine * mine) + jnp.sum(of_out * of_out)).reshape(1, 1)
    for k, out in enumerate((p0, p1, p2, p3)):
        to = lax.rem(at[0] + k, NX)
        part = mine[:6]
        for p in range(1, NX):
            part = jnp.where(to == p, mine[6 * p : 6 * p + 6], part)
        out[:6] = part
        out[6:8] = jnp.zeros((2, HC), F32)
        out[8:32, : 2 * NS] = rows[:, HC:WIDE]
        out[8:32, 2 * NS :] = jnp.zeros((24, HC - 2 * NS), F32)
        out[32:] = jnp.broadcast_to(local, (8, HC))


def square_kernel(at, a, b, c, d, square):
    refs = (a, b, c, d)
    bc = sum(r[8:32, : 2 * NS] for r in refs)
    total = sum(r[32:, :128] for r in refs)
    square[...] = total + jnp.sum(bc * bc).reshape(1, 1)


def last_kernel(at, a, b, c, d, rows_out, square, all_in, all_bc, all_out, parts):
    x = at[0]
    entries = DM * 1536 + DM * 256 + 1536 * DM
    factor = jnp.minimum(1.0, 1.0 / jnp.sqrt(square[:1, :1] / entries + 1e-06))
    for k, r in enumerate((a, b, c, d)):
        parts[k] = r[...]
    for p in range(NX):
        all_in[:, HC * p : HC * p + HC] = factor * parts[lax.rem(x - p + NX, NX), :6, :]
    rows = sum(r[8:32, : 2 * NS] for r in (a, b, c, d))
    mine = rows[:6]
    for p in range(1, NX):
        mine = jnp.where(x == p, rows[6 * p : 6 * p + 6], mine)
    all_bc[...] = factor * mine
    all_out[:, :HC] = factor * rows_out[:12]
    all_out[:, HC:] = factor * rows_out[12:]


def call(kernel, outs, scratch, args, flops=0):
    moved = sum(a.size * a.dtype.itemsize for a in args)
    return pl.pallas_call(
        kernel,
        out_shape=[jax.ShapeDtypeStruct(*o) for o in outs],
        in_specs=[SMEM] + vm(len(args) - 1),
        out_specs=vm(len(outs)),
        scratch_shapes=[pltpu.VMEM(*s) for s in scratch],
        compiler_params=PARAMS,
        cost_estimate=pl.CostEstimate(flops=flops, bytes_accessed=moved, transcendentals=0),
    )(*args)


def rows_exchange(s_p, s_m, s_2):
    r_2 = move(s_2, "y", 2)
    return [move(s_p, "y", 1), move(s_m, "y", -1), r_2]


def deal(at, which, terms, rows, cols):
    axis = {2: "y", 3: "z"}[which]
    p0, p1, p2, p3 = call(
        functools.partial(deal_kernel, which), [((rows, cols), F32)] * 4, [((4, rows, cols), F32)], [at, *terms]
    )
    r_2 = move(p2, axis, 2)
    return [p0, move(p1, axis, 1), r_2, move(p3, axis, 3)]


def body(tokens, cotangent, log_decay, w_in, w_bc, w_out):
    seq, rec = lax.axis_index("seq"), lax.axis_index("rec")
    x = seq % NX
    at = jnp.stack([x, rec % 2, seq // NX, rec // 2]).astype(jnp.int32)
    tie = lax.optimization_barrier

    (t0,) = pl.pallas_call(
        pack_kernel,
        out_shape=[jax.ShapeDtypeStruct((SEG + 8, DM), F32)],
        in_specs=vm(2),
        out_specs=vm(1),
        compiler_params=PARAMS,
    )(tokens[0], log_decay[0])
    c0 = cotangent[0].astype(F32)
    wi = lax.dynamic_slice(w_in, (0, x * HC), (DM, HC))
    wo = lax.dynamic_slice(w_out, (x * HC, 0), (HC, DM))
    t3, t1 = move(t0, "x", 1), move(t0, "x", -1)
    t3, c0 = tie((t3, c0))
    t2 = move(t3, "x", 1)
    c0_l, t1 = tie((c0, t1))
    c1 = move(c0_l, "x", -1)
    t1, wi, wo = tie((t1, wi, wo))

    tall = ((TALL, HC), F32)
    edges = ((2, NX, NS, HC), F32)

    def of_tokens(n):
        return [
            ((n, 8, SEG), F32), ((n, 8, SEG), F32), ((n, SEG, HC), F32), ((n, SEG, HC), F32),
            ((n, SEG, DM), BF16), ((n, SEG, HC), BF16), ((n, SEG, 2 * HC), BF16), ((n, SEG, 2 * NS), BF16),
        ]

    def ends(n):
        return ((n, NS, 2 * HC), F32)

    flops = 2 * SEG * (DM * (HC + 2 * NS) + NS * 2 * HC)
    row = ((8, SEG), F32)
    three = call(
        tok_kernel_a, [*of_tokens(3), ends(3)], [row], [at, tokens[0], log_decay[0], t1, t3, wi, w_bc], 3 * flops
    )
    def mats(n):
        return [((n, NH, SEG, SEG), BF16), ((n, NH, SEG, SEG), BF16), ((n, SEG, HC), F32)]

    within = 2 * SEG * SEG * 2 * HC
    mats_a = call(
        functools.partial(decay_kernel, 0, 3), mats(3), [], [at, *three[:4], three[5], three[7]], 3 * within
    )
    c0_r, t2, c1, *both = tie((c0, t2, c1, *three, *mats_a))
    three, mats_a = both[:9], both[9:]
    c3, c2 = move(c0_r, "x", 1), move(c1, "x", -1)
    cirow, cerow, ci, ce, tokb, xs, xfr, bc, pre_s, *s_rows = call(
        tok_kernel_b, [*of_tokens(4), edges, tall, tall, tall], [ends(4), row], [at, t2, wi, w_bc, *three], flops
    )
    q_rows = rows_exchange(*s_rows)
    two = [((2, SEG, DM), BF16), ((2, SEG, HC), BF16), ((2, SEG, 2 * HC), BF16)]
    flops = 1024 * (DM * HC + NS * 2 * HC)
    cotb_a, dy_a, dyfr_a, ends_a = call(
        cot_kernel_a, [*two, ends(2)], [ends(4)], [at, cotangent[0], c1, wo, ci, ce, bc], flops
    )
    mats_b = call(functools.partial(decay_kernel, 3, 1), mats(1), [], [at, cirow, cerow, ci, ce, xs, bc], within)
    c3, c2, ends_a, *mats_b = tie((c3, c2, ends_a, *mats_b))
    cotb_b, dy_b, dyfr_b, pre_d, *s_rows = call(
        cot_kernel_b, [*two, edges, tall, tall, tall], [ends(4)], [at, c3, c2, wo, ci, ce, bc, ends_a], flops
    )
    p_rows = rows_exchange(*s_rows)
    g_out, dxi, dci, dbi = call(
        inner_kernel,
        [((2, ROWS, HC), F32), ((NX, SEG, HC), F32), ((NX, SEG, NS), F32), ((NX, SEG, NS), F32)],
        [((NX, NS, 2 * HC), BF16), ((NX * SEG, HC), BF16)],
        [at, xs, bc, dy_a, dy_b, dyfr_a, dyfr_b, cotb_a, cotb_b, ci, ce, pre_s, *q_rows, *mats_a, *mats_b],
        2 * 1024 * (HC * DM + 5 * SEG * HC + 6 * NS * HC),
    )
    keep, send, dz = call(
        outer_kernel,
        [((ROWS, ALL), F32), ((ROWS, ALL), F32), ((NX, SEG, WIDE), BF16)],
        [((NX, NS, 2 * HC), BF16), ((2, ROWS, WIDE), F32)],
        [at, tokb, xfr, bc, ci, ce, pre_d, *p_rows, dxi, dci, dbi, g_out],
        2 * 1024 * (WIDE * DM + 4 * NS * HC),
    )
    got = move(send, "c", 1)
    terms = deal(at, 2, [keep, got], 96, ALL)
    whole, half = ((SEG, DM), F32), ((HALF, DM), F32)
    d0, d1, d2a, d2b, d3 = call(
        tokens_kernel, [whole, whole, half, half, whole], [], [at, dz, wi, w_bc], 2 * 1024 * WIDE * DM
    )
    r_a, r_b = move(d2a, "x", 1), move(d2b, "x", -1)
    s1, s3 = call(pass_kernel, [whole, whole], [], [at, d1, d3, r_a, r_b])
    m1, m3 = move(s1, "x", 1), move(s3, "x", -1)
    d_tok = (d0 + m1 + m3).astype(BF16)
    terms = deal(at, 3, terms, 24, ALL)
    p0, p1, p2, p3, rows_out = call(
        cut_kernel, [((40, HC), F32)] * 4 + [((24, HC), F32)], [], [at, *terms]
    )
    pieces = [p0, move(p1, "x", 1), move(p2, "x", 2), move(p3, "x", 3)]
    lanes = NX * NY
    pairs = [(r * lanes + i, 2 * NZ * NY * (i % NX) + r * NY + i // NX) for r in range(2 * NZ) for i in range(lanes)]
    rows_out = lax.ppermute(rows_out, ("rec", "seq"), pairs)
    (square,) = call(square_kernel, [((8, 128), F32)], [], [at, *pieces])
    for axis in ("y", "z"):
        square = square + (move(square, axis, 1) + move(square, axis, 3) + move(square, axis, 2))
    square = square + move(square, "c", 1)
    all_in, all_bc, all_out = call(
        last_kernel,
        [((6, NX * HC), F32), ((6, 2 * NS), F32), ((12, DM), F32)],
        [((NX, 40, HC), F32)],
        [at, *pieces, rows_out, square],
    )
    return d_tok[None], all_in, all_bc, all_out


def solution(mesh):
    in_specs = (P("rec", "seq", None), P("rec", "seq", None), P("rec", None, "seq"), P(), P(), P())
    out_specs = (
        P("rec", "seq", None),
        P(("rec", "seq"), None),
        P(("rec", "seq"), None),
        P(("rec", "seq"), None),
    )
    return jax.shard_map(body, mesh=mesh, in_specs=in_specs, out_specs=out_specs, check_vma=False)
```

```python
import functools

import jax
import jax.numpy as jnp
from jax import lax
from jax.experimental import pallas as pl
from jax.experimental.pallas import tpu as pltpu
from jax.sharding import PartitionSpec as P

F32 = jnp.float32
BF16 = jnp.bfloat16
NX = 4
NY = 4
NZ = 4
SEG = 256
HALF = SEG // 2
DM = 768
NS = 128
NH = 6
HD = 64
HC = NH * HD
ROWS = DM // 2
WIDE = HC + 2 * NS
ALL = WIDE + HC
TALL = NS + 8


def shift(axis, step, wrap=True):
    if axis == "c":
        return "rec", [(r, r ^ 1) for r in range(2 * NZ)]
    count, stride, total, name = {
        "x": (NX, 1, NX * NY, "seq"),
        "y": (NY, NX, NX * NY, "seq"),
        "z": (NZ, 2, 2 * NZ, "rec"),
    }[axis]
    pairs = []
    for i in range(total):
        at = (i // stride) % count
        to = at + step
        if not wrap and not 0 <= to < count:
            continue
        pairs.append((i, i + (to % count - at) * stride))
    return name, pairs


def move(value, axis, step, wrap=True):
    name, pairs = shift(axis, step, wrap)
    return lax.ppermute(value, name, pairs)


def dot(a, b, ca, cb):
    return lax.dot_general(a, b, (((ca,), (cb,)), ((), ())), preferred_element_type=F32)


def exact(a, b, ca, cb):
    return lax.dot_general(
        a, b, (((ca,), (cb,)), ((), ())), precision=lax.Precision.HIGHEST, preferred_element_type=F32
    )


def place(p, x):
    k = lax.rem(p - x + NX, NX)
    return k ^ (k >> 1)


def vm(n):
    return [pl.BlockSpec(memory_space=pltpu.VMEM)] * n


SMEM = pl.BlockSpec(memory_space=pltpu.SMEM)
PARAMS = pltpu.CompilerParams(vmem_limit_bytes=20 * 2**20)


def send_rows(up, down, log, y, s_p, s_m, s_2):
    s_p[:NS] = jnp.where(y == NY - 1, down, up)
    s_m[:NS] = jnp.where(y == 0, up, down)
    s_2[:NS] = jnp.where(y < 2, up, down)
    log = jnp.broadcast_to(log, (8, HC))
    for s in (s_p, s_m, s_2):
        s[NS:] = log


def from_rows(r_p, r_m, r_2, y):
    def on(yes):
        return jnp.where(yes, 1.0, 0.0).astype(F32)

    l_p, l_m, l_2 = (r[NS : NS + 1, :] for r in (r_p, r_m, r_2))
    v_p, v_m, v_2 = (r[:NS, :] for r in (r_p, r_m, r_2))
    up = v_p * on(y >= 1) + v_2 * (on(y >= 2) * jnp.exp(l_p)) + v_m * (on(y == 3) * jnp.exp(l_p + l_2))
    down = v_m * on(y <= 2) + v_2 * (on(y <= 1) * jnp.exp(l_m)) + v_p * (on(y == 0) * jnp.exp(l_m + l_2))
    return up, down


def row_scan(order, ends, cols, ci, x, pre, which):
    acc = jnp.zeros((NS, HC), F32)
    for p in order:
        k = place(p, x)
        pre[which, k] = acc
        acc = acc * jnp.exp(ci[k, SEG - 1 : SEG, :]) + ends[k, :, cols]
    return acc


def row_log(ci):
    return sum(ci[k, SEG - 1 : SEG, :] for k in range(NX))


FIRST, SECOND = slice(0, HC), slice(HC, 2 * HC)


def pack_kernel(tok, log, out):
    out[:SEG] = tok[...].astype(F32)
    for part in range(3):
        out[SEG:, SEG * part : SEG * part + SEG] = log[8 * part : 8 * part + 8]


def decays(x, toks, own, first, cirow, cerow, ci, ce, la):
    s = lax.broadcasted_iota(jnp.int32, (SEG, SEG), 0)
    t = lax.broadcasted_iota(jnp.int32, (SEG, SEG), 1)
    tri = jnp.where(s <= t, 1.0, 0.0).astype(F32)
    head = lax.broadcasted_iota(jnp.int32, (8, HC), 0) * HD
    lane = lax.broadcasted_iota(jnp.int32, (8, HC), 1)
    spread = jnp.where((lane >= head) & (lane < head + HD), 1.0, 0.0).astype(F32)
    la[...] = jnp.zeros((8, SEG), F32)
    for k, tok in enumerate(toks, first):
        for j in range(NH):
            mine = jnp.zeros((1, SEG), F32)
            for p in range(NX):
                h = NH * p + j
                if tok.shape[0] > SEG:
                    row, part = SEG + h % 8, h // 8
                    its = tok[row : row + 1, SEG * part : SEG * part + SEG]
                else:
                    its = own[h : h + 1]
                mine = jnp.where(x == p, its, mine)
            la[j : j + 1] = mine
        through = exact(la[...], tri, 1, 0)
        before = through - la[...]
        cirow[k] = through
        cerow[k] = before
        ci[k] = exact(through, spread, 0, 0)
        ce[k] = exact(before, spread, 0, 0)


def tok_part(at, toks, own, first, w_in, w_bc, cirow, cerow, ci, ce, tokb, xs, xfr, bc, ends, la):
    decays(at[0], toks, own, first, cirow, cerow, ci, ce, la)
    for k, t in enumerate(toks, first):
        tokb[k] = t[:SEG].astype(BF16)

    def segment(i, _):
        k = first + i
        t = tokb[k]
        xv = dot(t, w_in[...], 1, 0).astype(BF16)
        bv = dot(t, w_bc[...], 1, 0).astype(BF16)
        xs[k] = xv
        bc[k] = bv
        xf = xv.astype(F32)
        last = ci[k, SEG - 1 : SEG, :]
        xfr[k, :, :HC] = (xf * jnp.exp(last - ci[k])).astype(BF16)
        xfr[k, :, HC:] = (xf * jnp.exp(ce[k])).astype(BF16)
        ends[k] = dot(bv[:, :NS], xfr[k], 0, 0)
        return 0

    lax.fori_loop(0, len(toks), segment, 0)


def tok_kernel_a(at, t0, own, t1, t3, w_in, w_bc, *refs):
    tok_part(at, (t0, t1, t3), own, 0, w_in, w_bc, *refs)


def tok_kernel_b(at, t2, w_in, w_bc, *refs):
    given, full, (pre, s_p, s_m, s_2, ends, la) = refs[:9], refs[9:17], refs[17:]
    full = (*full, ends)
    for a, b in zip(given, full, strict=True):
        b[: NX - 1] = a[...]
    tok_part(at, (t2,), None, NX - 1, w_in, w_bc, *full, la)
    x, y, ci = at[0], at[2], full[2]
    up = row_scan(range(NX), ends, FIRST, ci, x, pre, 0)
    down = row_scan(reversed(range(NX)), ends, SECOND, ci, x, pre, 1)
    send_rows(up, down, row_log(ci), y, s_p, s_m, s_2)


def decay_kernel(first, count, at, cirow, cerow, ci, ce, xs, bc, mat, mat_t, y):
    def segment(i, _):
        k = first + i
        b, c = bc[k, :, :NS], bc[k, :, NS:]
        t = lax.broadcasted_iota(jnp.int32, (SEG, SEG), 0)
        s = lax.broadcasted_iota(jnp.int32, (SEG, SEG), 1)
        low, same = t > s, t == s
        scores = dot(c, b, 1, 1)
        lane = lax.broadcasted_iota(jnp.int32, (SEG, 2 * HD), 1)
        for pair in range(NH // 2):
            cols = slice(pair * 2 * HD, (pair + 1) * 2 * HD)
            xp = xs[k, :, cols]
            rows = jnp.zeros((SEG, 2 * HD), F32)
            for j in range(2):
                h = 2 * pair + j
                at_t = slice(h * HD, h * HD + 1)
                diff = jnp.where(
                    low,
                    ci[k, :, at_t] - cirow[k, h : h + 1, :],
                    cerow[k, h : h + 1, :] - ce[k, :, at_t],
                )
                decay = jnp.where(same, 2.0, jnp.exp(diff))
                mat[i, h] = decay.astype(BF16)
                w = (decay * scores).astype(BF16)
                mat_t[i, h] = w.T
                xm = jnp.where((lane < HD) if j == 0 else (lane >= HD), xp, jnp.zeros_like(xp))
                rows = rows + dot(w, xm, 1, 0)
            y[i, :, cols] = rows
        return 0

    lax.fori_loop(0, count, segment, 0)


def cot_part(cots, first, w_out, ci, ce, bc, cotb, dy, dyfr, ends):
    for i, t in enumerate(cots):
        cotb[i] = t[...].astype(BF16)

    def segment(i, _):
        k = first + i
        d = dot(cotb[i], w_out[...], 1, 1)
        dy[i] = d.astype(BF16)
        last = ci[k, SEG - 1 : SEG, :]
        dyfr[i, :, :HC] = (d * jnp.exp(ci[k])).astype(BF16)
        dyfr[i, :, HC:] = (d * jnp.exp(last - ce[k])).astype(BF16)
        ends[k] = dot(bc[k, :, NS:], dyfr[i], 0, 0)
        return 0

    lax.fori_loop(0, len(cots), segment, 0)


def cot_kernel_a(at, c0, c1, w_out, ci, ce, bc, cotb, dy, dyfr, ends_a, ends):
    cot_part((c0, c1), 0, w_out, ci, ce, bc, cotb, dy, dyfr, ends)
    ends_a[...] = ends[:2]


def cot_kernel_b(
    at, c2, c3, w_out, ci, ce, bc, ends_a, cotb, dy, dyfr, pre, s_p, s_m, s_2, ends
):
    x, y = at[0], at[2]
    ends[:2] = ends_a[...]
    cot_part((c2, c3), 2, w_out, ci, ce, bc, cotb, dy, dyfr, ends)
    down = row_scan(reversed(range(NX)), ends, FIRST, ci, x, pre, 0)
    up = row_scan(range(NX), ends, SECOND, ci, x, pre, 1)
    send_rows(up, down, row_log(ci), y, s_p, s_m, s_2)


def enter(pre, which, q, ci, x, order, out, cols):
    log = jnp.zeros((1, HC), F32)
    for p in order:
        k = place(p, x)
        out[k, :, cols] = (pre[which, k] + q * jnp.exp(log)).astype(BF16)
        log = log + ci[k, SEG - 1 : SEG, :]


def blocks():
    return [(j, j // 4 % 2, (4 * (j % 4) + j // 8) * 24) for j in range(2 * NZ * NY)]


def inner_kernel(
    at, xs, bc, dy_a, dy_b, dyfr_a, dyfr_b, cotb_a, cotb_b, ci, ce, pre, r_p, r_m, r_2,
    mat_a, mat_t_a, y_a, mat_b, mat_t_b, y_b,
    g, dxi, dci, dbi, sr, yb,
):
    x, y_at = at[0], at[2]
    up, down = from_rows(r_p, r_m, r_2, y_at)
    enter(pre, 0, up, ci, x, range(NX), sr, pl.ds(0, HC))
    enter(pre, 1, down, ci, x, reversed(range(NX)), sr, pl.ds(HC, HC))

    def run(first, count, mat, mat_t, y_in, m0, dy, dyfr, d0):
        def segment(n, _):
            k, m, i = first + n, m0 + n, d0 + n
            b, c = bc[k, :, :NS], bc[k, :, NS:]
            lane = lax.broadcasted_iota(jnp.int32, (SEG, 2 * HD), 1)
            carry = dot(c, sr[k], 1, 0)
            total = jnp.zeros((SEG, SEG), F32)
            for pair in range(NH // 2):
                cols = slice(pair * 2 * HD, (pair + 1) * 2 * HD)
                xp, dp = xs[k, :, cols], dy[i, :, cols]
                dx = jnp.zeros((SEG, 2 * HD), F32)
                for j in range(2):
                    h = 2 * pair + j
                    dm = jnp.where((lane < HD) if j == 0 else (lane >= HD), dp, jnp.zeros_like(dp))
                    total = total + mat[m, h].astype(F32) * dot(dm, xp, 1, 1)
                    dx = dx + dot(mat_t[m, h], dm, 1, 0)
                last = ci[k, SEG - 1 : SEG, cols]
                y = y_in[m, :, cols] + carry[:, cols] * jnp.exp(ci[k, :, cols])
                y = y + carry[:, slice(HC + cols.start, HC + cols.stop)] * jnp.exp(last - ce[k, :, cols])
                yb[pl.ds(k * SEG, SEG), cols] = y.astype(BF16)
                dxi[k, :, cols] = dx
            total = total.astype(BF16)
            dci[k] = dot(total, b, 1, 0) + dot(dyfr[i], sr[k], 1, 1)
            dbi[k] = dot(total, c, 0, 0)
            return 0

        lax.fori_loop(0, count, segment, 0)

    run(0, 2, mat_a, mat_t_a, y_a, 0, dy_a, dyfr_a, 0)
    run(2, 1, mat_a, mat_t_a, y_a, 2, dy_b, dyfr_b, 0)
    run(3, 1, mat_b, mat_t_b, y_b, 0, dy_b, dyfr_b, 1)
    half = 2 * SEG
    raw = dot(yb[:half, :], cotb_a[...].reshape(half, DM), 0, 0)
    raw = raw + dot(yb[half:, :], cotb_b[...].reshape(half, DM), 0, 0)
    for j, c, row in blocks():
        g[c, row : row + 12, :] = raw[12 * j : 12 * j + 12, :HC]
        g[c, row + 12 : row + 24, :] = raw[12 * j : 12 * j + 12, HC:]


def outer_kernel(
    at, tokb, xfr, bc, ci, ce, pre, r_p, r_m, r_2, dxi, dci, dbi, g_out, keep, send, dz, ds, g
):
    x, core, y_at = at[0], at[1], at[2]
    up, down = from_rows(r_p, r_m, r_2, y_at)
    enter(pre, 0, down, ci, x, reversed(range(NX)), ds, pl.ds(0, HC))
    enter(pre, 1, up, ci, x, range(NX), ds, pl.ds(HC, HC))

    def segment(k, _):
        b = bc[k, :, :NS]
        last = ci[k, SEG - 1 : SEG, :]
        back = dot(b, ds[k], 1, 0)
        dx = dxi[k] + back[:, :HC] * jnp.exp(last - ci[k]) + back[:, HC:] * jnp.exp(ce[k])
        dz[k, :, :HC] = dx.astype(BF16)
        dz[k, :, HC : HC + NS] = (dbi[k] + dot(xfr[k], ds[k], 1, 1)).astype(BF16)
        dz[k, :, HC + NS :] = dci[k].astype(BF16)
        return 0

    lax.fori_loop(0, NX, segment, 0)
    raw = dot(tokb[...].reshape(NX * SEG, DM), dz[...].reshape(NX * SEG, WIDE), 0, 0)
    for j, c, row in blocks():
        g[c, row : row + 24, :] = raw[24 * j : 24 * j + 24, :]
    for out, c in ((keep, core), (send, 1 - core)):
        out[:, :WIDE] = g[c]
        out[:, WIDE:] = g_out[c]


def tokens_kernel(at, dz, w_in, w_bc, d0, d1, d2a, d2b, d3):
    def tokens_of(k):
        return dot(dz[k, :, :HC], w_in[...], 1, 1) + dot(dz[k, :, HC:], w_bc[...], 1, 1)

    d = tokens_of(3)
    d2a[...] = d[:HALF]
    d2b[...] = d[HALF:]
    d1[...] = tokens_of(1)
    d3[...] = tokens_of(2)
    d0[...] = tokens_of(0)


def pass_kernel(at, d1, d3, r_a, r_b, s1, s3):
    s1[:HALF] = d1[:HALF] + r_a[...]
    s1[HALF:] = d1[HALF:]
    s3[:HALF] = d3[:HALF]
    s3[HALF:] = d3[HALF:] + r_b[...]


def deal_kernel(which, at, *refs):
    terms, outs, total = refs[:-5], refs[-5:-1], refs[-1]
    acc = terms[0][...]
    for term in terms[1:]:
        acc = acc + term[...]
    total[...] = acc.reshape(total.shape)
    for k, out in enumerate(outs):
        out[...] = total[lax.rem(at[which] + k, 4)]


def cut_kernel(at, a, b, c, d, p0, p1, p2, p3, rows_out):
    rows = a[...] + b[...] + c[...] + d[...]
    mine, of_out = rows[:, :HC], rows[:, WIDE:]
    rows_out[...] = of_out
    local = (jnp.sum(mine * mine) + jnp.sum(of_out * of_out)).reshape(1, 1)
    for k, out in enumerate((p0, p1, p2, p3)):
        to = lax.rem(at[0] + k, NX)
        part = mine[:6]
        for p in range(1, NX):
            part = jnp.where(to == p, mine[6 * p : 6 * p + 6], part)
        out[:6] = part
        out[6:8] = jnp.zeros((2, HC), F32)
        out[8:32, : 2 * NS] = rows[:, HC:WIDE]
        out[8:32, 2 * NS :] = jnp.zeros((24, HC - 2 * NS), F32)
        out[32:] = jnp.broadcast_to(local, (8, HC))


def square_kernel(at, a, b, c, d, square):
    refs = (a, b, c, d)
    bc = sum(r[8:32, : 2 * NS] for r in refs)
    total = sum(r[32:, :128] for r in refs)
    square[...] = total + jnp.sum(bc * bc).reshape(1, 1)


def last_kernel(at, a, b, c, d, rows_out, square, all_in, all_bc, all_out, parts):
    x = at[0]
    entries = DM * 1536 + DM * 256 + 1536 * DM
    factor = jnp.minimum(1.0, 1.0 / jnp.sqrt(square[:1, :1] / entries + 1e-06))
    for k, r in enumerate((a, b, c, d)):
        parts[k] = r[...]
    for p in range(NX):
        all_in[:, HC * p : HC * p + HC] = factor * parts[lax.rem(x - p + NX, NX), :6, :]
    rows = sum(r[8:32, : 2 * NS] for r in (a, b, c, d))
    mine = rows[:6]
    for p in range(1, NX):
        mine = jnp.where(x == p, rows[6 * p : 6 * p + 6], mine)
    all_bc[...] = factor * mine
    all_out[:, :HC] = factor * rows_out[:12]
    all_out[:, HC:] = factor * rows_out[12:]


def call(kernel, outs, scratch, args, flops=0):
    moved = sum(a.size * a.dtype.itemsize for a in args)
    return pl.pallas_call(
        kernel,
        out_shape=[jax.ShapeDtypeStruct(*o) for o in outs],
        in_specs=[SMEM] + vm(len(args) - 1),
        out_specs=vm(len(outs)),
        scratch_shapes=[pltpu.VMEM(*s) for s in scratch],
        compiler_params=PARAMS,
        cost_estimate=pl.CostEstimate(flops=flops, bytes_accessed=moved, transcendentals=0),
    )(*args)


def rows_exchange(s_p, s_m, s_2):
    r_2 = move(s_2, "y", 2)
    return [move(s_p, "y", 1), move(s_m, "y", -1), r_2]


def deal(at, which, terms, rows, cols):
    axis = {2: "y", 3: "z"}[which]
    p0, p1, p2, p3 = call(
        functools.partial(deal_kernel, which), [((rows, cols), F32)] * 4, [((4, rows, cols), F32)], [at, *terms]
    )
    r_2 = move(p2, axis, 2)
    return [p0, move(p1, axis, 1), r_2, move(p3, axis, 3)]


def body(tokens, cotangent, log_decay, w_in, w_bc, w_out):
    seq, rec = lax.axis_index("seq"), lax.axis_index("rec")
    x = seq % NX
    at = jnp.stack([x, rec % 2, seq // NX, rec // 2]).astype(jnp.int32)
    tie = lax.optimization_barrier

    (t0,) = pl.pallas_call(
        pack_kernel,
        out_shape=[jax.ShapeDtypeStruct((SEG + 8, DM), F32)],
        in_specs=vm(2),
        out_specs=vm(1),
        compiler_params=PARAMS,
    )(tokens[0], log_decay[0])
    c0 = cotangent[0].astype(F32)
    wi = lax.dynamic_slice(w_in, (0, x * HC), (DM, HC))
    wo = lax.dynamic_slice(w_out, (x * HC, 0), (HC, DM))
    t3, t1 = move(t0, "x", 1), move(t0, "x", -1)
    t3, c0 = tie((t3, c0))
    t2 = move(t3, "x", 1)
    c0, t1 = tie((c0, t1))
    c1, c3 = move(c0, "x", -1), move(c0, "x", 1)
    t1, wi, wo = tie((t1, wi, wo))

    tall = ((TALL, HC), F32)
    edges = ((2, NX, NS, HC), F32)

    def of_tokens(n):
        return [
            ((n, 8, SEG), F32), ((n, 8, SEG), F32), ((n, SEG, HC), F32), ((n, SEG, HC), F32),
            ((n, SEG, DM), BF16), ((n, SEG, HC), BF16), ((n, SEG, 2 * HC), BF16), ((n, SEG, 2 * NS), BF16),
        ]

    def ends(n):
        return ((n, NS, 2 * HC), F32)

    flops = 2 * SEG * (DM * (HC + 2 * NS) + NS * 2 * HC)
    row = ((8, SEG), F32)
    three = call(
        tok_kernel_a, [*of_tokens(3), ends(3)], [row], [at, tokens[0], log_decay[0], t1, t3, wi, w_bc], 3 * flops
    )
    def mats(n):
        return [((n, NH, SEG, SEG), BF16), ((n, NH, SEG, SEG), BF16), ((n, SEG, HC), F32)]

    within = 2 * SEG * SEG * 2 * HC
    mats_a = call(
        functools.partial(decay_kernel, 0, 3), mats(3), [], [at, *three[:4], three[5], three[7]], 3 * within
    )
    t2, c1, *both = tie((t2, c1, *three, *mats_a))
    three, mats_a = both[:9], both[9:]
    c2 = move(c1, "x", -1)
    cirow, cerow, ci, ce, tokb, xs, xfr, bc, pre_s, *s_rows = call(
        tok_kernel_b, [*of_tokens(4), edges, tall, tall, tall], [ends(4), row], [at, t2, wi, w_bc, *three], flops
    )
    q_rows = rows_exchange(*s_rows)
    two = [((2, SEG, DM), BF16), ((2, SEG, HC), BF16), ((2, SEG, 2 * HC), BF16)]
    flops = 1024 * (DM * HC + NS * 2 * HC)
    cotb_a, dy_a, dyfr_a, ends_a = call(
        cot_kernel_a, [*two, ends(2)], [ends(4)], [at, cotangent[0], c1, wo, ci, ce, bc], flops
    )
    mats_b = call(functools.partial(decay_kernel, 3, 1), mats(1), [], [at, cirow, cerow, ci, ce, xs, bc], within)
    c3, c2, ends_a, *mats_b = tie((c3, c2, ends_a, *mats_b))
    cotb_b, dy_b, dyfr_b, pre_d, *s_rows = call(
        cot_kernel_b, [*two, edges, tall, tall, tall], [ends(4)], [at, c3, c2, wo, ci, ce, bc, ends_a], flops
    )
    p_rows = rows_exchange(*s_rows)
    g_out, dxi, dci, dbi = call(
        inner_kernel,
        [((2, ROWS, HC), F32), ((NX, SEG, HC), F32), ((NX, SEG, NS), F32), ((NX, SEG, NS), F32)],
        [((NX, NS, 2 * HC), BF16), ((NX * SEG, HC), BF16)],
        [at, xs, bc, dy_a, dy_b, dyfr_a, dyfr_b, cotb_a, cotb_b, ci, ce, pre_s, *q_rows, *mats_a, *mats_b],
        2 * 1024 * (HC * DM + 5 * SEG * HC + 6 * NS * HC),
    )
    keep, send, dz = call(
        outer_kernel,
        [((ROWS, ALL), F32), ((ROWS, ALL), F32), ((NX, SEG, WIDE), BF16)],
        [((NX, NS, 2 * HC), BF16), ((2, ROWS, WIDE), F32)],
        [at, tokb, xfr, bc, ci, ce, pre_d, *p_rows, dxi, dci, dbi, g_out],
        2 * 1024 * (WIDE * DM + 4 * NS * HC),
    )
    got = move(send, "c", 1)
    terms = deal(at, 2, [keep, got], 96, ALL)
    whole, half = ((SEG, DM), F32), ((HALF, DM), F32)
    d0, d1, d2a, d2b, d3 = call(
        tokens_kernel, [whole, whole, half, half, whole], [], [at, dz, wi, w_bc], 2 * 1024 * WIDE * DM
    )
    r_a, r_b = move(d2a, "x", 1), move(d2b, "x", -1)
    s1, s3 = call(pass_kernel, [whole, whole], [], [at, d1, d3, r_a, r_b])
    m1, m3 = move(s1, "x", 1), move(s3, "x", -1)
    d_tok = (d0 + m1 + m3).astype(BF16)
    terms = deal(at, 3, terms, 24, ALL)
    p0, p1, p2, p3, rows_out = call(
        cut_kernel, [((40, HC), F32)] * 4 + [((24, HC), F32)], [], [at, *terms]
    )
    pieces = [p0, move(p1, "x", 1), move(p2, "x", 2), move(p3, "x", 3)]
    lanes = NX * NY
    pairs = [(r * lanes + i, 2 * NZ * NY * (i % NX) + r * NY + i // NX) for r in range(2 * NZ) for i in range(lanes)]
    rows_out = lax.ppermute(rows_out, ("rec", "seq"), pairs)
    (square,) = call(square_kernel, [((8, 128), F32)], [], [at, *pieces])
    for axis in ("y", "z"):
        square = square + (move(square, axis, 1) + move(square, axis, 3) + move(square, axis, 2))
    square = square + move(square, "c", 1)
    all_in, all_bc, all_out = call(
        last_kernel,
        [((6, NX * HC), F32), ((6, 2 * NS), F32), ((12, DM), F32)],
        [((NX, 40, HC), F32)],
        [at, *pieces, rows_out, square],
    )
    return d_tok[None], all_in, all_bc, all_out


def solution(mesh):
    in_specs = (P("rec", "seq", None), P("rec", "seq", None), P("rec", None, "seq"), P(), P(), P())
    out_specs = (
        P("rec", "seq", None),
        P(("rec", "seq"), None),
        P(("rec", "seq"), None),
        P(("rec", "seq"), None),
    )
    return jax.shard_map(body, mesh=mesh, in_specs=in_specs, out_specs=out_specs, check_vma=False)
```

```python
import functools

import jax
import jax.numpy as jnp
from jax import lax
from jax.experimental import pallas as pl
from jax.experimental.pallas import tpu as pltpu
from jax.sharding import PartitionSpec as P

F32 = jnp.float32
BF16 = jnp.bfloat16
NX = 4
NY = 4
NZ = 4
SEG = 256
DM = 768
NS = 128
NH = 6
HD = 64
HC = NH * HD
ROWS = DM // 2
WIDE = HC + 2 * NS
ALL = WIDE + HC
TALL = NS + 8


def shift(axis, step, wrap=True):
    if axis == "c":
        return "rec", [(r, r ^ 1) for r in range(2 * NZ)]
    count, stride, total, name = {
        "x": (NX, 1, NX * NY, "seq"),
        "y": (NY, NX, NX * NY, "seq"),
        "z": (NZ, 2, 2 * NZ, "rec"),
    }[axis]
    pairs = []
    for i in range(total):
        at = (i // stride) % count
        to = at + step
        if not wrap and not 0 <= to < count:
            continue
        pairs.append((i, i + (to % count - at) * stride))
    return name, pairs


def move(value, axis, step, wrap=True):
    name, pairs = shift(axis, step, wrap)
    return lax.ppermute(value, name, pairs)


def dot(a, b, ca, cb):
    return lax.dot_general(a, b, (((ca,), (cb,)), ((), ())), preferred_element_type=F32)


def exact(a, b, ca, cb):
    return lax.dot_general(
        a, b, (((ca,), (cb,)), ((), ())), precision=lax.Precision.HIGHEST, preferred_element_type=F32
    )


def place(p, x):
    k = lax.rem(p - x + NX, NX)
    return k ^ (k >> 1)


def vm(n):
    return [pl.BlockSpec(memory_space=pltpu.VMEM)] * n


SMEM = pl.BlockSpec(memory_space=pltpu.SMEM)
PARAMS = pltpu.CompilerParams(vmem_limit_bytes=20 * 2**20)


def send_rows(up, down, log, y, s_p, s_m, s_2):
    s_p[:NS] = jnp.where(y == NY - 1, down, up)
    s_m[:NS] = jnp.where(y == 0, up, down)
    s_2[:NS] = jnp.where(y < 2, up, down)
    log = jnp.broadcast_to(log, (8, HC))
    for s in (s_p, s_m, s_2):
        s[NS:] = log


def from_rows(r_p, r_m, r_2, y):
    def on(yes):
        return jnp.where(yes, 1.0, 0.0).astype(F32)

    l_p, l_m, l_2 = (r[NS : NS + 1, :] for r in (r_p, r_m, r_2))
    v_p, v_m, v_2 = (r[:NS, :] for r in (r_p, r_m, r_2))
    up = v_p * on(y >= 1) + v_2 * (on(y >= 2) * jnp.exp(l_p)) + v_m * (on(y == 3) * jnp.exp(l_p + l_2))
    down = v_m * on(y <= 2) + v_2 * (on(y <= 1) * jnp.exp(l_m)) + v_p * (on(y == 0) * jnp.exp(l_m + l_2))
    return up, down


def row_scan(order, ends, cols, ci, x, pre, which):
    acc = jnp.zeros((NS, HC), F32)
    for p in order:
        k = place(p, x)
        pre[which, k] = acc
        acc = acc * jnp.exp(ci[k, SEG - 1 : SEG, :]) + ends[k, :, cols]
    return acc


def row_log(ci):
    return sum(ci[k, SEG - 1 : SEG, :] for k in range(NX))


FIRST, SECOND = slice(0, HC), slice(HC, 2 * HC)


def pack_kernel(tok, log, out):
    out[:SEG] = tok[...].astype(F32)
    for part in range(3):
        out[SEG:, SEG * part : SEG * part + SEG] = log[8 * part : 8 * part + 8]


def decays(x, toks, own, first, cirow, cerow, ci, ce, la):
    s = lax.broadcasted_iota(jnp.int32, (SEG, SEG), 0)
    t = lax.broadcasted_iota(jnp.int32, (SEG, SEG), 1)
    tri = jnp.where(s <= t, 1.0, 0.0).astype(F32)
    head = lax.broadcasted_iota(jnp.int32, (8, HC), 0) * HD
    lane = lax.broadcasted_iota(jnp.int32, (8, HC), 1)
    spread = jnp.where((lane >= head) & (lane < head + HD), 1.0, 0.0).astype(F32)
    la[...] = jnp.zeros((8, SEG), F32)
    for k, tok in enumerate(toks, first):
        for j in range(NH):
            mine = jnp.zeros((1, SEG), F32)
            for p in range(NX):
                h = NH * p + j
                if tok.shape[0] > SEG:
                    row, part = SEG + h % 8, h // 8
                    its = tok[row : row + 1, SEG * part : SEG * part + SEG]
                else:
                    its = own[h : h + 1]
                mine = jnp.where(x == p, its, mine)
            la[j : j + 1] = mine
        through = exact(la[...], tri, 1, 0)
        before = through - la[...]
        cirow[k] = through
        cerow[k] = before
        ci[k] = exact(through, spread, 0, 0)
        ce[k] = exact(before, spread, 0, 0)


def tok_part(at, toks, own, first, w_in, w_bc, cirow, cerow, ci, ce, tokb, xs, xfr, bc, ends, la):
    decays(at[0], toks, own, first, cirow, cerow, ci, ce, la)
    for k, t in enumerate(toks, first):
        tokb[k] = t[:SEG].astype(BF16)

    def segment(i, _):
        k = first + i
        t = tokb[k]
        xv = dot(t, w_in[...], 1, 0).astype(BF16)
        bv = dot(t, w_bc[...], 1, 0).astype(BF16)
        xs[k] = xv
        bc[k] = bv
        xf = xv.astype(F32)
        last = ci[k, SEG - 1 : SEG, :]
        xfr[k, :, :HC] = (xf * jnp.exp(last - ci[k])).astype(BF16)
        xfr[k, :, HC:] = (xf * jnp.exp(ce[k])).astype(BF16)
        ends[k] = dot(bv[:, :NS], xfr[k], 0, 0)
        return 0

    lax.fori_loop(0, len(toks), segment, 0)


def tok_kernel_a(at, t0, own, t1, t3, w_in, w_bc, *refs):
    tok_part(at, (t0, t1, t3), own, 0, w_in, w_bc, *refs)


def tok_kernel_b(at, t2, w_in, w_bc, *refs):
    given, full, (pre, s_p, s_m, s_2, ends, la) = refs[:9], refs[9:17], refs[17:]
    full = (*full, ends)
    for a, b in zip(given, full, strict=True):
        b[: NX - 1] = a[...]
    tok_part(at, (t2,), None, NX - 1, w_in, w_bc, *full, la)
    x, y, ci = at[0], at[2], full[2]
    up = row_scan(range(NX), ends, FIRST, ci, x, pre, 0)
    down = row_scan(reversed(range(NX)), ends, SECOND, ci, x, pre, 1)
    send_rows(up, down, row_log(ci), y, s_p, s_m, s_2)


def decay_kernel(first, count, at, cirow, cerow, ci, ce, xs, bc, mat, mat_t, y):
    def segment(i, _):
        k = first + i
        b, c = bc[k, :, :NS], bc[k, :, NS:]
        t = lax.broadcasted_iota(jnp.int32, (SEG, SEG), 0)
        s = lax.broadcasted_iota(jnp.int32, (SEG, SEG), 1)
        low, same = t > s, t == s
        scores = dot(c, b, 1, 1)
        lane = lax.broadcasted_iota(jnp.int32, (SEG, 2 * HD), 1)
        for pair in range(NH // 2):
            cols = slice(pair * 2 * HD, (pair + 1) * 2 * HD)
            xp = xs[k, :, cols]
            rows = jnp.zeros((SEG, 2 * HD), F32)
            for j in range(2):
                h = 2 * pair + j
                at_t = slice(h * HD, h * HD + 1)
                diff = jnp.where(
                    low,
                    ci[k, :, at_t] - cirow[k, h : h + 1, :],
                    cerow[k, h : h + 1, :] - ce[k, :, at_t],
                )
                decay = jnp.where(same, 2.0, jnp.exp(diff))
                mat[i, h] = decay.astype(BF16)
                w = (decay * scores).astype(BF16)
                mat_t[i, h] = w.T
                xm = jnp.where((lane < HD) if j == 0 else (lane >= HD), xp, jnp.zeros_like(xp))
                rows = rows + dot(w, xm, 1, 0)
            y[i, :, cols] = rows
        return 0

    lax.fori_loop(0, count, segment, 0)


def cot_part(cots, first, w_out, ci, ce, bc, cotb, dy, dyfr, ends):
    for i, t in enumerate(cots):
        cotb[i] = t[...].astype(BF16)

    def segment(i, _):
        k = first + i
        d = dot(cotb[i], w_out[...], 1, 1)
        dy[i] = d.astype(BF16)
        last = ci[k, SEG - 1 : SEG, :]
        dyfr[i, :, :HC] = (d * jnp.exp(ci[k])).astype(BF16)
        dyfr[i, :, HC:] = (d * jnp.exp(last - ce[k])).astype(BF16)
        ends[k] = dot(bc[k, :, NS:], dyfr[i], 0, 0)
        return 0

    lax.fori_loop(0, len(cots), segment, 0)


def cot_kernel_a(at, c0, c1, w_out, ci, ce, bc, cotb, dy, dyfr, ends_a, ends):
    cot_part((c0, c1), 0, w_out, ci, ce, bc, cotb, dy, dyfr, ends)
    ends_a[...] = ends[:2]


def cot_kernel_b(
    at, c2, c3, w_out, ci, ce, bc, ends_a, cotb, dy, dyfr, pre, s_p, s_m, s_2, ends
):
    x, y = at[0], at[2]
    ends[:2] = ends_a[...]
    cot_part((c2, c3), 2, w_out, ci, ce, bc, cotb, dy, dyfr, ends)
    down = row_scan(reversed(range(NX)), ends, FIRST, ci, x, pre, 0)
    up = row_scan(range(NX), ends, SECOND, ci, x, pre, 1)
    send_rows(up, down, row_log(ci), y, s_p, s_m, s_2)


def enter(pre, which, q, ci, x, order, out, cols):
    log = jnp.zeros((1, HC), F32)
    for p in order:
        k = place(p, x)
        out[k, :, cols] = (pre[which, k] + q * jnp.exp(log)).astype(BF16)
        log = log + ci[k, SEG - 1 : SEG, :]


def blocks():
    return [(j, j // 4 % 2, (4 * (j % 4) + j // 8) * 24) for j in range(2 * NZ * NY)]


def inner_kernel(
    at, xs, bc, dy_a, dy_b, dyfr_a, dyfr_b, cotb_a, cotb_b, ci, ce, pre, r_p, r_m, r_2,
    mat_a, mat_t_a, y_a, mat_b, mat_t_b, y_b,
    g, dxi, dci, dbi, sr, yb,
):
    x, y_at = at[0], at[2]
    up, down = from_rows(r_p, r_m, r_2, y_at)
    enter(pre, 0, up, ci, x, range(NX), sr, pl.ds(0, HC))
    enter(pre, 1, down, ci, x, reversed(range(NX)), sr, pl.ds(HC, HC))

    def run(first, count, mat, mat_t, y_in, m0, dy, dyfr, d0):
        def segment(n, _):
            k, m, i = first + n, m0 + n, d0 + n
            b, c = bc[k, :, :NS], bc[k, :, NS:]
            lane = lax.broadcasted_iota(jnp.int32, (SEG, 2 * HD), 1)
            carry = dot(c, sr[k], 1, 0)
            total = jnp.zeros((SEG, SEG), F32)
            for pair in range(NH // 2):
                cols = slice(pair * 2 * HD, (pair + 1) * 2 * HD)
                xp, dp = xs[k, :, cols], dy[i, :, cols]
                dx = jnp.zeros((SEG, 2 * HD), F32)
                for j in range(2):
                    h = 2 * pair + j
                    dm = jnp.where((lane < HD) if j == 0 else (lane >= HD), dp, jnp.zeros_like(dp))
                    total = total + mat[m, h].astype(F32) * dot(dm, xp, 1, 1)
                    dx = dx + dot(mat_t[m, h], dm, 1, 0)
                last = ci[k, SEG - 1 : SEG, cols]
                y = y_in[m, :, cols] + carry[:, cols] * jnp.exp(ci[k, :, cols])
                y = y + carry[:, slice(HC + cols.start, HC + cols.stop)] * jnp.exp(last - ce[k, :, cols])
                yb[pl.ds(k * SEG, SEG), cols] = y.astype(BF16)
                dxi[k, :, cols] = dx
            total = total.astype(BF16)
            dci[k] = dot(total, b, 1, 0) + dot(dyfr[i], sr[k], 1, 1)
            dbi[k] = dot(total, c, 0, 0)
            return 0

        lax.fori_loop(0, count, segment, 0)

    run(0, 2, mat_a, mat_t_a, y_a, 0, dy_a, dyfr_a, 0)
    run(2, 1, mat_a, mat_t_a, y_a, 2, dy_b, dyfr_b, 0)
    run(3, 1, mat_b, mat_t_b, y_b, 0, dy_b, dyfr_b, 1)
    half = 2 * SEG
    raw = dot(yb[:half, :], cotb_a[...].reshape(half, DM), 0, 0)
    raw = raw + dot(yb[half:, :], cotb_b[...].reshape(half, DM), 0, 0)
    for j, c, row in blocks():
        g[c, row : row + 12, :] = raw[12 * j : 12 * j + 12, :HC]
        g[c, row + 12 : row + 24, :] = raw[12 * j : 12 * j + 12, HC:]


def outer_kernel(
    at, tokb, xfr, bc, ci, ce, pre, r_p, r_m, r_2, dxi, dci, dbi, g_out, keep, send, dz, ds, g
):
    x, core, y_at = at[0], at[1], at[2]
    up, down = from_rows(r_p, r_m, r_2, y_at)
    enter(pre, 0, down, ci, x, reversed(range(NX)), ds, pl.ds(0, HC))
    enter(pre, 1, up, ci, x, range(NX), ds, pl.ds(HC, HC))

    def segment(k, _):
        b = bc[k, :, :NS]
        last = ci[k, SEG - 1 : SEG, :]
        back = dot(b, ds[k], 1, 0)
        dx = dxi[k] + back[:, :HC] * jnp.exp(last - ci[k]) + back[:, HC:] * jnp.exp(ce[k])
        dz[k, :, :HC] = dx.astype(BF16)
        dz[k, :, HC : HC + NS] = (dbi[k] + dot(xfr[k], ds[k], 1, 1)).astype(BF16)
        dz[k, :, HC + NS :] = dci[k].astype(BF16)
        return 0

    lax.fori_loop(0, NX, segment, 0)
    g[...] = dot(tokb[...].reshape(NX * SEG, DM), dz[...].reshape(NX * SEG, WIDE), 0, 0)
    for out, c in ((keep, core), (send, 1 - core)):
        for z in range(NZ):
            for y in range(NY):
                first = pl.multiple_of(24 * (8 * z + y) + 96 * c, 8)
                row = (4 * y + z) * 24
                out[row : row + 24, :WIDE] = g[pl.ds(first, 24), :]
        out[:, WIDE:] = g_out[c]


def tokens_kernel(at, dz, w_in, w_bc, d0, d1, d2, d3):
    def tokens_of(k):
        return dot(dz[k, :, :HC], w_in[...], 1, 1) + dot(dz[k, :, HC:], w_bc[...], 1, 1)

    d2[...] = tokens_of(3)
    d1[...] = tokens_of(1)
    d3[...] = tokens_of(2)
    d0[...] = tokens_of(0)


def pass_kernel(at, a, b, out):
    out[...] = a[...] + b[...]


def deal_kernel(which, at, *refs):
    terms, outs, total = refs[:-5], refs[-5:-1], refs[-1]
    acc = terms[0][...]
    for term in terms[1:]:
        acc = acc + term[...]
    total[...] = acc.reshape(total.shape)
    for k, out in enumerate(outs):
        out[...] = total[lax.rem(at[which] + k, 4)]


def cut_kernel(at, a, b, c, d, p0, p1, p2, p3, rows_out):
    rows = a[...] + b[...] + c[...] + d[...]
    mine, of_out = rows[:, :HC], rows[:, WIDE:]
    rows_out[...] = of_out
    local = (jnp.sum(mine * mine) + jnp.sum(of_out * of_out)).reshape(1, 1)
    for k, out in enumerate((p0, p1, p2, p3)):
        to = lax.rem(at[0] + k, NX)
        part = mine[:6]
        for p in range(1, NX):
            part = jnp.where(to == p, mine[6 * p : 6 * p + 6], part)
        out[:6] = part
        out[6:8] = jnp.zeros((2, HC), F32)
        out[8:32, : 2 * NS] = rows[:, HC:WIDE]
        out[8:32, 2 * NS :] = jnp.zeros((24, HC - 2 * NS), F32)
        out[32:] = jnp.broadcast_to(local, (8, HC))


def square_kernel(at, a, b, c, d, square):
    refs = (a, b, c, d)
    bc = sum(r[8:32, : 2 * NS] for r in refs)
    total = sum(r[32:, :128] for r in refs)
    square[...] = total + jnp.sum(bc * bc).reshape(1, 1)


def last_kernel(at, a, b, c, d, rows_out, square, all_in, all_bc, all_out, parts):
    x = at[0]
    entries = DM * 1536 + DM * 256 + 1536 * DM
    factor = jnp.minimum(1.0, 1.0 / jnp.sqrt(square[:1, :1] / entries + 1e-06))
    for k, r in enumerate((a, b, c, d)):
        parts[k] = r[...]
    for p in range(NX):
        all_in[:, HC * p : HC * p + HC] = factor * parts[lax.rem(x - p + NX, NX), :6, :]
    rows = sum(r[8:32, : 2 * NS] for r in (a, b, c, d))
    mine = rows[:6]
    for p in range(1, NX):
        mine = jnp.where(x == p, rows[6 * p : 6 * p + 6], mine)
    all_bc[...] = factor * mine
    all_out[:, :HC] = factor * rows_out[:12]
    all_out[:, HC:] = factor * rows_out[12:]


def call(kernel, outs, scratch, args, flops=0):
    moved = sum(a.size * a.dtype.itemsize for a in args)
    return pl.pallas_call(
        kernel,
        out_shape=[jax.ShapeDtypeStruct(*o) for o in outs],
        in_specs=[SMEM] + vm(len(args) - 1),
        out_specs=vm(len(outs)),
        scratch_shapes=[pltpu.VMEM(*s) for s in scratch],
        compiler_params=PARAMS,
        cost_estimate=pl.CostEstimate(flops=flops, bytes_accessed=moved, transcendentals=0),
    )(*args)


def rows_exchange(s_p, s_m, s_2):
    r_2 = move(s_2, "y", 2)
    return [move(s_p, "y", 1), move(s_m, "y", -1), r_2]


def deal(at, which, terms, rows, cols):
    axis = {2: "y", 3: "z"}[which]
    p0, p1, p2, p3 = call(
        functools.partial(deal_kernel, which), [((rows, cols), F32)] * 4, [((4, rows, cols), F32)], [at, *terms]
    )
    r_2 = move(p2, axis, 2)
    return [p0, move(p1, axis, 1), r_2, move(p3, axis, 3)]


def body(tokens, cotangent, log_decay, w_in, w_bc, w_out):
    seq, rec = lax.axis_index("seq"), lax.axis_index("rec")
    x = seq % NX
    at = jnp.stack([x, rec % 2, seq // NX, rec // 2]).astype(jnp.int32)
    tie = lax.optimization_barrier

    (t0,) = pl.pallas_call(
        pack_kernel,
        out_shape=[jax.ShapeDtypeStruct((SEG + 8, DM), F32)],
        in_specs=vm(2),
        out_specs=vm(1),
        compiler_params=PARAMS,
    )(tokens[0], log_decay[0])
    c0 = cotangent[0].astype(F32)
    wi = lax.dynamic_slice(w_in, (0, x * HC), (DM, HC))
    wo = lax.dynamic_slice(w_out, (x * HC, 0), (HC, DM))
    t3, t1 = move(t0, "x", 1), move(t0, "x", -1)
    t3, c0 = tie((t3, c0))
    t2 = move(t3, "x", 1)
    c0, t1 = tie((c0, t1))
    c1, c3 = move(c0, "x", -1), move(c0, "x", 1)
    t1, wi, wo = tie((t1, wi, wo))

    tall = ((TALL, HC), F32)
    edges = ((2, NX, NS, HC), F32)

    def of_tokens(n):
        return [
            ((n, 8, SEG), F32), ((n, 8, SEG), F32), ((n, SEG, HC), F32), ((n, SEG, HC), F32),
            ((n, SEG, DM), BF16), ((n, SEG, HC), BF16), ((n, SEG, 2 * HC), BF16), ((n, SEG, 2 * NS), BF16),
        ]

    def ends(n):
        return ((n, NS, 2 * HC), F32)

    flops = 2 * SEG * (DM * (HC + 2 * NS) + NS * 2 * HC)
    row = ((8, SEG), F32)
    three = call(
        tok_kernel_a, [*of_tokens(3), ends(3)], [row], [at, tokens[0], log_decay[0], t1, t3, wi, w_bc], 3 * flops
    )
    def mats(n):
        return [((n, NH, SEG, SEG), BF16), ((n, NH, SEG, SEG), BF16), ((n, SEG, HC), F32)]

    within = 2 * SEG * SEG * 2 * HC
    mats_a = call(
        functools.partial(decay_kernel, 0, 3), mats(3), [], [at, *three[:4], three[5], three[7]], 3 * within
    )
    t2, c1, *both = tie((t2, c1, *three, *mats_a))
    three, mats_a = both[:9], both[9:]
    c2 = move(c1, "x", -1)
    cirow, cerow, ci, ce, tokb, xs, xfr, bc, pre_s, *s_rows = call(
        tok_kernel_b, [*of_tokens(4), edges, tall, tall, tall], [ends(4), row], [at, t2, wi, w_bc, *three], flops
    )
    q_rows = rows_exchange(*s_rows)
    two = [((2, SEG, DM), BF16), ((2, SEG, HC), BF16), ((2, SEG, 2 * HC), BF16)]
    flops = 1024 * (DM * HC + NS * 2 * HC)
    cotb_a, dy_a, dyfr_a, ends_a = call(
        cot_kernel_a, [*two, ends(2)], [ends(4)], [at, cotangent[0], c1, wo, ci, ce, bc], flops
    )
    mats_b = call(functools.partial(decay_kernel, 3, 1), mats(1), [], [at, cirow, cerow, ci, ce, xs, bc], within)
    c3, c2, ends_a, *mats_b = tie((c3, c2, ends_a, *mats_b))
    cotb_b, dy_b, dyfr_b, pre_d, *s_rows = call(
        cot_kernel_b, [*two, edges, tall, tall, tall], [ends(4)], [at, c3, c2, wo, ci, ce, bc, ends_a], flops
    )
    p_rows = rows_exchange(*s_rows)
    g_out, dxi, dci, dbi = call(
        inner_kernel,
        [((2, ROWS, HC), F32), ((NX, SEG, HC), F32), ((NX, SEG, NS), F32), ((NX, SEG, NS), F32)],
        [((NX, NS, 2 * HC), BF16), ((NX * SEG, HC), BF16)],
        [at, xs, bc, dy_a, dy_b, dyfr_a, dyfr_b, cotb_a, cotb_b, ci, ce, pre_s, *q_rows, *mats_a, *mats_b],
        2 * 1024 * (HC * DM + 5 * SEG * HC + 6 * NS * HC),
    )
    keep, send, dz = call(
        outer_kernel,
        [((ROWS, ALL), F32), ((ROWS, ALL), F32), ((NX, SEG, WIDE), BF16)],
        [((NX, NS, 2 * HC), BF16), ((DM, WIDE), F32)],
        [at, tokb, xfr, bc, ci, ce, pre_d, *p_rows, dxi, dci, dbi, g_out],
        2 * 1024 * (WIDE * DM + 4 * NS * HC),
    )
    got = move(send, "c", 1)
    terms = deal(at, 2, [keep, got], 96, ALL)
    whole = ((SEG, DM), F32)
    d0, d1, d2, d3 = call(tokens_kernel, [whole] * 4, [], [at, dz, wi, w_bc], 2 * 1024 * WIDE * DM)
    far, d3 = tie((move(d2, "x", 1), d3))
    (s1,) = call(pass_kernel, [whole], [], [at, d1, far])
    m1, m3 = move(s1, "x", 1), move(d3, "x", -1)
    d_tok = (d0 + m1 + m3).astype(BF16)
    terms = deal(at, 3, terms, 24, ALL)
    p0, p1, p2, p3, rows_out = call(
        cut_kernel, [((40, HC), F32)] * 4 + [((24, HC), F32)], [], [at, *terms]
    )
    pieces = [p0, move(p1, "x", 1), move(p2, "x", 2), move(p3, "x", 3)]
    lanes = NX * NY
    pairs = [(r * lanes + i, 2 * NZ * NY * (i % NX) + r * NY + i // NX) for r in range(2 * NZ) for i in range(lanes)]
    rows_out = lax.ppermute(rows_out, ("rec", "seq"), pairs)
    (square,) = call(square_kernel, [((8, 128), F32)], [], [at, *pieces])
    for axis in ("y", "z"):
        square = square + (move(square, axis, 1) + move(square, axis, 3) + move(square, axis, 2))
    square = square + move(square, "c", 1)
    all_in, all_bc, all_out = call(
        last_kernel,
        [((6, NX * HC), F32), ((6, 2 * NS), F32), ((12, DM), F32)],
        [((NX, 40, HC), F32)],
        [at, *pieces, rows_out, square],
    )
    return d_tok[None], all_in, all_bc, all_out


def solution(mesh):
    in_specs = (P("rec", "seq", None), P("rec", "seq", None), P("rec", None, "seq"), P(), P(), P())
    out_specs = (
        P("rec", "seq", None),
        P(("rec", "seq"), None),
        P(("rec", "seq"), None),
        P(("rec", "seq"), None),
    )
    return jax.shard_map(body, mesh=mesh, in_specs=in_specs, out_specs=out_specs, check_vma=False)
```

```python
import functools

import jax
import jax.numpy as jnp
from jax import lax
from jax.experimental import pallas as pl
from jax.experimental.pallas import tpu as pltpu
from jax.sharding import PartitionSpec as P

F32 = jnp.float32
BF16 = jnp.bfloat16
NX = 4
NY = 4
NZ = 4
SEG = 256
HALF = SEG // 2
DM = 768
NS = 128
NH = 6
HD = 64
HC = NH * HD
ROWS = DM // 2
WIDE = HC + 2 * NS
ALL = WIDE + HC
TALL = NS + 8


def shift(axis, step, wrap=True):
    if axis == "c":
        return "rec", [(r, r ^ 1) for r in range(2 * NZ)]
    count, stride, total, name = {
        "x": (NX, 1, NX * NY, "seq"),
        "y": (NY, NX, NX * NY, "seq"),
        "z": (NZ, 2, 2 * NZ, "rec"),
    }[axis]
    pairs = []
    for i in range(total):
        at = (i // stride) % count
        to = at + step
        if not wrap and not 0 <= to < count:
            continue
        pairs.append((i, i + (to % count - at) * stride))
    return name, pairs


def move(value, axis, step, wrap=True):
    name, pairs = shift(axis, step, wrap)
    return lax.ppermute(value, name, pairs)


def dot(a, b, ca, cb):
    return lax.dot_general(a, b, (((ca,), (cb,)), ((), ())), preferred_element_type=F32)


def exact(a, b, ca, cb):
    return lax.dot_general(
        a, b, (((ca,), (cb,)), ((), ())), precision=lax.Precision.HIGHEST, preferred_element_type=F32
    )


def place(p, x):
    k = lax.rem(p - x + NX, NX)
    return k ^ (k >> 1)


def vm(n):
    return [pl.BlockSpec(memory_space=pltpu.VMEM)] * n


SMEM = pl.BlockSpec(memory_space=pltpu.SMEM)
PARAMS = pltpu.CompilerParams(vmem_limit_bytes=20 * 2**20)


def send_rows(up, down, log, y, s_p, s_m, s_2):
    s_p[:NS] = jnp.where(y == NY - 1, down, up)
    s_m[:NS] = jnp.where(y == 0, up, down)
    s_2[:NS] = jnp.where(y < 2, up, down)
    log = jnp.broadcast_to(log, (8, HC))
    for s in (s_p, s_m, s_2):
        s[NS:] = log


def from_rows(r_p, r_m, r_2, y):
    def on(yes):
        return jnp.where(yes, 1.0, 0.0).astype(F32)

    l_p, l_m, l_2 = (r[NS : NS + 1, :] for r in (r_p, r_m, r_2))
    v_p, v_m, v_2 = (r[:NS, :] for r in (r_p, r_m, r_2))
    up = v_p * on(y >= 1) + v_2 * (on(y >= 2) * jnp.exp(l_p)) + v_m * (on(y == 3) * jnp.exp(l_p + l_2))
    down = v_m * on(y <= 2) + v_2 * (on(y <= 1) * jnp.exp(l_m)) + v_p * (on(y == 0) * jnp.exp(l_m + l_2))
    return up, down


def row_scan(order, ends, cols, ci, x, pre, which):
    acc = jnp.zeros((NS, HC), F32)
    for p in order:
        k = place(p, x)
        pre[which, k] = acc
        acc = acc * jnp.exp(ci[k, SEG - 1 : SEG, :]) + ends[k, :, cols]
    return acc


def row_log(ci):
    return sum(ci[k, SEG - 1 : SEG, :] for k in range(NX))


FIRST, SECOND = slice(0, HC), slice(HC, 2 * HC)


def pack_kernel(tok, log, out):
    out[:SEG] = tok[...].astype(F32)
    for part in range(3):
        out[SEG:, SEG * part : SEG * part + SEG] = log[8 * part : 8 * part + 8]


def decays(x, toks, own, first, cirow, cerow, ci, ce, la):
    s = lax.broadcasted_iota(jnp.int32, (SEG, SEG), 0)
    t = lax.broadcasted_iota(jnp.int32, (SEG, SEG), 1)
    tri = jnp.where(s <= t, 1.0, 0.0).astype(F32)
    head = lax.broadcasted_iota(jnp.int32, (8, HC), 0) * HD
    lane = lax.broadcasted_iota(jnp.int32, (8, HC), 1)
    spread = jnp.where((lane >= head) & (lane < head + HD), 1.0, 0.0).astype(F32)
    la[...] = jnp.zeros((8, SEG), F32)
    for k, tok in enumerate(toks, first):
        for j in range(NH):
            mine = jnp.zeros((1, SEG), F32)
            for p in range(NX):
                h = NH * p + j
                if tok.shape[0] > SEG:
                    row, part = SEG + h % 8, h // 8
                    its = tok[row : row + 1, SEG * part : SEG * part + SEG]
                else:
                    its = own[h : h + 1]
                mine = jnp.where(x == p, its, mine)
            la[j : j + 1] = mine
        through = exact(la[...], tri, 1, 0)
        before = through - la[...]
        cirow[k] = through
        cerow[k] = before
        ci[k] = exact(through, spread, 0, 0)
        ce[k] = exact(before, spread, 0, 0)


def tok_part(at, toks, own, first, w_in, w_bc, cirow, cerow, ci, ce, tokb, xs, xfr, bc, ends, la):
    decays(at[0], toks, own, first, cirow, cerow, ci, ce, la)
    for k, t in enumerate(toks, first):
        tokb[k] = t[:SEG].astype(BF16)

    def segment(i, _):
        k = first + i
        t = tokb[k]
        xv = dot(t, w_in[...], 1, 0).astype(BF16)
        bv = dot(t, w_bc[...], 1, 0).astype(BF16)
        xs[k] = xv
        bc[k] = bv
        xf = xv.astype(F32)
        last = ci[k, SEG - 1 : SEG, :]
        xfr[k, :, :HC] = (xf * jnp.exp(last - ci[k])).astype(BF16)
        xfr[k, :, HC:] = (xf * jnp.exp(ce[k])).astype(BF16)
        ends[k] = dot(bv[:, :NS], xfr[k], 0, 0)
        return 0

    lax.fori_loop(0, len(toks), segment, 0)


def tok_kernel_a(at, t0, own, t1, t3, w_in, w_bc, *refs):
    tok_part(at, (t0, t1, t3), own, 0, w_in, w_bc, *refs)


def tok_kernel_b(at, t2, w_in, w_bc, *refs):
    given, full, (pre, s_p, s_m, s_2, ends, la) = refs[:9], refs[9:17], refs[17:]
    full = (*full, ends)
    for a, b in zip(given, full, strict=True):
        b[: NX - 1] = a[...]
    tok_part(at, (t2,), None, NX - 1, w_in, w_bc, *full, la)
    x, y, ci = at[0], at[2], full[2]
    up = row_scan(range(NX), ends, FIRST, ci, x, pre, 0)
    down = row_scan(reversed(range(NX)), ends, SECOND, ci, x, pre, 1)
    send_rows(up, down, row_log(ci), y, s_p, s_m, s_2)


def decay_kernel(first, count, at, cirow, cerow, ci, ce, xs, bc, mat, mat_t, y):
    def segment(i, _):
        k = first + i
        b, c = bc[k, :, :NS], bc[k, :, NS:]
        t = lax.broadcasted_iota(jnp.int32, (SEG, SEG), 0)
        s = lax.broadcasted_iota(jnp.int32, (SEG, SEG), 1)
        low, same = t > s, t == s
        scores = dot(c, b, 1, 1)
        lane = lax.broadcasted_iota(jnp.int32, (SEG, 2 * HD), 1)
        for pair in range(NH // 2):
            cols = slice(pair * 2 * HD, (pair + 1) * 2 * HD)
            xp = xs[k, :, cols]
            rows = jnp.zeros((SEG, 2 * HD), F32)
            for j in range(2):
                h = 2 * pair + j
                at_t = slice(h * HD, h * HD + 1)
                diff = jnp.where(
                    low,
                    ci[k, :, at_t] - cirow[k, h : h + 1, :],
                    cerow[k, h : h + 1, :] - ce[k, :, at_t],
                )
                decay = jnp.where(same, 2.0, jnp.exp(diff))
                mat[i, h] = decay.astype(BF16)
                w = (decay * scores).astype(BF16)
                mat_t[i, h] = w.T
                xm = jnp.where((lane < HD) if j == 0 else (lane >= HD), xp, jnp.zeros_like(xp))
                rows = rows + dot(w, xm, 1, 0)
            y[i, :, cols] = rows
        return 0

    lax.fori_loop(0, count, segment, 0)


def cot_part(cots, first, w_out, ci, ce, bc, cotb, dy, dyfr, ends):
    for i, t in enumerate(cots):
        cotb[i] = t[...].astype(BF16)

    def segment(i, _):
        k = first + i
        d = dot(cotb[i], w_out[...], 1, 1)
        dy[i] = d.astype(BF16)
        last = ci[k, SEG - 1 : SEG, :]
        dyfr[i, :, :HC] = (d * jnp.exp(ci[k])).astype(BF16)
        dyfr[i, :, HC:] = (d * jnp.exp(last - ce[k])).astype(BF16)
        ends[k] = dot(bc[k, :, NS:], dyfr[i], 0, 0)
        return 0

    lax.fori_loop(0, len(cots), segment, 0)


def cot_kernel_a(at, c0, c1, w_out, ci, ce, bc, cotb, dy, dyfr, ends_a, ends):
    cot_part((c0, c1), 0, w_out, ci, ce, bc, cotb, dy, dyfr, ends)
    ends_a[...] = ends[:2]


def cot_kernel_b(
    at, c2, c3, w_out, ci, ce, bc, ends_a, cotb, dy, dyfr, pre, s_p, s_m, s_2, ends
):
    x, y = at[0], at[2]
    ends[:2] = ends_a[...]
    cot_part((c2, c3), 2, w_out, ci, ce, bc, cotb, dy, dyfr, ends)
    down = row_scan(reversed(range(NX)), ends, FIRST, ci, x, pre, 0)
    up = row_scan(range(NX), ends, SECOND, ci, x, pre, 1)
    send_rows(up, down, row_log(ci), y, s_p, s_m, s_2)


def enter(pre, which, q, ci, x, order, out, cols):
    log = jnp.zeros((1, HC), F32)
    for p in order:
        k = place(p, x)
        out[k, :, cols] = (pre[which, k] + q * jnp.exp(log)).astype(BF16)
        log = log + ci[k, SEG - 1 : SEG, :]


def blocks():
    rows = []
    for j in range(2 * NZ * NY):
        z, c, y = j // 8, j // 4 % 2, j % 4
        rows.append((j, c, 24 * (4 * y + z if c == 0 else 4 * z + y)))
    return rows


def inner_kernel(
    at, xs, bc, dy_a, dy_b, dyfr_a, dyfr_b, cotb_a, cotb_b, ci, ce, pre, r_p, r_m, r_2,
    mat_a, mat_t_a, y_a, mat_b, mat_t_b, y_b,
    g, dxi, dci, dbi, sr, yb,
):
    x, y_at = at[0], at[2]
    up, down = from_rows(r_p, r_m, r_2, y_at)
    enter(pre, 0, up, ci, x, range(NX), sr, pl.ds(0, HC))
    enter(pre, 1, down, ci, x, reversed(range(NX)), sr, pl.ds(HC, HC))

    def run(first, count, mat, mat_t, y_in, m0, dy, dyfr, d0):
        def segment(n, _):
            k, m, i = first + n, m0 + n, d0 + n
            b, c = bc[k, :, :NS], bc[k, :, NS:]
            lane = lax.broadcasted_iota(jnp.int32, (SEG, 2 * HD), 1)
            carry = dot(c, sr[k], 1, 0)
            total = jnp.zeros((SEG, SEG), F32)
            for pair in range(NH // 2):
                cols = slice(pair * 2 * HD, (pair + 1) * 2 * HD)
                xp, dp = xs[k, :, cols], dy[i, :, cols]
                dx = jnp.zeros((SEG, 2 * HD), F32)
                for j in range(2):
                    h = 2 * pair + j
                    dm = jnp.where((lane < HD) if j == 0 else (lane >= HD), dp, jnp.zeros_like(dp))
                    total = total + mat[m, h].astype(F32) * dot(dm, xp, 1, 1)
                    dx = dx + dot(mat_t[m, h], dm, 1, 0)
                last = ci[k, SEG - 1 : SEG, cols]
                y = y_in[m, :, cols] + carry[:, cols] * jnp.exp(ci[k, :, cols])
                y = y + carry[:, slice(HC + cols.start, HC + cols.stop)] * jnp.exp(last - ce[k, :, cols])
                yb[pl.ds(k * SEG, SEG), cols] = y.astype(BF16)
                dxi[k, :, cols] = dx
            total = total.astype(BF16)
            dci[k] = dot(total, b, 1, 0) + dot(dyfr[i], sr[k], 1, 1)
            dbi[k] = dot(total, c, 0, 0)
            return 0

        lax.fori_loop(0, count, segment, 0)

    run(0, 2, mat_a, mat_t_a, y_a, 0, dy_a, dyfr_a, 0)
    run(2, 1, mat_a, mat_t_a, y_a, 2, dy_b, dyfr_b, 0)
    run(3, 1, mat_b, mat_t_b, y_b, 0, dy_b, dyfr_b, 1)
    half = 2 * SEG
    raw = dot(yb[:half, :], cotb_a[...].reshape(half, DM), 0, 0)
    raw = raw + dot(yb[half:, :], cotb_b[...].reshape(half, DM), 0, 0)
    for j, c, row in blocks():
        g[c, row : row + 12, :] = raw[12 * j : 12 * j + 12, :HC]
        g[c, row + 12 : row + 24, :] = raw[12 * j : 12 * j + 12, HC:]


def outer_kernel(
    at, tokb, xfr, bc, ci, ce, pre, r_p, r_m, r_2, dxi, dci, dbi, g_out, keep, send, dz, ds, g
):
    x, core, y_at = at[0], at[1], at[2]
    up, down = from_rows(r_p, r_m, r_2, y_at)
    enter(pre, 0, down, ci, x, reversed(range(NX)), ds, pl.ds(0, HC))
    enter(pre, 1, up, ci, x, range(NX), ds, pl.ds(HC, HC))

    def segment(k, _):
        b = bc[k, :, :NS]
        last = ci[k, SEG - 1 : SEG, :]
        back = dot(b, ds[k], 1, 0)
        dx = dxi[k] + back[:, :HC] * jnp.exp(last - ci[k]) + back[:, HC:] * jnp.exp(ce[k])
        dz[k, :, :HC] = dx.astype(BF16)
        dz[k, :, HC : HC + NS] = (dbi[k] + dot(xfr[k], ds[k], 1, 1)).astype(BF16)
        dz[k, :, HC + NS :] = dci[k].astype(BF16)
        return 0

    lax.fori_loop(0, NX, segment, 0)
    raw = dot(tokb[...].reshape(NX * SEG, DM), dz[...].reshape(NX * SEG, WIDE), 0, 0)
    for j, c, row in blocks():
        g[c, row : row + 24, :] = raw[24 * j : 24 * j + 24, :]
    for out, c in ((keep, core), (send, 1 - core)):
        out[:, :WIDE] = g[c]
        out[:, WIDE:] = g_out[c]


def tokens_kernel(at, dz, w_in, w_bc, d0, d1, d2a, d2b, d3):
    def tokens_of(k):
        return dot(dz[k, :, :HC], w_in[...], 1, 1) + dot(dz[k, :, HC:], w_bc[...], 1, 1)

    d = tokens_of(3)
    d2a[...] = d[:HALF]
    d2b[...] = d[HALF:]
    d1[...] = tokens_of(1)
    d3[...] = tokens_of(2)
    d0[...] = tokens_of(0)


def pass_kernel(at, d1, d3, r_a, r_b, s1, s3):
    s1[:HALF] = d1[:HALF] + r_a[...]
    s1[HALF:] = d1[HALF:]
    s3[:HALF] = d3[:HALF]
    s3[HALF:] = d3[HALF:] + r_b[...]


def deal_kernel(which, at, *refs):
    terms, outs, total = refs[:-5], refs[-5:-1], refs[-1]
    acc = terms[0][...]
    for term in terms[1:]:
        acc = acc + term[...]
    total[...] = acc.reshape(total.shape)
    for k, out in enumerate(outs):
        out[...] = total[lax.rem(at[which] + k, 4)]


def cut_kernel(at, a, b, c, d, p0, p1, p2, p3, rows_out):
    rows = a[...] + b[...] + c[...] + d[...]
    mine, of_out = rows[:, :HC], rows[:, WIDE:]
    rows_out[...] = of_out
    local = (jnp.sum(mine * mine) + jnp.sum(of_out * of_out)).reshape(1, 1)
    for k, out in enumerate((p0, p1, p2, p3)):
        to = lax.rem(at[0] + k, NX)
        part = mine[:6]
        for p in range(1, NX):
            part = jnp.where(to == p, mine[6 * p : 6 * p + 6], part)
        out[:6] = part
        out[6:8] = jnp.zeros((2, HC), F32)
        out[8:32, : 2 * NS] = rows[:, HC:WIDE]
        out[8:32, 2 * NS :] = jnp.zeros((24, HC - 2 * NS), F32)
        out[32:] = jnp.broadcast_to(local, (8, HC))


def square_kernel(at, a, b, c, d, square):
    refs = (a, b, c, d)
    bc = sum(r[8:32, : 2 * NS] for r in refs)
    total = sum(r[32:, :128] for r in refs)
    square[...] = total + jnp.sum(bc * bc).reshape(1, 1)


def last_kernel(at, a, b, c, d, rows_out, square, all_in, all_bc, all_out, parts):
    x = at[0]
    entries = DM * 1536 + DM * 256 + 1536 * DM
    factor = jnp.minimum(1.0, 1.0 / jnp.sqrt(square[:1, :1] / entries + 1e-06))
    for k, r in enumerate((a, b, c, d)):
        parts[k] = r[...]
    for p in range(NX):
        all_in[:, HC * p : HC * p + HC] = factor * parts[lax.rem(x - p + NX, NX), :6, :]
    rows = sum(r[8:32, : 2 * NS] for r in (a, b, c, d))
    mine = rows[:6]
    for p in range(1, NX):
        mine = jnp.where(x == p, rows[6 * p : 6 * p + 6], mine)
    all_bc[...] = factor * mine
    all_out[:, :HC] = factor * rows_out[:12]
    all_out[:, HC:] = factor * rows_out[12:]


def call(kernel, outs, scratch, args, flops=0):
    moved = sum(a.size * a.dtype.itemsize for a in args)
    return pl.pallas_call(
        kernel,
        out_shape=[jax.ShapeDtypeStruct(*o) for o in outs],
        in_specs=[SMEM] + vm(len(args) - 1),
        out_specs=vm(len(outs)),
        scratch_shapes=[pltpu.VMEM(*s) for s in scratch],
        compiler_params=PARAMS,
        cost_estimate=pl.CostEstimate(flops=flops, bytes_accessed=moved, transcendentals=0),
    )(*args)


def rows_exchange(s_p, s_m, s_2):
    r_2 = move(s_2, "y", 2)
    return [move(s_p, "y", 1), move(s_m, "y", -1), r_2]


def deal(at, which, terms, rows, cols):
    p0, p1, p2, p3 = call(
        functools.partial(deal_kernel, which), [((rows, cols), F32)] * 4, [((4, rows, cols), F32)], [at, *terms]
    )

    def send(value, step):
        lanes, pairs = NX * NY, []
        for r in range(2 * NZ):
            for i in range(lanes):
                if (r % 2 == 0) == (which == 4):
                    to = r * lanes + (i + step * NX) % lanes
                else:
                    to = (r + 2 * step) % (2 * NZ) * lanes + i
                pairs.append((r * lanes + i, to))
        return lax.ppermute(value, ("rec", "seq"), pairs)

    r_2 = send(p2, 2)
    return [p0, send(p1, 1), r_2, send(p3, 3)]


def body(tokens, cotangent, log_decay, w_in, w_bc, w_out):
    seq, rec = lax.axis_index("seq"), lax.axis_index("rec")
    x = seq % NX
    core, y, z = rec % 2, seq // NX, rec // 2
    at = jnp.stack([x, core, y, z, jnp.where(core == 0, y, z), jnp.where(core == 0, z, y)]).astype(jnp.int32)
    tie = lax.optimization_barrier

    (t0,) = pl.pallas_call(
        pack_kernel,
        out_shape=[jax.ShapeDtypeStruct((SEG + 8, DM), F32)],
        in_specs=vm(2),
        out_specs=vm(1),
        compiler_params=PARAMS,
    )(tokens[0], log_decay[0])
    c0 = cotangent[0].astype(F32)
    wi = lax.dynamic_slice(w_in, (0, x * HC), (DM, HC))
    wo = lax.dynamic_slice(w_out, (x * HC, 0), (HC, DM))
    t3, t1 = move(t0, "x", 1), move(t0, "x", -1)
    t3, c0 = tie((t3, c0))
    t2 = move(t3, "x", 1)
    c0, t1 = tie((c0, t1))
    c1, c3 = move(c0, "x", -1), move(c0, "x", 1)
    t1, wi, wo = tie((t1, wi, wo))

    tall = ((TALL, HC), F32)
    edges = ((2, NX, NS, HC), F32)

    def of_tokens(n):
        return [
            ((n, 8, SEG), F32), ((n, 8, SEG), F32), ((n, SEG, HC), F32), ((n, SEG, HC), F32),
            ((n, SEG, DM), BF16), ((n, SEG, HC), BF16), ((n, SEG, 2 * HC), BF16), ((n, SEG, 2 * NS), BF16),
        ]

    def ends(n):
        return ((n, NS, 2 * HC), F32)

    flops = 2 * SEG * (DM * (HC + 2 * NS) + NS * 2 * HC)
    row = ((8, SEG), F32)
    three = call(
        tok_kernel_a, [*of_tokens(3), ends(3)], [row], [at, tokens[0], log_decay[0], t1, t3, wi, w_bc], 3 * flops
    )
    def mats(n):
        return [((n, NH, SEG, SEG), BF16), ((n, NH, SEG, SEG), BF16), ((n, SEG, HC), F32)]

    within = 2 * SEG * SEG * 2 * HC
    mats_a = call(
        functools.partial(decay_kernel, 0, 3), mats(3), [], [at, *three[:4], three[5], three[7]], 3 * within
    )
    t2, c1, *both = tie((t2, c1, *three, *mats_a))
    three, mats_a = both[:9], both[9:]
    c2 = move(c1, "x", -1)
    cirow, cerow, ci, ce, tokb, xs, xfr, bc, pre_s, *s_rows = call(
        tok_kernel_b, [*of_tokens(4), edges, tall, tall, tall], [ends(4), row], [at, t2, wi, w_bc, *three], flops
    )
    q_rows = rows_exchange(*s_rows)
    two = [((2, SEG, DM), BF16), ((2, SEG, HC), BF16), ((2, SEG, 2 * HC), BF16)]
    flops = 1024 * (DM * HC + NS * 2 * HC)
    cotb_a, dy_a, dyfr_a, ends_a = call(
        cot_kernel_a, [*two, ends(2)], [ends(4)], [at, cotangent[0], c1, wo, ci, ce, bc], flops
    )
    mats_b = call(functools.partial(decay_kernel, 3, 1), mats(1), [], [at, cirow, cerow, ci, ce, xs, bc], within)
    c3, c2, ends_a, *mats_b = tie((c3, c2, ends_a, *mats_b))
    cotb_b, dy_b, dyfr_b, pre_d, *s_rows = call(
        cot_kernel_b, [*two, edges, tall, tall, tall], [ends(4)], [at, c3, c2, wo, ci, ce, bc, ends_a], flops
    )
    p_rows = rows_exchange(*s_rows)
    g_out, dxi, dci, dbi = call(
        inner_kernel,
        [((2, ROWS, HC), F32), ((NX, SEG, HC), F32), ((NX, SEG, NS), F32), ((NX, SEG, NS), F32)],
        [((NX, NS, 2 * HC), BF16), ((NX * SEG, HC), BF16)],
        [at, xs, bc, dy_a, dy_b, dyfr_a, dyfr_b, cotb_a, cotb_b, ci, ce, pre_s, *q_rows, *mats_a, *mats_b],
        2 * 1024 * (HC * DM + 5 * SEG * HC + 6 * NS * HC),
    )
    keep, send, dz = call(
        outer_kernel,
        [((ROWS, ALL), F32), ((ROWS, ALL), F32), ((NX, SEG, WIDE), BF16)],
        [((NX, NS, 2 * HC), BF16), ((2, ROWS, WIDE), F32)],
        [at, tokb, xfr, bc, ci, ce, pre_d, *p_rows, dxi, dci, dbi, g_out],
        2 * 1024 * (WIDE * DM + 4 * NS * HC),
    )
    got = move(send, "c", 1)
    terms = deal(at, 4, [keep, got], 96, ALL)
    whole, half = ((SEG, DM), F32), ((HALF, DM), F32)
    d0, d1, d2a, d2b, d3 = call(
        tokens_kernel, [whole, whole, half, half, whole], [], [at, dz, wi, w_bc], 2 * 1024 * WIDE * DM
    )
    r_a, r_b = move(d2a, "x", 1), move(d2b, "x", -1)
    s1, s3 = call(pass_kernel, [whole, whole], [], [at, d1, d3, r_a, r_b])
    m1, m3 = move(s1, "x", 1), move(s3, "x", -1)
    d_tok = (d0 + m1 + m3).astype(BF16)
    terms = deal(at, 5, terms, 24, ALL)
    p0, p1, p2, p3, rows_out = call(
        cut_kernel, [((40, HC), F32)] * 4 + [((24, HC), F32)], [], [at, *terms]
    )
    pieces = [p0, move(p1, "x", 1), move(p2, "x", 2), move(p3, "x", 3)]
    lanes = NX * NY
    pairs = [(r * lanes + i, 2 * NZ * NY * (i % NX) + r * NY + i // NX) for r in range(2 * NZ) for i in range(lanes)]
    rows_out = lax.ppermute(rows_out, ("rec", "seq"), pairs)
    (square,) = call(square_kernel, [((8, 128), F32)], [], [at, *pieces])
    for axis in ("y", "z"):
        square = square + (move(square, axis, 1) + move(square, axis, 3) + move(square, axis, 2))
    square = square + move(square, "c", 1)
    all_in, all_bc, all_out = call(
        last_kernel,
        [((6, NX * HC), F32), ((6, 2 * NS), F32), ((12, DM), F32)],
        [((NX, 40, HC), F32)],
        [at, *pieces, rows_out, square],
    )
    return d_tok[None], all_in, all_bc, all_out


def solution(mesh):
    in_specs = (P("rec", "seq", None), P("rec", "seq", None), P("rec", None, "seq"), P(), P(), P())
    out_specs = (
        P("rec", "seq", None),
        P(("rec", "seq"), None),
        P(("rec", "seq"), None),
        P(("rec", "seq"), None),
    )
    return jax.shard_map(body, mesh=mesh, in_specs=in_specs, out_specs=out_specs, check_vma=False)
```

```python
import functools

import jax
import jax.numpy as jnp
from jax import lax
from jax.experimental import pallas as pl
from jax.experimental.pallas import tpu as pltpu
from jax.sharding import PartitionSpec as P

F32 = jnp.float32
BF16 = jnp.bfloat16
NX = 4
NY = 4
NZ = 4
SEG = 256
HALF = SEG // 2
DM = 768
NS = 128
NH = 6
HD = 64
HC = NH * HD
ROWS = DM // 2
WIDE = HC + 2 * NS
ALL = WIDE + HC
TALL = NS + 8


def shift(axis, step, wrap=True):
    if axis == "c":
        return "rec", [(r, r ^ 1) for r in range(2 * NZ)]
    count, stride, total, name = {
        "x": (NX, 1, NX * NY, "seq"),
        "y": (NY, NX, NX * NY, "seq"),
        "z": (NZ, 2, 2 * NZ, "rec"),
    }[axis]
    pairs = []
    for i in range(total):
        at = (i // stride) % count
        to = at + step
        if not wrap and not 0 <= to < count:
            continue
        pairs.append((i, i + (to % count - at) * stride))
    return name, pairs


def move(value, axis, step, wrap=True):
    name, pairs = shift(axis, step, wrap)
    return lax.ppermute(value, name, pairs)


def dot(a, b, ca, cb):
    return lax.dot_general(a, b, (((ca,), (cb,)), ((), ())), preferred_element_type=F32)


def exact(a, b, ca, cb):
    return lax.dot_general(
        a, b, (((ca,), (cb,)), ((), ())), precision=lax.Precision.HIGHEST, preferred_element_type=F32
    )


def place(p, x):
    k = lax.rem(p - x + NX, NX)
    return k ^ (k >> 1)


def vm(n):
    return [pl.BlockSpec(memory_space=pltpu.VMEM)] * n


SMEM = pl.BlockSpec(memory_space=pltpu.SMEM)
PARAMS = pltpu.CompilerParams(vmem_limit_bytes=20 * 2**20)


def send_rows(up, down, log, y, s_p, s_m, s_2):
    s_p[:NS] = jnp.where(y == NY - 1, down, up)
    s_m[:NS] = jnp.where(y == 0, up, down)
    s_2[:NS] = jnp.where(y < 2, up, down)
    log = jnp.broadcast_to(log, (8, HC))
    for s in (s_p, s_m, s_2):
        s[NS:] = log


def from_rows(r_p, r_m, r_2, y):
    def on(yes):
        return jnp.where(yes, 1.0, 0.0).astype(F32)

    l_p, l_m, l_2 = (r[NS : NS + 1, :] for r in (r_p, r_m, r_2))
    v_p, v_m, v_2 = (r[:NS, :] for r in (r_p, r_m, r_2))
    up = v_p * on(y >= 1) + v_2 * (on(y >= 2) * jnp.exp(l_p)) + v_m * (on(y == 3) * jnp.exp(l_p + l_2))
    down = v_m * on(y <= 2) + v_2 * (on(y <= 1) * jnp.exp(l_m)) + v_p * (on(y == 0) * jnp.exp(l_m + l_2))
    return up, down


def row_scan(order, ends, cols, ci, x, pre, which):
    acc = jnp.zeros((NS, HC), F32)
    for p in order:
        k = place(p, x)
        pre[which, k] = acc
        acc = acc * jnp.exp(ci[k, SEG - 1 : SEG, :]) + ends[k, :, cols]
    return acc


def row_log(ci):
    return sum(ci[k, SEG - 1 : SEG, :] for k in range(NX))


FIRST, SECOND = slice(0, HC), slice(HC, 2 * HC)


def pack_kernel(tok, log, out):
    out[:SEG] = tok[...].astype(F32)
    for part in range(3):
        out[SEG:, SEG * part : SEG * part + SEG] = log[8 * part : 8 * part + 8]


def decays(x, toks, own, first, cirow, cerow, ci, ce, la):
    s = lax.broadcasted_iota(jnp.int32, (SEG, SEG), 0)
    t = lax.broadcasted_iota(jnp.int32, (SEG, SEG), 1)
    tri = jnp.where(s <= t, 1.0, 0.0).astype(F32)
    head = lax.broadcasted_iota(jnp.int32, (8, HC), 0) * HD
    lane = lax.broadcasted_iota(jnp.int32, (8, HC), 1)
    spread = jnp.where((lane >= head) & (lane < head + HD), 1.0, 0.0).astype(F32)
    la[...] = jnp.zeros((8, SEG), F32)
    for k, tok in enumerate(toks, first):
        for j in range(NH):
            mine = jnp.zeros((1, SEG), F32)
            for p in range(NX):
                h = NH * p + j
                if tok.shape[0] > SEG:
                    row, part = SEG + h % 8, h // 8
                    its = tok[row : row + 1, SEG * part : SEG * part + SEG]
                else:
                    its = own[h : h + 1]
                mine = jnp.where(x == p, its, mine)
            la[j : j + 1] = mine
        through = exact(la[...], tri, 1, 0)
        before = through - la[...]
        cirow[k] = through
        cerow[k] = before
        ci[k] = exact(through, spread, 0, 0)
        ce[k] = exact(before, spread, 0, 0)


def tok_part(at, toks, own, first, w_in, w_bc, cirow, cerow, ci, ce, tokt, xs, xfr, bc, ends, la, tokb):
    decays(at[0], toks, own, first, cirow, cerow, ci, ce, la)
    for k, t in enumerate(toks, first):
        v = t[:SEG].astype(BF16)
        tokb[k - first] = v
        tokt[:, SEG * k : SEG * k + SEG] = v.T

    def segment(i, _):
        k = first + i
        t = tokb[i]
        xv = dot(t, w_in[...], 1, 0).astype(BF16)
        bv = dot(t, w_bc[...], 1, 0).astype(BF16)
        xs[k] = xv
        bc[k] = bv
        xf = xv.astype(F32)
        last = ci[k, SEG - 1 : SEG, :]
        xfr[k, :, :HC] = (xf * jnp.exp(last - ci[k])).astype(BF16)
        xfr[k, :, HC:] = (xf * jnp.exp(ce[k])).astype(BF16)
        ends[k] = dot(bv[:, :NS], xfr[k], 0, 0)
        return 0

    lax.fori_loop(0, len(toks), segment, 0)


def tok_kernel_a(at, t0, own, t1, t3, w_in, w_bc, *refs):
    tok_part(at, (t0, t1, t3), own, 0, w_in, w_bc, *refs)


def tok_kernel_b(at, t2, w_in, w_bc, *refs):
    given, full, (pre, s_p, s_m, s_2, ends, la, tokb) = refs[:9], refs[9:17], refs[17:]
    full = (*full, ends)
    for a, b in zip(given, full, strict=True):
        if len(a.shape) == 2:
            b[:, : a.shape[1]] = a[...]
        else:
            b[: NX - 1] = a[...]
    tok_part(at, (t2,), None, NX - 1, w_in, w_bc, *full, la, tokb)
    x, y, ci = at[0], at[2], full[2]
    up = row_scan(range(NX), ends, FIRST, ci, x, pre, 0)
    down = row_scan(reversed(range(NX)), ends, SECOND, ci, x, pre, 1)
    send_rows(up, down, row_log(ci), y, s_p, s_m, s_2)


def decay_kernel(first, count, at, cirow, cerow, ci, ce, xs, bc, mat, mat_t, y):
    def segment(i, _):
        k = first + i
        b, c = bc[k, :, :NS], bc[k, :, NS:]
        t = lax.broadcasted_iota(jnp.int32, (SEG, SEG), 0)
        s = lax.broadcasted_iota(jnp.int32, (SEG, SEG), 1)
        low, same = t > s, t == s
        scores = dot(c, b, 1, 1)
        lane = lax.broadcasted_iota(jnp.int32, (SEG, 2 * HD), 1)
        for pair in range(NH // 2):
            cols = slice(pair * 2 * HD, (pair + 1) * 2 * HD)
            xp = xs[k, :, cols]
            rows = jnp.zeros((SEG, 2 * HD), F32)
            for j in range(2):
                h = 2 * pair + j
                at_t = slice(h * HD, h * HD + 1)
                diff = jnp.where(
                    low,
                    ci[k, :, at_t] - cirow[k, h : h + 1, :],
                    cerow[k, h : h + 1, :] - ce[k, :, at_t],
                )
                decay = jnp.where(same, 2.0, jnp.exp(diff))
                mat[i, h] = decay.astype(BF16)
                w = (decay * scores).astype(BF16)
                mat_t[i, h] = w.T
                xm = jnp.where((lane < HD) if j == 0 else (lane >= HD), xp, jnp.zeros_like(xp))
                rows = rows + dot(w, xm, 1, 0)
            y[i, :, cols] = rows
        return 0

    lax.fori_loop(0, count, segment, 0)


def cot_part(cots, first, w_out, ci, ce, bc, cotb, dy, dyfr, ends):
    for i, t in enumerate(cots):
        cotb[i] = t[...].astype(BF16)

    def segment(i, _):
        k = first + i
        d = dot(cotb[i], w_out[...], 1, 1)
        dy[i] = d.astype(BF16)
        last = ci[k, SEG - 1 : SEG, :]
        dyfr[i, :, :HC] = (d * jnp.exp(ci[k])).astype(BF16)
        dyfr[i, :, HC:] = (d * jnp.exp(last - ce[k])).astype(BF16)
        ends[k] = dot(bc[k, :, NS:], dyfr[i], 0, 0)
        return 0

    lax.fori_loop(0, len(cots), segment, 0)


def cot_kernel_a(at, c0, c1, w_out, ci, ce, bc, cotb, dy, dyfr, ends_a, ends):
    cot_part((c0, c1), 0, w_out, ci, ce, bc, cotb, dy, dyfr, ends)
    ends_a[...] = ends[:2]


def cot_kernel_b(
    at, c2, c3, w_out, ci, ce, bc, ends_a, cotb, dy, dyfr, pre, s_p, s_m, s_2, ends
):
    x, y = at[0], at[2]
    ends[:2] = ends_a[...]
    cot_part((c2, c3), 2, w_out, ci, ce, bc, cotb, dy, dyfr, ends)
    down = row_scan(reversed(range(NX)), ends, FIRST, ci, x, pre, 0)
    up = row_scan(range(NX), ends, SECOND, ci, x, pre, 1)
    send_rows(up, down, row_log(ci), y, s_p, s_m, s_2)


def enter(pre, which, q, ci, x, order, out, cols):
    log = jnp.zeros((1, HC), F32)
    for p in order:
        k = place(p, x)
        out[k, :, cols] = (pre[which, k] + q * jnp.exp(log)).astype(BF16)
        log = log + ci[k, SEG - 1 : SEG, :]


def blocks():
    rows = []
    for j in range(2 * NZ * NY):
        z, c, y = j // 8, j // 4 % 2, j % 4
        rows.append((j, c, 24 * (4 * y + z if c == 0 else 4 * z + y)))
    return rows


def inner_kernel(
    at, xs, bc, dy_a, dy_b, dyfr_a, dyfr_b, cotb_a, cotb_b, ci, ce, pre, r_p, r_m, r_2,
    mat_a, mat_t_a, y_a, mat_b, mat_t_b, y_b,
    g, dxi, dci, dbi, sr, yb,
):
    x, y_at = at[0], at[2]
    up, down = from_rows(r_p, r_m, r_2, y_at)
    enter(pre, 0, up, ci, x, range(NX), sr, pl.ds(0, HC))
    enter(pre, 1, down, ci, x, reversed(range(NX)), sr, pl.ds(HC, HC))

    def run(first, count, mat, mat_t, y_in, m0, dy, dyfr, d0):
        def segment(n, _):
            k, m, i = first + n, m0 + n, d0 + n
            b, c = bc[k, :, :NS], bc[k, :, NS:]
            lane = lax.broadcasted_iota(jnp.int32, (SEG, 2 * HD), 1)
            carry = dot(c, sr[k], 1, 0)
            total = jnp.zeros((SEG, SEG), F32)
            for pair in range(NH // 2):
                cols = slice(pair * 2 * HD, (pair + 1) * 2 * HD)
                xp, dp = xs[k, :, cols], dy[i, :, cols]
                dx = jnp.zeros((SEG, 2 * HD), F32)
                for j in range(2):
                    h = 2 * pair + j
                    dm = jnp.where((lane < HD) if j == 0 else (lane >= HD), dp, jnp.zeros_like(dp))
                    total = total + mat[m, h].astype(F32) * dot(dm, xp, 1, 1)
                    dx = dx + dot(mat_t[m, h], dm, 1, 0)
                last = ci[k, SEG - 1 : SEG, cols]
                y = y_in[m, :, cols] + carry[:, cols] * jnp.exp(ci[k, :, cols])
                y = y + carry[:, slice(HC + cols.start, HC + cols.stop)] * jnp.exp(last - ce[k, :, cols])
                yb[pl.ds(k * SEG, SEG), cols] = y.astype(BF16)
                dxi[k, :, cols] = dx
            total = total.astype(BF16)
            dci[k] = dot(total, b, 1, 0) + dot(dyfr[i], sr[k], 1, 1)
            dbi[k] = dot(total, c, 0, 0)
            return 0

        lax.fori_loop(0, count, segment, 0)

    run(0, 2, mat_a, mat_t_a, y_a, 0, dy_a, dyfr_a, 0)
    run(2, 1, mat_a, mat_t_a, y_a, 2, dy_b, dyfr_b, 0)
    run(3, 1, mat_b, mat_t_b, y_b, 0, dy_b, dyfr_b, 1)
    half = 2 * SEG
    raw = dot(yb[:half, :], cotb_a[...].reshape(half, DM), 0, 0)
    raw = raw + dot(yb[half:, :], cotb_b[...].reshape(half, DM), 0, 0)
    for j, c, row in blocks():
        g[c, row : row + 12, :] = raw[12 * j : 12 * j + 12, :HC]
        g[c, row + 12 : row + 24, :] = raw[12 * j : 12 * j + 12, HC:]


def outer_kernel(
    at, tokt, xfr, bc, ci, ce, pre, r_p, r_m, r_2, dxi, dci, dbi, g_out, keep, send, dz, ds, g
):
    x, core, y_at = at[0], at[1], at[2]
    up, down = from_rows(r_p, r_m, r_2, y_at)
    enter(pre, 0, down, ci, x, reversed(range(NX)), ds, pl.ds(0, HC))
    enter(pre, 1, up, ci, x, range(NX), ds, pl.ds(HC, HC))

    def segment(k, _):
        b = bc[k, :, :NS]
        last = ci[k, SEG - 1 : SEG, :]
        back = dot(b, ds[k], 1, 0)
        dx = dxi[k] + back[:, :HC] * jnp.exp(last - ci[k]) + back[:, HC:] * jnp.exp(ce[k])
        dz[k, :, :HC] = dx.astype(BF16)
        dz[k, :, HC : HC + NS] = (dbi[k] + dot(xfr[k], ds[k], 1, 1)).astype(BF16)
        dz[k, :, HC + NS :] = dci[k].astype(BF16)
        return 0

    lax.fori_loop(0, NX, segment, 0)
    raw = dot(tokt[...], dz[...].reshape(NX * SEG, WIDE), 1, 0)
    for j, c, row in blocks():
        g[c, row : row + 24, :] = raw[24 * j : 24 * j + 24, :]
    for out, c in ((keep, core), (send, 1 - core)):
        out[:, :WIDE] = g[c]
        out[:, WIDE:] = g_out[c]


def tokens_of(k, dz, w_in, w_bc):
    return dot(dz[k, :, :HC], w_in[...], 1, 1) + dot(dz[k, :, HC:], w_bc[...], 1, 1)


def far_kernel(at, dz, w_in, w_bc, d2a, d2b):
    d = tokens_of(3, dz, w_in, w_bc)
    d2a[...] = d[:HALF]
    d2b[...] = d[HALF:]


def tokens_kernel(at, dz, w_in, w_bc, d0, d1, d3):
    for k, d in enumerate((d0, d1, d3)):
        d[...] = tokens_of(k, dz, w_in, w_bc)


def pass_kernel(at, d1, d3, r_a, r_b, s1, s3):
    s1[:HALF] = d1[:HALF] + r_a[...]
    s1[HALF:] = d1[HALF:]
    s3[:HALF] = d3[:HALF]
    s3[HALF:] = d3[HALF:] + r_b[...]


def deal_kernel(which, at, *refs):
    terms, outs, total = refs[:-5], refs[-5:-1], refs[-1]
    acc = terms[0][...]
    for term in terms[1:]:
        acc = acc + term[...]
    total[...] = acc.reshape(total.shape)
    for k, out in enumerate(outs):
        out[...] = total[lax.rem(at[which] + k, 4)]


def cut_kernel(at, a, b, c, d, p0, p1, p2, p3, rows_out):
    rows = a[...] + b[...] + c[...] + d[...]
    mine, of_out = rows[:, :HC], rows[:, WIDE:]
    rows_out[...] = of_out
    local = (jnp.sum(mine * mine) + jnp.sum(of_out * of_out)).reshape(1, 1)
    for k, out in enumerate((p0, p1, p2, p3)):
        to = lax.rem(at[0] + k, NX)
        part = mine[:6]
        for p in range(1, NX):
            part = jnp.where(to == p, mine[6 * p : 6 * p + 6], part)
        out[:6] = part
        out[6:8] = jnp.zeros((2, HC), F32)
        out[8:32, : 2 * NS] = rows[:, HC:WIDE]
        out[8:32, 2 * NS :] = jnp.zeros((24, HC - 2 * NS), F32)
        out[32:] = jnp.broadcast_to(local, (8, HC))


def square_kernel(at, a, b, c, d, square):
    refs = (a, b, c, d)
    bc = sum(r[8:32, : 2 * NS] for r in refs)
    total = sum(r[32:, :128] for r in refs)
    square[...] = total + jnp.sum(bc * bc).reshape(1, 1)


def last_kernel(at, a, b, c, d, rows_out, square, all_in, all_bc, all_out, parts):
    x = at[0]
    entries = DM * 1536 + DM * 256 + 1536 * DM
    factor = jnp.minimum(1.0, 1.0 / jnp.sqrt(square[:1, :1] / entries + 1e-06))
    for k, r in enumerate((a, b, c, d)):
        parts[k] = r[...]
    for p in range(NX):
        all_in[:, HC * p : HC * p + HC] = factor * parts[lax.rem(x - p + NX, NX), :6, :]
    rows = sum(r[8:32, : 2 * NS] for r in (a, b, c, d))
    mine = rows[:6]
    for p in range(1, NX):
        mine = jnp.where(x == p, rows[6 * p : 6 * p + 6], mine)
    all_bc[...] = factor * mine
    all_out[:, :HC] = factor * rows_out[:12]
    all_out[:, HC:] = factor * rows_out[12:]


def call(kernel, outs, scratch, args, flops=0):
    moved = sum(a.size * a.dtype.itemsize for a in args)
    return pl.pallas_call(
        kernel,
        out_shape=[jax.ShapeDtypeStruct(*o) for o in outs],
        in_specs=[SMEM] + vm(len(args) - 1),
        out_specs=vm(len(outs)),
        scratch_shapes=[pltpu.VMEM(*s) for s in scratch],
        compiler_params=PARAMS,
        cost_estimate=pl.CostEstimate(flops=flops, bytes_accessed=moved, transcendentals=0),
    )(*args)


def rows_exchange(s_p, s_m, s_2):
    r_2 = move(s_2, "y", 2)
    return [move(s_p, "y", 1), move(s_m, "y", -1), r_2]


def deal(at, which, terms, rows, cols):
    p0, p1, p2, p3 = call(
        functools.partial(deal_kernel, which), [((rows, cols), F32)] * 4, [((4, rows, cols), F32)], [at, *terms]
    )

    def send(value, step):
        lanes, pairs = NX * NY, []
        for r in range(2 * NZ):
            for i in range(lanes):
                if (r % 2 == 0) == (which == 4):
                    to = r * lanes + (i + step * NX) % lanes
                else:
                    to = (r + 2 * step) % (2 * NZ) * lanes + i
                pairs.append((r * lanes + i, to))
        return lax.ppermute(value, ("rec", "seq"), pairs)

    r_2 = send(p2, 2)
    return [p0, send(p1, 1), r_2, send(p3, 3)]


def body(tokens, cotangent, log_decay, w_in, w_bc, w_out):
    seq, rec = lax.axis_index("seq"), lax.axis_index("rec")
    x = seq % NX
    core, y, z = rec % 2, seq // NX, rec // 2
    at = jnp.stack([x, core, y, z, jnp.where(core == 0, y, z), jnp.where(core == 0, z, y)]).astype(jnp.int32)
    tie = lax.optimization_barrier

    (t0,) = pl.pallas_call(
        pack_kernel,
        out_shape=[jax.ShapeDtypeStruct((SEG + 8, DM), F32)],
        in_specs=vm(2),
        out_specs=vm(1),
        compiler_params=PARAMS,
    )(tokens[0], log_decay[0])
    c0 = cotangent[0].astype(F32)
    wi = lax.dynamic_slice(w_in, (0, x * HC), (DM, HC))
    wo = lax.dynamic_slice(w_out, (x * HC, 0), (HC, DM))
    t3, t1 = move(t0, "x", 1), move(t0, "x", -1)
    t3, c0 = tie((t3, c0))
    t2 = move(t3, "x", 1)
    c0, t1 = tie((c0, t1))
    c1, c3 = move(c0, "x", -1), move(c0, "x", 1)
    t1, wi, wo = tie((t1, wi, wo))

    tall = ((TALL, HC), F32)
    edges = ((2, NX, NS, HC), F32)

    def of_tokens(n):
        return [
            ((n, 8, SEG), F32), ((n, 8, SEG), F32), ((n, SEG, HC), F32), ((n, SEG, HC), F32),
            ((DM, n * SEG), BF16), ((n, SEG, HC), BF16), ((n, SEG, 2 * HC), BF16), ((n, SEG, 2 * NS), BF16),
        ]

    def ends(n):
        return ((n, NS, 2 * HC), F32)

    flops = 2 * SEG * (DM * (HC + 2 * NS) + NS * 2 * HC)
    row = ((8, SEG), F32)
    three = call(
        tok_kernel_a, [*of_tokens(3), ends(3)], [row, ((3, SEG, DM), BF16)], [at, tokens[0], log_decay[0], t1, t3, wi, w_bc], 3 * flops
    )
    def mats(n):
        return [((n, NH, SEG, SEG), BF16), ((n, NH, SEG, SEG), BF16), ((n, SEG, HC), F32)]

    within = 2 * SEG * SEG * 2 * HC
    mats_a = call(
        functools.partial(decay_kernel, 0, 3), mats(3), [], [at, *three[:4], three[5], three[7]], 3 * within
    )
    t2, c1, *both = tie((t2, c1, *three, *mats_a))
    three, mats_a = both[:9], both[9:]
    c2 = move(c1, "x", -1)
    cirow, cerow, ci, ce, tokt, xs, xfr, bc, pre_s, *s_rows = call(
        tok_kernel_b, [*of_tokens(4), edges, tall, tall, tall], [ends(4), row, ((1, SEG, DM), BF16)], [at, t2, wi, w_bc, *three], flops
    )
    q_rows = rows_exchange(*s_rows)
    two = [((2, SEG, DM), BF16), ((2, SEG, HC), BF16), ((2, SEG, 2 * HC), BF16)]
    flops = 1024 * (DM * HC + NS * 2 * HC)
    cotb_a, dy_a, dyfr_a, ends_a = call(
        cot_kernel_a, [*two, ends(2)], [ends(4)], [at, cotangent[0], c1, wo, ci, ce, bc], flops
    )
    mats_b = call(functools.partial(decay_kernel, 3, 1), mats(1), [], [at, cirow, cerow, ci, ce, xs, bc], within)
    c3, c2, ends_a, *mats_b = tie((c3, c2, ends_a, *mats_b))
    cotb_b, dy_b, dyfr_b, pre_d, *s_rows = call(
        cot_kernel_b, [*two, edges, tall, tall, tall], [ends(4)], [at, c3, c2, wo, ci, ce, bc, ends_a], flops
    )
    p_rows = rows_exchange(*s_rows)
    g_out, dxi, dci, dbi = call(
        inner_kernel,
        [((2, ROWS, HC), F32), ((NX, SEG, HC), F32), ((NX, SEG, NS), F32), ((NX, SEG, NS), F32)],
        [((NX, NS, 2 * HC), BF16), ((NX * SEG, HC), BF16)],
        [at, xs, bc, dy_a, dy_b, dyfr_a, dyfr_b, cotb_a, cotb_b, ci, ce, pre_s, *q_rows, *mats_a, *mats_b],
        2 * 1024 * (HC * DM + 5 * SEG * HC + 6 * NS * HC),
    )
    keep, send, dz = call(
        outer_kernel,
        [((ROWS, ALL), F32), ((ROWS, ALL), F32), ((NX, SEG, WIDE), BF16)],
        [((NX, NS, 2 * HC), BF16), ((2, ROWS, WIDE), F32)],
        [at, tokt, xfr, bc, ci, ce, pre_d, *p_rows, dxi, dci, dbi, g_out],
        2 * 1024 * (WIDE * DM + 4 * NS * HC),
    )
    got = move(send, "c", 1)
    terms = deal(at, 4, [keep, got], 96, ALL)
    whole, half = ((SEG, DM), F32), ((HALF, DM), F32)
    flops = 2 * SEG * WIDE * DM
    d2a, d2b = call(far_kernel, [half, half], [], [at, dz, wi, w_bc], flops)
    terms[0], dz_later = tie((terms[0], dz))
    d0, d1, d3 = call(tokens_kernel, [whole] * 3, [], [at, dz_later, wi, w_bc], 3 * flops)
    r_a, r_b = move(d2a, "x", 1), move(d2b, "x", -1)
    s1, s3 = call(pass_kernel, [whole, whole], [], [at, d1, d3, r_a, r_b])
    m1, m3 = move(s1, "x", 1), move(s3, "x", -1)
    d_tok = (d0 + m1 + m3).astype(BF16)
    terms = deal(at, 5, terms, 24, ALL)
    p0, p1, p2, p3, rows_out = call(
        cut_kernel, [((40, HC), F32)] * 4 + [((24, HC), F32)], [], [at, *terms]
    )
    pieces = [p0, move(p1, "x", 1), move(p2, "x", 2), move(p3, "x", 3)]
    lanes = NX * NY
    pairs = [(r * lanes + i, 2 * NZ * NY * (i % NX) + r * NY + i // NX) for r in range(2 * NZ) for i in range(lanes)]
    rows_out = lax.ppermute(rows_out, ("rec", "seq"), pairs)
    (square,) = call(square_kernel, [((8, 128), F32)], [], [at, *pieces])
    for axis in ("y", "z"):
        square = square + (move(square, axis, 1) + move(square, axis, 3) + move(square, axis, 2))
    square = square + move(square, "c", 1)
    all_in, all_bc, all_out = call(
        last_kernel,
        [((6, NX * HC), F32), ((6, 2 * NS), F32), ((12, DM), F32)],
        [((NX, 40, HC), F32)],
        [at, *pieces, rows_out, square],
    )
    return d_tok[None], all_in, all_bc, all_out


def solution(mesh):
    in_specs = (P("rec", "seq", None), P("rec", "seq", None), P("rec", None, "seq"), P(), P(), P())
    out_specs = (
        P("rec", "seq", None),
        P(("rec", "seq"), None),
        P(("rec", "seq"), None),
        P(("rec", "seq"), None),
    )
    return jax.shard_map(body, mesh=mesh, in_specs=in_specs, out_specs=out_specs, check_vma=False)
```

```python
import functools

import jax
import jax.numpy as jnp
from jax import lax
from jax.experimental import pallas as pl
from jax.experimental.pallas import tpu as pltpu
from jax.sharding import PartitionSpec as P

F32 = jnp.float32
BF16 = jnp.bfloat16
NX = 4
NY = 4
NZ = 4
SEG = 256
HALF = SEG // 2
DM = 768
NS = 128
NH = 6
HD = 64
HC = NH * HD
ROWS = DM // 2
WIDE = HC + 2 * NS
ALL = WIDE + HC
TALL = NS + 8


def shift(axis, step, wrap=True):
    if axis == "c":
        return "rec", [(r, r ^ 1) for r in range(2 * NZ)]
    count, stride, total, name = {
        "x": (NX, 1, NX * NY, "seq"),
        "y": (NY, NX, NX * NY, "seq"),
        "z": (NZ, 2, 2 * NZ, "rec"),
    }[axis]
    pairs = []
    for i in range(total):
        at = (i // stride) % count
        to = at + step
        if not wrap and not 0 <= to < count:
            continue
        pairs.append((i, i + (to % count - at) * stride))
    return name, pairs


def move(value, axis, step, wrap=True):
    name, pairs = shift(axis, step, wrap)
    return lax.ppermute(value, name, pairs)


def dot(a, b, ca, cb):
    return lax.dot_general(a, b, (((ca,), (cb,)), ((), ())), preferred_element_type=F32)


def exact(a, b, ca, cb):
    return lax.dot_general(
        a, b, (((ca,), (cb,)), ((), ())), precision=lax.Precision.HIGHEST, preferred_element_type=F32
    )


def place(p, x):
    k = lax.rem(p - x + NX, NX)
    return k ^ (k >> 1)


def vm(n):
    return [pl.BlockSpec(memory_space=pltpu.VMEM)] * n


SMEM = pl.BlockSpec(memory_space=pltpu.SMEM)
PARAMS = pltpu.CompilerParams(vmem_limit_bytes=20 * 2**20)


def send_rows(up, down, log, y, s_p, s_m, s_2):
    s_p[:NS] = jnp.where(y == NY - 1, down, up)
    s_m[:NS] = jnp.where(y == 0, up, down)
    s_2[:NS] = jnp.where(y < 2, up, down)
    log = jnp.broadcast_to(log, (8, HC))
    for s in (s_p, s_m, s_2):
        s[NS:] = log


def from_rows(r_p, r_m, r_2, y):
    def on(yes):
        return jnp.where(yes, 1.0, 0.0).astype(F32)

    l_p, l_m, l_2 = (r[NS : NS + 1, :] for r in (r_p, r_m, r_2))
    v_p, v_m, v_2 = (r[:NS, :] for r in (r_p, r_m, r_2))
    up = v_p * on(y >= 1) + v_2 * (on(y >= 2) * jnp.exp(l_p)) + v_m * (on(y == 3) * jnp.exp(l_p + l_2))
    down = v_m * on(y <= 2) + v_2 * (on(y <= 1) * jnp.exp(l_m)) + v_p * (on(y == 0) * jnp.exp(l_m + l_2))
    return up, down


def row_scan(order, ends, cols, ci, x, pre, which):
    acc = jnp.zeros((NS, HC), F32)
    for p in order:
        k = place(p, x)
        pre[which, k] = acc
        acc = acc * jnp.exp(ci[k, SEG - 1 : SEG, :]) + ends[k, :, cols]
    return acc


def row_log(ci):
    return sum(ci[k, SEG - 1 : SEG, :] for k in range(NX))


FIRST, SECOND = slice(0, HC), slice(HC, 2 * HC)


def pack_kernel(tok, log, out):
    out[:SEG] = tok[...].astype(F32)
    for part in range(3):
        out[SEG:, SEG * part : SEG * part + SEG] = log[8 * part : 8 * part + 8]


def decays(x, toks, own, first, cirow, cerow, ci, ce, la):
    s = lax.broadcasted_iota(jnp.int32, (SEG, SEG), 0)
    t = lax.broadcasted_iota(jnp.int32, (SEG, SEG), 1)
    tri = jnp.where(s <= t, 1.0, 0.0).astype(F32)
    head = lax.broadcasted_iota(jnp.int32, (8, HC), 0) * HD
    lane = lax.broadcasted_iota(jnp.int32, (8, HC), 1)
    spread = jnp.where((lane >= head) & (lane < head + HD), 1.0, 0.0).astype(F32)
    la[...] = jnp.zeros((8, SEG), F32)
    for k, tok in enumerate(toks, first):
        for j in range(NH):
            mine = jnp.zeros((1, SEG), F32)
            for p in range(NX):
                h = NH * p + j
                if tok.shape[0] > SEG:
                    row, part = SEG + h % 8, h // 8
                    its = tok[row : row + 1, SEG * part : SEG * part + SEG]
                else:
                    its = own[h : h + 1]
                mine = jnp.where(x == p, its, mine)
            la[j : j + 1] = mine
        through = exact(la[...], tri, 1, 0)
        before = through - la[...]
        cirow[k] = through
        cerow[k] = before
        ci[k] = exact(through, spread, 0, 0)
        ce[k] = exact(before, spread, 0, 0)


def tok_part(at, toks, own, first, w_in, w_bc, cirow, cerow, ci, ce, tokt, xs, xfr, bc, ends, la, tokb):
    decays(at[0], toks, own, first, cirow, cerow, ci, ce, la)
    for k, t in enumerate(toks, first):
        v = t[:SEG].astype(BF16)
        tokb[k - first] = v
        tokt[:, SEG * k : SEG * k + SEG] = v.T

    def segment(i, _):
        k = first + i
        t = tokb[i]
        xv = dot(t, w_in[...], 1, 0).astype(BF16)
        bv = dot(t, w_bc[...], 1, 0).astype(BF16)
        xs[k] = xv
        bc[k] = bv
        xf = xv.astype(F32)
        last = ci[k, SEG - 1 : SEG, :]
        xfr[k, :, :HC] = (xf * jnp.exp(last - ci[k])).astype(BF16)
        xfr[k, :, HC:] = (xf * jnp.exp(ce[k])).astype(BF16)
        ends[k] = dot(bv[:, :NS], xfr[k], 0, 0)
        return 0

    lax.fori_loop(0, len(toks), segment, 0)


def tok_kernel_a(at, t0, own, t1, t3, w_in, w_bc, *refs):
    tok_part(at, (t0, t1, t3), own, 0, w_in, w_bc, *refs)


def tok_kernel_b(at, t2, w_in, w_bc, *refs):
    given, full, (pre, s_p, s_m, s_2, ends, la, tokb) = refs[:9], refs[9:17], refs[17:]
    full = (*full, ends)
    for a, b in zip(given, full, strict=True):
        if len(a.shape) == 2:
            b[:, : a.shape[1]] = a[...]
        else:
            b[: NX - 1] = a[...]
    tok_part(at, (t2,), None, NX - 1, w_in, w_bc, *full, la, tokb)
    x, y, ci = at[0], at[2], full[2]
    up = row_scan(range(NX), ends, FIRST, ci, x, pre, 0)
    down = row_scan(reversed(range(NX)), ends, SECOND, ci, x, pre, 1)
    send_rows(up, down, row_log(ci), y, s_p, s_m, s_2)


def decay_kernel(first, count, at, cirow, cerow, ci, ce, xs, bc, mat, mat_t, y):
    def segment(i, _):
        k = first + i
        b, c = bc[k, :, :NS], bc[k, :, NS:]
        t = lax.broadcasted_iota(jnp.int32, (SEG, SEG), 0)
        s = lax.broadcasted_iota(jnp.int32, (SEG, SEG), 1)
        low, same = t > s, t == s
        scores = dot(c, b, 1, 1)
        lane = lax.broadcasted_iota(jnp.int32, (SEG, 2 * HD), 1)
        for pair in range(NH // 2):
            cols = slice(pair * 2 * HD, (pair + 1) * 2 * HD)
            xp = xs[k, :, cols]
            rows = jnp.zeros((SEG, 2 * HD), F32)
            for j in range(2):
                h = 2 * pair + j
                at_t = slice(h * HD, h * HD + 1)
                diff = jnp.where(
                    low,
                    ci[k, :, at_t] - cirow[k, h : h + 1, :],
                    cerow[k, h : h + 1, :] - ce[k, :, at_t],
                )
                decay = jnp.where(same, 2.0, jnp.exp(diff))
                mat[i, h] = decay.astype(BF16)
                w = (decay * scores).astype(BF16)
                mat_t[i, h] = w.T
                xm = jnp.where((lane < HD) if j == 0 else (lane >= HD), xp, jnp.zeros_like(xp))
                rows = rows + dot(w, xm, 1, 0)
            y[i, :, cols] = rows
        return 0

    lax.fori_loop(0, count, segment, 0)


def cot_part(cots, first, w_out, ci, ce, bc, cotb, dy, dyfr, ends):
    for i, t in enumerate(cots):
        cotb[i] = t[...].astype(BF16)

    def segment(i, _):
        k = first + i
        d = dot(cotb[i], w_out[...], 1, 1)
        dy[i] = d.astype(BF16)
        last = ci[k, SEG - 1 : SEG, :]
        dyfr[i, :, :HC] = (d * jnp.exp(ci[k])).astype(BF16)
        dyfr[i, :, HC:] = (d * jnp.exp(last - ce[k])).astype(BF16)
        ends[k] = dot(bc[k, :, NS:], dyfr[i], 0, 0)
        return 0

    lax.fori_loop(0, len(cots), segment, 0)


def cot_kernel_a(at, c0, c1, w_out, ci, ce, bc, cotb, dy, dyfr, ends_a, ends):
    cot_part((c0, c1), 0, w_out, ci, ce, bc, cotb, dy, dyfr, ends)
    ends_a[...] = ends[:2]


def cot_kernel_b(
    at, c2, c3, w_out, ci, ce, bc, ends_a, cotb, dy, dyfr, pre, s_p, s_m, s_2, ends
):
    x, y = at[0], at[2]
    ends[:2] = ends_a[...]
    cot_part((c2, c3), 2, w_out, ci, ce, bc, cotb, dy, dyfr, ends)
    down = row_scan(reversed(range(NX)), ends, FIRST, ci, x, pre, 0)
    up = row_scan(range(NX), ends, SECOND, ci, x, pre, 1)
    send_rows(up, down, row_log(ci), y, s_p, s_m, s_2)


def enter(pre, which, q, ci, x, order, out, cols):
    log = jnp.zeros((1, HC), F32)
    for p in order:
        k = place(p, x)
        out[k, :, cols] = (pre[which, k] + q * jnp.exp(log)).astype(BF16)
        log = log + ci[k, SEG - 1 : SEG, :]


def blocks():
    rows = []
    for j in range(2 * NZ * NY):
        z, c, y = j // 8, j // 4 % 2, j % 4
        rows.append((j, c, 24 * (4 * y + z if c == 0 else 4 * z + y)))
    return rows


def inner_kernel(
    at, xs, bc, dy_a, dy_b, dyfr_a, dyfr_b, cotb_a, cotb_b, ci, ce, pre, r_p, r_m, r_2,
    mat_a, mat_t_a, y_a, mat_b, mat_t_b, y_b,
    g, dxi, dci, dbi, sr, yb,
):
    x, y_at = at[0], at[2]
    up, down = from_rows(r_p, r_m, r_2, y_at)
    enter(pre, 0, up, ci, x, range(NX), sr, pl.ds(0, HC))
    enter(pre, 1, down, ci, x, reversed(range(NX)), sr, pl.ds(HC, HC))

    def run(first, count, mat, mat_t, y_in, m0, dy, dyfr, d0):
        def segment(n, _):
            k, m, i = first + n, m0 + n, d0 + n
            b, c = bc[k, :, :NS], bc[k, :, NS:]
            lane = lax.broadcasted_iota(jnp.int32, (SEG, 2 * HD), 1)
            carry = dot(c, sr[k], 1, 0)
            total = jnp.zeros((SEG, SEG), F32)
            for pair in range(NH // 2):
                cols = slice(pair * 2 * HD, (pair + 1) * 2 * HD)
                xp, dp = xs[k, :, cols], dy[i, :, cols]
                dx = jnp.zeros((SEG, 2 * HD), F32)
                for j in range(2):
                    h = 2 * pair + j
                    dm = jnp.where((lane < HD) if j == 0 else (lane >= HD), dp, jnp.zeros_like(dp))
                    total = total + mat[m, h].astype(F32) * dot(dm, xp, 1, 1)
                    dx = dx + dot(mat_t[m, h], dm, 1, 0)
                last = ci[k, SEG - 1 : SEG, cols]
                y = y_in[m, :, cols] + carry[:, cols] * jnp.exp(ci[k, :, cols])
                y = y + carry[:, slice(HC + cols.start, HC + cols.stop)] * jnp.exp(last - ce[k, :, cols])
                yb[pl.ds(k * SEG, SEG), cols] = y.astype(BF16)
                dxi[k, :, cols] = dx
            total = total.astype(BF16)
            dci[k] = dot(total, b, 1, 0) + dot(dyfr[i], sr[k], 1, 1)
            dbi[k] = dot(total, c, 0, 0)
            return 0

        lax.fori_loop(0, count, segment, 0)

    run(0, 2, mat_a, mat_t_a, y_a, 0, dy_a, dyfr_a, 0)
    run(2, 1, mat_a, mat_t_a, y_a, 2, dy_b, dyfr_b, 0)
    run(3, 1, mat_b, mat_t_b, y_b, 0, dy_b, dyfr_b, 1)
    half = 2 * SEG
    raw = dot(yb[:half, :], cotb_a[...].reshape(half, DM), 0, 0)
    raw = raw + dot(yb[half:, :], cotb_b[...].reshape(half, DM), 0, 0)
    for j, c, row in blocks():
        g[c, row : row + 12, :] = raw[12 * j : 12 * j + 12, :HC]
        g[c, row + 12 : row + 24, :] = raw[12 * j : 12 * j + 12, HC:]


def outer_kernel(
    at, tokt, xfr, bc, ci, ce, pre, r_p, r_m, r_2, dxi, dci, dbi, g_out, keep, send, dz, ds, g
):
    x, core, y_at = at[0], at[1], at[2]
    up, down = from_rows(r_p, r_m, r_2, y_at)
    enter(pre, 0, down, ci, x, reversed(range(NX)), ds, pl.ds(0, HC))
    enter(pre, 1, up, ci, x, range(NX), ds, pl.ds(HC, HC))

    def segment(k, _):
        b = bc[k, :, :NS]
        last = ci[k, SEG - 1 : SEG, :]
        back = dot(b, ds[k], 1, 0)
        dx = dxi[k] + back[:, :HC] * jnp.exp(last - ci[k]) + back[:, HC:] * jnp.exp(ce[k])
        dz[k, :, :HC] = dx.astype(BF16)
        dz[k, :, HC : HC + NS] = (dbi[k] + dot(xfr[k], ds[k], 1, 1)).astype(BF16)
        dz[k, :, HC + NS :] = dci[k].astype(BF16)
        return 0

    lax.fori_loop(0, NX, segment, 0)
    raw = dot(tokt[...], dz[...].reshape(NX * SEG, WIDE), 1, 0)
    for j, c, row in blocks():
        g[c, row : row + 24, :] = raw[24 * j : 24 * j + 24, :]
    for out, c in ((keep, core), (send, 1 - core)):
        out[:, :WIDE] = g[c]
        out[:, WIDE:] = g_out[c]


def tokens_of(k, dz, w_in, w_bc):
    return dot(dz[k, :, :HC], w_in[...], 1, 1) + dot(dz[k, :, HC:], w_bc[...], 1, 1)


def far_kernel(at, dz, w_in, w_bc, d2a, d2b):
    d = tokens_of(3, dz, w_in, w_bc)
    d2a[...] = d[:HALF]
    d2b[...] = d[HALF:]


def tokens_kernel(at, dz, w_in, w_bc, d0, d1, d3):
    for k, d in enumerate((d0, d1, d3)):
        d[...] = tokens_of(k, dz, w_in, w_bc)


def pass_kernel(at, d1, d3, r_a, r_b, s1, s3):
    s1[:HALF] = d1[:HALF] + r_a[...]
    s1[HALF:] = d1[HALF:]
    s3[:HALF] = d3[:HALF]
    s3[HALF:] = d3[HALF:] + r_b[...]


def deal_kernel(which, at, *refs):
    terms, outs, total = refs[:-5], refs[-5:-1], refs[-1]
    acc = terms[0][...]
    for term in terms[1:]:
        acc = acc + term[...]
    total[...] = acc.reshape(total.shape)
    for k, out in enumerate(outs):
        out[...] = total[lax.rem(at[which] + k, 4)]


def cut_kernel(at, a, b, c, d, p0, p1, p2, p3, rows_out):
    rows = a[...] + b[...] + c[...] + d[...]
    mine, of_out = rows[:, :HC], rows[:, WIDE:]
    rows_out[...] = of_out
    local = (jnp.sum(mine * mine) + jnp.sum(of_out * of_out)).reshape(1, 1)
    for k, out in enumerate((p0, p1, p2, p3)):
        to = lax.rem(at[0] + k, NX)
        part = mine[:6]
        for p in range(1, NX):
            part = jnp.where(to == p, mine[6 * p : 6 * p + 6], part)
        out[:6] = part
        out[6:8] = jnp.zeros((2, HC), F32)
        out[8:32, : 2 * NS] = rows[:, HC:WIDE]
        out[8:32, 2 * NS :] = jnp.zeros((24, HC - 2 * NS), F32)
        out[32:] = jnp.broadcast_to(local, (8, HC))


def square_kernel(at, a, b, c, d, square):
    refs = (a, b, c, d)
    bc = sum(r[8:32, : 2 * NS] for r in refs)
    total = sum(r[32:, :128] for r in refs)
    square[...] = total + jnp.sum(bc * bc).reshape(1, 1)


def last_kernel(at, a, b, c, d, rows_out, square, all_in, all_bc, all_out, parts):
    x = at[0]
    entries = DM * 1536 + DM * 256 + 1536 * DM
    factor = jnp.minimum(1.0, 1.0 / jnp.sqrt(square[:1, :1] / entries + 1e-06))
    for k, r in enumerate((a, b, c, d)):
        parts[k] = r[...]
    for p in range(NX):
        all_in[:, HC * p : HC * p + HC] = factor * parts[lax.rem(x - p + NX, NX), :6, :]
    rows = sum(r[8:32, : 2 * NS] for r in (a, b, c, d))
    mine = rows[:6]
    for p in range(1, NX):
        mine = jnp.where(x == p, rows[6 * p : 6 * p + 6], mine)
    all_bc[...] = factor * mine
    all_out[:, :HC] = factor * rows_out[:12]
    all_out[:, HC:] = factor * rows_out[12:]


def call(kernel, outs, scratch, args, flops=0):
    moved = sum(a.size * a.dtype.itemsize for a in args)
    return pl.pallas_call(
        kernel,
        out_shape=[jax.ShapeDtypeStruct(*o) for o in outs],
        in_specs=[SMEM] + vm(len(args) - 1),
        out_specs=vm(len(outs)),
        scratch_shapes=[pltpu.VMEM(*s) for s in scratch],
        compiler_params=PARAMS,
        cost_estimate=pl.CostEstimate(flops=flops, bytes_accessed=moved, transcendentals=0),
    )(*args)


def rows_exchange(s_p, s_m, s_2):
    r_2 = move(s_2, "y", 2)
    return [move(s_p, "y", 1), move(s_m, "y", -1), r_2]


def deal(at, which, terms, rows, cols):
    p0, p1, p2, p3 = call(
        functools.partial(deal_kernel, which), [((rows, cols), F32)] * 4, [((4, rows, cols), F32)], [at, *terms]
    )

    def send(value, step):
        lanes, pairs = NX * NY, []
        for r in range(2 * NZ):
            for i in range(lanes):
                if (r % 2 == 0) == (which == 4):
                    to = r * lanes + (i + step * NX) % lanes
                else:
                    to = (r + 2 * step) % (2 * NZ) * lanes + i
                pairs.append((r * lanes + i, to))
        return lax.ppermute(value, ("rec", "seq"), pairs)

    r_2 = send(p2, 2)
    return [p0, send(p1, 1), r_2, send(p3, 3)]


def body(tokens, cotangent, log_decay, w_in, w_bc, w_out):
    seq, rec = lax.axis_index("seq"), lax.axis_index("rec")
    x = seq % NX
    core, y, z = rec % 2, seq // NX, rec // 2
    at = jnp.stack([x, core, y, z, jnp.where(core == 0, y, z), jnp.where(core == 0, z, y)]).astype(jnp.int32)
    tie = lax.optimization_barrier

    (t0,) = pl.pallas_call(
        pack_kernel,
        out_shape=[jax.ShapeDtypeStruct((SEG + 8, DM), F32)],
        in_specs=vm(2),
        out_specs=vm(1),
        compiler_params=PARAMS,
    )(tokens[0], log_decay[0])
    c0 = cotangent[0].astype(F32)
    wi = lax.dynamic_slice(w_in, (0, x * HC), (DM, HC))
    wo = lax.dynamic_slice(w_out, (x * HC, 0), (HC, DM))
    t3, t1 = move(t0, "x", 1), move(t0, "x", -1)
    t3, c0 = tie((t3, c0))
    t2 = move(t3, "x", 1)
    c0, t1 = tie((c0, t1))
    c1, c3 = move(c0, "x", -1), move(c0, "x", 1)
    t1, wi, wo = tie((t1, wi, wo))

    tall = ((TALL, HC), F32)
    edges = ((2, NX, NS, HC), F32)

    def of_tokens(n):
        return [
            ((n, 8, SEG), F32), ((n, 8, SEG), F32), ((n, SEG, HC), F32), ((n, SEG, HC), F32),
            ((DM, n * SEG), BF16), ((n, SEG, HC), BF16), ((n, SEG, 2 * HC), BF16), ((n, SEG, 2 * NS), BF16),
        ]

    def ends(n):
        return ((n, NS, 2 * HC), F32)

    flops = 2 * SEG * (DM * (HC + 2 * NS) + NS * 2 * HC)
    row = ((8, SEG), F32)
    three = call(
        tok_kernel_a, [*of_tokens(3), ends(3)], [row, ((3, SEG, DM), BF16)], [at, tokens[0], log_decay[0], t1, t3, wi, w_bc], 3 * flops
    )
    def mats(n):
        return [((n, NH, SEG, SEG), BF16), ((n, NH, SEG, SEG), BF16), ((n, SEG, HC), F32)]

    within = 2 * SEG * SEG * 2 * HC
    mats_a = call(
        functools.partial(decay_kernel, 0, 3), mats(3), [], [at, *three[:4], three[5], three[7]], 3 * within
    )
    t2, c1, *both = tie((t2, c1, *three, *mats_a))
    three, mats_a = both[:9], both[9:]
    c2 = move(c1, "x", -1)
    cirow, cerow, ci, ce, tokt, xs, xfr, bc, pre_s, *s_rows = call(
        tok_kernel_b, [*of_tokens(4), edges, tall, tall, tall], [ends(4), row, ((1, SEG, DM), BF16)], [at, t2, wi, w_bc, *three], flops
    )
    q_rows = rows_exchange(*s_rows)
    two = [((2, SEG, DM), BF16), ((2, SEG, HC), BF16), ((2, SEG, 2 * HC), BF16)]
    flops = 1024 * (DM * HC + NS * 2 * HC)
    cotb_a, dy_a, dyfr_a, ends_a = call(
        cot_kernel_a, [*two, ends(2)], [ends(4)], [at, cotangent[0], c1, wo, ci, ce, bc], flops
    )
    mats_b = call(functools.partial(decay_kernel, 3, 1), mats(1), [], [at, cirow, cerow, ci, ce, xs, bc], within)
    c3, c2, ends_a, *mats_b = tie((c3, c2, ends_a, *mats_b))
    cotb_b, dy_b, dyfr_b, pre_d, *s_rows = call(
        cot_kernel_b, [*two, edges, tall, tall, tall], [ends(4)], [at, c3, c2, wo, ci, ce, bc, ends_a], flops
    )
    p_rows = rows_exchange(*s_rows)
    g_out, dxi, dci, dbi = call(
        inner_kernel,
        [((2, ROWS, HC), F32), ((NX, SEG, HC), F32), ((NX, SEG, NS), F32), ((NX, SEG, NS), F32)],
        [((NX, NS, 2 * HC), BF16), ((NX * SEG, HC), BF16)],
        [at, xs, bc, dy_a, dy_b, dyfr_a, dyfr_b, cotb_a, cotb_b, ci, ce, pre_s, *q_rows, *mats_a, *mats_b],
        2 * 1024 * (HC * DM + 5 * SEG * HC + 6 * NS * HC),
    )
    keep, send, dz = call(
        outer_kernel,
        [((ROWS, ALL), F32), ((ROWS, ALL), F32), ((NX, SEG, WIDE), BF16)],
        [((NX, NS, 2 * HC), BF16), ((2, ROWS, WIDE), F32)],
        [at, tokt, xfr, bc, ci, ce, pre_d, *p_rows, dxi, dci, dbi, g_out],
        2 * 1024 * (WIDE * DM + 4 * NS * HC),
    )
    got = move(send, "c", 1)
    terms = deal(at, 4, [keep, got], 96, ALL)
    whole, half = ((SEG, DM), F32), ((HALF, DM), F32)
    flops = 2 * SEG * WIDE * DM
    d2a, d2b = call(far_kernel, [half, half], [], [at, dz, wi, w_bc], flops)
    terms[0], dz_later = tie((terms[0], dz))
    d0, d1, d3 = call(tokens_kernel, [whole] * 3, [], [at, dz_later, wi, w_bc], 3 * flops)
    r_a, r_b = move(d2a, "x", 1), move(d2b, "x", -1)
    s1, s3 = call(pass_kernel, [whole, whole], [], [at, d1, d3, r_a, r_b])
    m1, m3 = move(s1, "x", 1), move(s3, "x", -1)
    terms = deal(at, 5, terms, 24, ALL)
    p0, p1, p2, p3, rows_out = call(
        cut_kernel, [((40, HC), F32)] * 4 + [((24, HC), F32)], [], [at, *terms]
    )
    pieces = [p0, move(p1, "x", 1), move(p2, "x", 2), move(p3, "x", 3)]
    lanes = NX * NY
    pairs = [(r * lanes + i, 2 * NZ * NY * (i % NX) + r * NY + i // NX) for r in range(2 * NZ) for i in range(lanes)]
    rows_out = lax.ppermute(rows_out, ("rec", "seq"), pairs)
    (square,) = call(square_kernel, [((8, 128), F32)], [], [at, *pieces])
    for axis in ("y", "z"):
        square = square + (move(square, axis, 1) + move(square, axis, 3) + move(square, axis, 2))
    square, m1, m3, d0 = tie((square, m1, m3, d0))
    d_tok = (d0 + m1 + m3).astype(BF16)
    square = square + move(square, "c", 1)
    square, d_tok = tie((square, d_tok))
    all_in, all_bc, all_out = call(
        last_kernel,
        [((6, NX * HC), F32), ((6, 2 * NS), F32), ((12, DM), F32)],
        [((NX, 40, HC), F32)],
        [at, *pieces, rows_out, square],
    )
    return d_tok[None], all_in, all_bc, all_out


def solution(mesh):
    in_specs = (P("rec", "seq", None), P("rec", "seq", None), P("rec", None, "seq"), P(), P(), P())
    out_specs = (
        P("rec", "seq", None),
        P(("rec", "seq"), None),
        P(("rec", "seq"), None),
        P(("rec", "seq"), None),
    )
    return jax.shard_map(body, mesh=mesh, in_specs=in_specs, out_specs=out_specs, check_vma=False)
```

```python
import functools

import jax
import jax.numpy as jnp
from jax import lax
from jax.experimental import pallas as pl
from jax.experimental.pallas import tpu as pltpu
from jax.sharding import PartitionSpec as P

F32 = jnp.float32
BF16 = jnp.bfloat16
NX = 4
NY = 4
NZ = 4
SEG = 256
HALF = SEG // 2
DM = 768
NS = 128
NH = 6
HD = 64
HC = NH * HD
ROWS = DM // 2
WIDE = HC + 2 * NS
ALL = WIDE + HC
TALL = NS + 8


def shift(axis, step, wrap=True):
    if axis == "c":
        return "rec", [(r, r ^ 1) for r in range(2 * NZ)]
    count, stride, total, name = {
        "x": (NX, 1, NX * NY, "seq"),
        "y": (NY, NX, NX * NY, "seq"),
        "z": (NZ, 2, 2 * NZ, "rec"),
    }[axis]
    pairs = []
    for i in range(total):
        at = (i // stride) % count
        to = at + step
        if not wrap and not 0 <= to < count:
            continue
        pairs.append((i, i + (to % count - at) * stride))
    return name, pairs


def move(value, axis, step, wrap=True):
    name, pairs = shift(axis, step, wrap)
    return lax.ppermute(value, name, pairs)


def dot(a, b, ca, cb):
    return lax.dot_general(a, b, (((ca,), (cb,)), ((), ())), preferred_element_type=F32)


def exact(a, b, ca, cb):
    return lax.dot_general(
        a, b, (((ca,), (cb,)), ((), ())), precision=lax.Precision.HIGHEST, preferred_element_type=F32
    )


def place(p, x):
    k = lax.rem(p - x + NX, NX)
    return k ^ (k >> 1)


def vm(n):
    return [pl.BlockSpec(memory_space=pltpu.VMEM)] * n


SMEM = pl.BlockSpec(memory_space=pltpu.SMEM)
PARAMS = pltpu.CompilerParams(vmem_limit_bytes=20 * 2**20)


def send_rows(up, down, log, y, s_p, s_m, s_2):
    s_p[:NS] = jnp.where(y == NY - 1, down, up)
    s_m[:NS] = jnp.where(y == 0, up, down)
    s_2[:NS] = jnp.where(y < 2, up, down)
    log = jnp.broadcast_to(log, (8, HC))
    for s in (s_p, s_m, s_2):
        s[NS:] = log


def from_rows(r_p, r_m, r_2, y):
    def on(yes):
        return jnp.where(yes, 1.0, 0.0).astype(F32)

    l_p, l_m, l_2 = (r[NS : NS + 1, :] for r in (r_p, r_m, r_2))
    v_p, v_m, v_2 = (r[:NS, :] for r in (r_p, r_m, r_2))
    up = v_p * on(y >= 1) + v_2 * (on(y >= 2) * jnp.exp(l_p)) + v_m * (on(y == 3) * jnp.exp(l_p + l_2))
    down = v_m * on(y <= 2) + v_2 * (on(y <= 1) * jnp.exp(l_m)) + v_p * (on(y == 0) * jnp.exp(l_m + l_2))
    return up, down


def row_scan(order, ends, cols, ci, x, pre, which):
    acc = jnp.zeros((NS, HC), F32)
    for p in order:
        k = place(p, x)
        pre[which, k] = acc
        acc = acc * jnp.exp(ci[k, SEG - 1 : SEG, :]) + ends[k, :, cols]
    return acc


def row_log(ci):
    return sum(ci[k, SEG - 1 : SEG, :] for k in range(NX))


FIRST, SECOND = slice(0, HC), slice(HC, 2 * HC)


def pack_kernel(tok, log, out):
    out[:SEG] = tok[...].astype(F32)
    for part in range(3):
        out[SEG:, SEG * part : SEG * part + SEG] = log[8 * part : 8 * part + 8]


def decays(x, toks, own, first, cirow, cerow, ci, ce, la):
    s = lax.broadcasted_iota(jnp.int32, (SEG, SEG), 0)
    t = lax.broadcasted_iota(jnp.int32, (SEG, SEG), 1)
    tri = jnp.where(s <= t, 1.0, 0.0).astype(F32)
    head = lax.broadcasted_iota(jnp.int32, (8, HC), 0) * HD
    lane = lax.broadcasted_iota(jnp.int32, (8, HC), 1)
    spread = jnp.where((lane >= head) & (lane < head + HD), 1.0, 0.0).astype(F32)
    la[...] = jnp.zeros((8, SEG), F32)
    for k, tok in enumerate(toks, first):
        for j in range(NH):
            mine = jnp.zeros((1, SEG), F32)
            for p in range(NX):
                h = NH * p + j
                if tok.shape[0] > SEG:
                    row, part = SEG + h % 8, h // 8
                    its = tok[row : row + 1, SEG * part : SEG * part + SEG]
                else:
                    its = own[h : h + 1]
                mine = jnp.where(x == p, its, mine)
            la[j : j + 1] = mine
        through = exact(la[...], tri, 1, 0)
        before = through - la[...]
        cirow[k] = through
        cerow[k] = before
        ci[k] = exact(through, spread, 0, 0)
        ce[k] = exact(before, spread, 0, 0)


def tok_part(at, toks, own, first, w_in, w_bc, cirow, cerow, ci, ce, tokt, xs, xfr, bc, ends, la, tokb):
    decays(at[0], toks, own, first, cirow, cerow, ci, ce, la)
    for k, t in enumerate(toks, first):
        v = t[:SEG].astype(BF16)
        tokb[k - first] = v
        tokt[:, SEG * k : SEG * k + SEG] = v.T

    def segment(i, _):
        k = first + i
        t = tokb[i]
        xv = dot(t, w_in[...], 1, 0).astype(BF16)
        bv = dot(t, w_bc[...], 1, 0).astype(BF16)
        xs[k] = xv
        bc[k] = bv
        xf = xv.astype(F32)
        last = ci[k, SEG - 1 : SEG, :]
        xfr[k, :, :HC] = (xf * jnp.exp(last - ci[k])).astype(BF16)
        xfr[k, :, HC:] = (xf * jnp.exp(ce[k])).astype(BF16)
        ends[k] = dot(bv[:, :NS], xfr[k], 0, 0)
        return 0

    lax.fori_loop(0, len(toks), segment, 0)


def tok_kernel_a(at, t0, own, t1, t3, w_in, w_bc, *refs):
    tok_part(at, (t0, t1, t3), own, 0, w_in, w_bc, *refs)


def tok_kernel_b(at, t2, w_in, w_bc, *refs):
    given, full, (pre, s_p, s_m, s_2, ends, la, tokb) = refs[:9], refs[9:17], refs[17:]
    full = (*full, ends)
    for a, b in zip(given, full, strict=True):
        if len(a.shape) == 2:
            b[:, : a.shape[1]] = a[...]
        else:
            b[: NX - 1] = a[...]
    tok_part(at, (t2,), None, NX - 1, w_in, w_bc, *full, la, tokb)
    x, y, ci = at[0], at[2], full[2]
    up = row_scan(range(NX), ends, FIRST, ci, x, pre, 0)
    down = row_scan(reversed(range(NX)), ends, SECOND, ci, x, pre, 1)
    send_rows(up, down, row_log(ci), y, s_p, s_m, s_2)


def decay_kernel(first, count, at, cirow, cerow, ci, ce, xs, bc, mat, mat_t, y):
    def segment(i, _):
        k = first + i
        b, c = bc[k, :, :NS], bc[k, :, NS:]
        t = lax.broadcasted_iota(jnp.int32, (SEG, SEG), 0)
        s = lax.broadcasted_iota(jnp.int32, (SEG, SEG), 1)
        low, same = t > s, t == s
        scores = dot(c, b, 1, 1)
        lane = lax.broadcasted_iota(jnp.int32, (SEG, 2 * HD), 1)
        for pair in range(NH // 2):
            cols = slice(pair * 2 * HD, (pair + 1) * 2 * HD)
            xp = xs[k, :, cols]
            rows = jnp.zeros((SEG, 2 * HD), F32)
            for j in range(2):
                h = 2 * pair + j
                at_t = slice(h * HD, h * HD + 1)
                diff = jnp.where(
                    low,
                    ci[k, :, at_t] - cirow[k, h : h + 1, :],
                    cerow[k, h : h + 1, :] - ce[k, :, at_t],
                )
                decay = jnp.where(same, 2.0, jnp.exp(diff))
                mat[i, h] = decay.astype(BF16)
                w = (decay * scores).astype(BF16)
                mat_t[i, h] = w.T
                xm = jnp.where((lane < HD) if j == 0 else (lane >= HD), xp, jnp.zeros_like(xp))
                rows = rows + dot(w, xm, 1, 0)
            y[i, :, cols] = rows
        return 0

    lax.fori_loop(0, count, segment, 0)


def cot_part(cots, first, w_out, ci, ce, bc, cotb, dy, dyfr, ends):
    for i, t in enumerate(cots):
        cotb[i] = t[...].astype(BF16)

    def segment(i, _):
        k = first + i
        d = dot(cotb[i], w_out[...], 1, 1)
        dy[i] = d.astype(BF16)
        last = ci[k, SEG - 1 : SEG, :]
        dyfr[i, :, :HC] = (d * jnp.exp(ci[k])).astype(BF16)
        dyfr[i, :, HC:] = (d * jnp.exp(last - ce[k])).astype(BF16)
        ends[k] = dot(bc[k, :, NS:], dyfr[i], 0, 0)
        return 0

    lax.fori_loop(0, len(cots), segment, 0)


def cot_kernel_a(at, c0, c1, w_out, ci, ce, bc, cotb, dy, dyfr, ends_a, ends):
    cot_part((c0, c1), 0, w_out, ci, ce, bc, cotb, dy, dyfr, ends)
    ends_a[...] = ends[:2]


def cot_kernel_b(
    at, c2, c3, w_out, ci, ce, bc, ends_a, cotb, dy, dyfr, pre, s_p, s_m, s_2, ends
):
    x, y = at[0], at[2]
    ends[:2] = ends_a[...]
    cot_part((c2, c3), 2, w_out, ci, ce, bc, cotb, dy, dyfr, ends)
    down = row_scan(reversed(range(NX)), ends, FIRST, ci, x, pre, 0)
    up = row_scan(range(NX), ends, SECOND, ci, x, pre, 1)
    send_rows(up, down, row_log(ci), y, s_p, s_m, s_2)


def enter(pre, which, q, ci, x, order, out, cols):
    log = jnp.zeros((1, HC), F32)
    for p in order:
        k = place(p, x)
        out[k, :, cols] = (pre[which, k] + q * jnp.exp(log)).astype(BF16)
        log = log + ci[k, SEG - 1 : SEG, :]


def blocks():
    rows = []
    for j in range(2 * NZ * NY):
        z, c, y = j // 8, j // 4 % 2, j % 4
        rows.append((j, c, 24 * (4 * y + z if c == 0 else 4 * z + y)))
    return rows


def inner_kernel(
    at, xs, bc, dy_a, dy_b, dyfr_a, dyfr_b, cotb_a, cotb_b, ci, ce, pre, r_p, r_m, r_2,
    mat_a, mat_t_a, y_a, mat_b, mat_t_b, y_b,
    g, dxi, dci, dbi, sr, yb,
):
    x, y_at = at[0], at[2]
    up, down = from_rows(r_p, r_m, r_2, y_at)
    enter(pre, 0, up, ci, x, range(NX), sr, pl.ds(0, HC))
    enter(pre, 1, down, ci, x, reversed(range(NX)), sr, pl.ds(HC, HC))

    def run(first, count, mat, mat_t, y_in, m0, dy, dyfr, d0):
        def segment(n, _):
            k, m, i = first + n, m0 + n, d0 + n
            b, c = bc[k, :, :NS], bc[k, :, NS:]
            lane = lax.broadcasted_iota(jnp.int32, (SEG, 2 * HD), 1)
            carry = dot(c, sr[k], 1, 0)
            total = jnp.zeros((SEG, SEG), F32)
            for pair in range(NH // 2):
                cols = slice(pair * 2 * HD, (pair + 1) * 2 * HD)
                xp, dp = xs[k, :, cols], dy[i, :, cols]
                dx = jnp.zeros((SEG, 2 * HD), F32)
                for j in range(2):
                    h = 2 * pair + j
                    dm = jnp.where((lane < HD) if j == 0 else (lane >= HD), dp, jnp.zeros_like(dp))
                    total = total + mat[m, h].astype(F32) * dot(dm, xp, 1, 1)
                    dx = dx + dot(mat_t[m, h], dm, 1, 0)
                last = ci[k, SEG - 1 : SEG, cols]
                y = y_in[m, :, cols] + carry[:, cols] * jnp.exp(ci[k, :, cols])
                y = y + carry[:, slice(HC + cols.start, HC + cols.stop)] * jnp.exp(last - ce[k, :, cols])
                yb[pl.ds(k * SEG, SEG), cols] = y.astype(BF16)
                dxi[k, :, cols] = dx
            total = total.astype(BF16)
            dci[k] = dot(total, b, 1, 0) + dot(dyfr[i], sr[k], 1, 1)
            dbi[k] = dot(total, c, 0, 0)
            return 0

        lax.fori_loop(0, count, segment, 0)

    run(0, 2, mat_a, mat_t_a, y_a, 0, dy_a, dyfr_a, 0)
    run(2, 1, mat_a, mat_t_a, y_a, 2, dy_b, dyfr_b, 0)
    run(3, 1, mat_b, mat_t_b, y_b, 0, dy_b, dyfr_b, 1)
    half = 2 * SEG
    raw = dot(yb[:half, :], cotb_a[...].reshape(half, DM), 0, 0)
    raw = raw + dot(yb[half:, :], cotb_b[...].reshape(half, DM), 0, 0)
    for j, c, row in blocks():
        g[c, row : row + 12, :] = raw[12 * j : 12 * j + 12, :HC]
        g[c, row + 12 : row + 24, :] = raw[12 * j : 12 * j + 12, HC:]


def outer_kernel(
    at, tokt, xfr, bc, ci, ce, pre, r_p, r_m, r_2, dxi, dci, dbi, g_out, keep, send, dz, ds, g
):
    x, core, y_at = at[0], at[1], at[2]
    up, down = from_rows(r_p, r_m, r_2, y_at)
    enter(pre, 0, down, ci, x, reversed(range(NX)), ds, pl.ds(0, HC))
    enter(pre, 1, up, ci, x, range(NX), ds, pl.ds(HC, HC))

    def segment(k, _):
        b = bc[k, :, :NS]
        last = ci[k, SEG - 1 : SEG, :]
        back = dot(b, ds[k], 1, 0)
        dx = dxi[k] + back[:, :HC] * jnp.exp(last - ci[k]) + back[:, HC:] * jnp.exp(ce[k])
        dz[k, :, :HC] = dx.astype(BF16)
        dz[k, :, HC : HC + NS] = (dbi[k] + dot(xfr[k], ds[k], 1, 1)).astype(BF16)
        dz[k, :, HC + NS :] = dci[k].astype(BF16)
        return 0

    lax.fori_loop(0, NX, segment, 0)
    raw = dot(tokt[...], dz[...].reshape(NX * SEG, WIDE), 1, 0)
    for j, c, row in blocks():
        g[c, row : row + 24, :] = raw[24 * j : 24 * j + 24, :]
    for out, c in ((keep, core), (send, 1 - core)):
        out[:, :WIDE] = g[c]
        out[:, WIDE:] = g_out[c]


def tokens_of(k, dz, w_in, w_bc):
    return dot(dz[k, :, :HC], w_in[...], 1, 1) + dot(dz[k, :, HC:], w_bc[...], 1, 1)


def far_kernel(at, dz, w_in, w_bc, d2a, d2b):
    d = tokens_of(3, dz, w_in, w_bc)
    d2a[...] = d[:HALF]
    d2b[...] = d[HALF:]


def tokens_kernel(at, dz, w_in, w_bc, d0, d1, d3):
    for k, d in enumerate((d0, d1, d3)):
        d[...] = tokens_of(k, dz, w_in, w_bc)


def pass_kernel(at, d1, d3, r_a, r_b, s1, s3):
    s1[:HALF] = d1[:HALF] + r_a[...]
    s1[HALF:] = d1[HALF:]
    s3[:HALF] = d3[:HALF]
    s3[HALF:] = d3[HALF:] + r_b[...]


def deal_kernel(which, at, *refs):
    terms, outs, total = refs[:-5], refs[-5:-1], refs[-1]
    acc = terms[0][...]
    for term in terms[1:]:
        acc = acc + term[...]
    total[...] = acc.reshape(total.shape)
    for k, out in enumerate(outs):
        out[...] = total[lax.rem(at[which] + k, 4)]


def cut_kernel(at, a, b, c, d, p0, p1, p2, p3, rows_out):
    rows = a[...] + b[...] + c[...] + d[...]
    mine, of_out = rows[:, :HC], rows[:, WIDE:]
    rows_out[...] = of_out
    local = (jnp.sum(mine * mine) + jnp.sum(of_out * of_out)).reshape(1, 1)
    for k, out in enumerate((p0, p1, p2, p3)):
        to = lax.rem(at[0] + k, NX)
        part = mine[:6]
        for p in range(1, NX):
            part = jnp.where(to == p, mine[6 * p : 6 * p + 6], part)
        out[:6] = part
        out[6:8] = jnp.zeros((2, HC), F32)
        out[8:32, : 2 * NS] = rows[:, HC:WIDE]
        out[8:32, 2 * NS :] = jnp.zeros((24, HC - 2 * NS), F32)
        out[32:] = jnp.broadcast_to(local, (8, HC))


def square_kernel(at, a, b, c, d, square):
    refs = (a, b, c, d)
    bc = sum(r[8:32, : 2 * NS] for r in refs)
    total = sum(r[32:, :128] for r in refs)
    square[...] = total + jnp.sum(bc * bc).reshape(1, 1)


def last_kernel(at, a, b, c, d, rows_out, square, all_in, all_bc, all_out, parts):
    x = at[0]
    entries = DM * 1536 + DM * 256 + 1536 * DM
    factor = jnp.minimum(1.0, 1.0 / jnp.sqrt(square[:1, :1] / entries + 1e-06))
    for k, r in enumerate((a, b, c, d)):
        parts[k] = r[...]
    for p in range(NX):
        all_in[:, HC * p : HC * p + HC] = factor * parts[lax.rem(x - p + NX, NX), :6, :]
    rows = sum(r[8:32, : 2 * NS] for r in (a, b, c, d))
    mine = rows[:6]
    for p in range(1, NX):
        mine = jnp.where(x == p, rows[6 * p : 6 * p + 6], mine)
    all_bc[...] = factor * mine
    all_out[:, :HC] = factor * rows_out[:12]
    all_out[:, HC:] = factor * rows_out[12:]


def call(kernel, outs, scratch, args, flops=0):
    moved = sum(a.size * a.dtype.itemsize for a in args)
    return pl.pallas_call(
        kernel,
        out_shape=[jax.ShapeDtypeStruct(*o) for o in outs],
        in_specs=[SMEM] + vm(len(args) - 1),
        out_specs=vm(len(outs)),
        scratch_shapes=[pltpu.VMEM(*s) for s in scratch],
        compiler_params=PARAMS,
        cost_estimate=pl.CostEstimate(flops=flops, bytes_accessed=moved, transcendentals=0),
    )(*args)


def rows_exchange(s_p, s_m, s_2):
    r_2 = move(s_2, "y", 2)
    return [move(s_p, "y", 1), move(s_m, "y", -1), r_2]


def deal(at, which, terms, rows, cols):
    p0, p1, p2, p3 = call(
        functools.partial(deal_kernel, which), [((rows, cols), F32)] * 4, [((4, rows, cols), F32)], [at, *terms]
    )

    def send(value, step):
        lanes, pairs = NX * NY, []
        for r in range(2 * NZ):
            for i in range(lanes):
                if (r % 2 == 0) == (which == 4):
                    to = r * lanes + (i + step * NX) % lanes
                else:
                    to = (r + 2 * step) % (2 * NZ) * lanes + i
                pairs.append((r * lanes + i, to))
        return lax.ppermute(value, ("rec", "seq"), pairs)

    r_2 = send(p2, 2)
    return [p0, send(p1, 1), r_2, send(p3, 3)]


def body(tokens, cotangent, log_decay, w_in, w_bc, w_out):
    seq, rec = lax.axis_index("seq"), lax.axis_index("rec")
    x = seq % NX
    core, y, z = rec % 2, seq // NX, rec // 2
    at = jnp.stack([x, core, y, z, jnp.where(core == 0, y, z), jnp.where(core == 0, z, y)]).astype(jnp.int32)
    tie = lax.optimization_barrier

    (t0,) = pl.pallas_call(
        pack_kernel,
        out_shape=[jax.ShapeDtypeStruct((SEG + 8, DM), F32)],
        in_specs=vm(2),
        out_specs=vm(1),
        compiler_params=PARAMS,
    )(tokens[0], log_decay[0])
    c0 = cotangent[0].astype(F32)
    wi = lax.dynamic_slice(w_in, (0, x * HC), (DM, HC))
    wo = lax.dynamic_slice(w_out, (x * HC, 0), (HC, DM))
    t3, t1 = move(t0, "x", 1), move(t0, "x", -1)
    t3, c0 = tie((t3, c0))
    t2 = move(t3, "x", 1)
    c0, t1 = tie((c0, t1))
    c1, c3 = move(c0, "x", -1), move(c0, "x", 1)
    t1, wi, wo = tie((t1, wi, wo))

    tall = ((TALL, HC), F32)
    edges = ((2, NX, NS, HC), F32)

    def of_tokens(n):
        return [
            ((n, 8, SEG), F32), ((n, 8, SEG), F32), ((n, SEG, HC), F32), ((n, SEG, HC), F32),
            ((DM, n * SEG), BF16), ((n, SEG, HC), BF16), ((n, SEG, 2 * HC), BF16), ((n, SEG, 2 * NS), BF16),
        ]

    def ends(n):
        return ((n, NS, 2 * HC), F32)

    flops = 2 * SEG * (DM * (HC + 2 * NS) + NS * 2 * HC)
    row = ((8, SEG), F32)
    three = call(
        tok_kernel_a, [*of_tokens(3), ends(3)], [row, ((3, SEG, DM), BF16)], [at, tokens[0], log_decay[0], t1, t3, wi, w_bc], 3 * flops
    )
    def mats(n):
        return [((n, NH, SEG, SEG), BF16), ((n, NH, SEG, SEG), BF16), ((n, SEG, HC), F32)]

    within = 2 * SEG * SEG * 2 * HC
    mats_a = call(
        functools.partial(decay_kernel, 0, 3), mats(3), [], [at, *three[:4], three[5], three[7]], 3 * within
    )
    t2, c1, *both = tie((t2, c1, *three, *mats_a))
    three, mats_a = both[:9], both[9:]
    c2 = move(c1, "x", -1)
    cirow, cerow, ci, ce, tokt, xs, xfr, bc, pre_s, *s_rows = call(
        tok_kernel_b, [*of_tokens(4), edges, tall, tall, tall], [ends(4), row, ((1, SEG, DM), BF16)], [at, t2, wi, w_bc, *three], flops
    )
    q_rows = rows_exchange(*s_rows)
    two = [((2, SEG, DM), BF16), ((2, SEG, HC), BF16), ((2, SEG, 2 * HC), BF16)]
    flops = 1024 * (DM * HC + NS * 2 * HC)
    cotb_a, dy_a, dyfr_a, ends_a = call(
        cot_kernel_a, [*two, ends(2)], [ends(4)], [at, cotangent[0], c1, wo, ci, ce, bc], flops
    )
    mats_b = call(functools.partial(decay_kernel, 3, 1), mats(1), [], [at, cirow, cerow, ci, ce, xs, bc], within)
    c3, c2, ends_a, *mats_b = tie((c3, c2, ends_a, *mats_b))
    cotb_b, dy_b, dyfr_b, pre_d, *s_rows = call(
        cot_kernel_b, [*two, edges, tall, tall, tall], [ends(4)], [at, c3, c2, wo, ci, ce, bc, ends_a], flops
    )
    p_rows = rows_exchange(*s_rows)
    g_out, dxi, dci, dbi = call(
        inner_kernel,
        [((2, ROWS, HC), F32), ((NX, SEG, HC), F32), ((NX, SEG, NS), F32), ((NX, SEG, NS), F32)],
        [((NX, NS, 2 * HC), BF16), ((NX * SEG, HC), BF16)],
        [at, xs, bc, dy_a, dy_b, dyfr_a, dyfr_b, cotb_a, cotb_b, ci, ce, pre_s, *q_rows, *mats_a, *mats_b],
        2 * 1024 * (HC * DM + 5 * SEG * HC + 6 * NS * HC),
    )
    keep, send, dz = call(
        outer_kernel,
        [((ROWS, ALL), F32), ((ROWS, ALL), F32), ((NX, SEG, WIDE), BF16)],
        [((NX, NS, 2 * HC), BF16), ((2, ROWS, WIDE), F32)],
        [at, tokt, xfr, bc, ci, ce, pre_d, *p_rows, dxi, dci, dbi, g_out],
        2 * 1024 * (WIDE * DM + 4 * NS * HC),
    )
    got = move(send, "c", 1)
    terms = deal(at, 4, [keep, got], 96, ALL)
    whole, half = ((SEG, DM), F32), ((HALF, DM), F32)
    flops = 2 * SEG * WIDE * DM
    d2a, d2b = call(far_kernel, [half, half], [], [at, dz, wi, w_bc], flops)
    terms[0], dz_later = tie((terms[0], dz))
    d0, d1, d3 = call(tokens_kernel, [whole] * 3, [], [at, dz_later, wi, w_bc], 3 * flops)
    r_a, r_b = move(d2a, "x", 1), move(d2b, "x", -1)
    s1, s3 = call(pass_kernel, [whole, whole], [], [at, d1, d3, r_a, r_b])
    m1, m3 = move(s1, "x", 1), move(s3, "x", -1)
    terms = deal(at, 5, terms, 24, ALL)
    p0, p1, p2, p3, rows_out = call(
        cut_kernel, [((40, HC), F32)] * 4 + [((24, HC), F32)], [], [at, *terms]
    )
    pieces = [p0, move(p1, "x", 1), move(p2, "x", 2), move(p3, "x", 3)]
    lanes = NX * NY
    pairs = [(r * lanes + i, 2 * NZ * NY * (i % NX) + r * NY + i // NX) for r in range(2 * NZ) for i in range(lanes)]
    rows_out = lax.ppermute(rows_out, ("rec", "seq"), pairs)
    (square,) = call(square_kernel, [((8, 128), F32)], [], [at, *pieces])
    for partner in (lambda i: i ^ 1, lambda i: 3 - i):
        square = square + lax.ppermute(square, "seq", [(i, partner(i // NX) * NX + i % NX) for i in range(lanes)])
    for partner in (lambda i: i ^ 1, lambda i: 3 - i):
        square = square + lax.ppermute(square, "rec", [(r, partner(r // 2) * 2 + r % 2) for r in range(2 * NZ)])
    square, m1, m3, d0 = tie((square, m1, m3, d0))
    d_tok = (d0 + m1 + m3).astype(BF16)
    square = square + move(square, "c", 1)
    square, d_tok = tie((square, d_tok))
    all_in, all_bc, all_out = call(
        last_kernel,
        [((6, NX * HC), F32), ((6, 2 * NS), F32), ((12, DM), F32)],
        [((NX, 40, HC), F32)],
        [at, *pieces, rows_out, square],
    )
    return d_tok[None], all_in, all_bc, all_out


def solution(mesh):
    in_specs = (P("rec", "seq", None), P("rec", "seq", None), P("rec", None, "seq"), P(), P(), P())
    out_specs = (
        P("rec", "seq", None),
        P(("rec", "seq"), None),
        P(("rec", "seq"), None),
        P(("rec", "seq"), None),
    )
    return jax.shard_map(body, mesh=mesh, in_specs=in_specs, out_specs=out_specs, check_vma=False)
```

```python
import functools

import jax
import jax.numpy as jnp
from jax import lax
from jax.experimental import pallas as pl
from jax.experimental.pallas import tpu as pltpu
from jax.sharding import PartitionSpec as P

F32 = jnp.float32
BF16 = jnp.bfloat16
NX = 4
NY = 4
NZ = 4
SEG = 256
HALF = SEG // 2
DM = 768
NS = 128
NH = 6
HD = 64
HC = NH * HD
ROWS = DM // 2
WIDE = HC + 2 * NS
ALL = WIDE + HC
TALL = NS + 8


def shift(axis, step, wrap=True):
    if axis == "c":
        return "rec", [(r, r ^ 1) for r in range(2 * NZ)]
    count, stride, total, name = {
        "x": (NX, 1, NX * NY, "seq"),
        "y": (NY, NX, NX * NY, "seq"),
        "z": (NZ, 2, 2 * NZ, "rec"),
    }[axis]
    pairs = []
    for i in range(total):
        at = (i // stride) % count
        to = at + step
        if not wrap and not 0 <= to < count:
            continue
        pairs.append((i, i + (to % count - at) * stride))
    return name, pairs


def move(value, axis, step, wrap=True):
    name, pairs = shift(axis, step, wrap)
    return lax.ppermute(value, name, pairs)


def dot(a, b, ca, cb):
    return lax.dot_general(a, b, (((ca,), (cb,)), ((), ())), preferred_element_type=F32)


def exact(a, b, ca, cb):
    return lax.dot_general(
        a, b, (((ca,), (cb,)), ((), ())), precision=lax.Precision.HIGHEST, preferred_element_type=F32
    )


def place(p, x):
    k = lax.rem(p - x + NX, NX)
    return k ^ (k >> 1)


def vm(n):
    return [pl.BlockSpec(memory_space=pltpu.VMEM)] * n


SMEM = pl.BlockSpec(memory_space=pltpu.SMEM)
PARAMS = pltpu.CompilerParams(vmem_limit_bytes=20 * 2**20)


def send_rows(up, down, log, y, s_p, s_m, s_2):
    s_p[:NS] = jnp.where(y == NY - 1, down, up)
    s_m[:NS] = jnp.where(y == 0, up, down)
    s_2[:NS] = jnp.where(y < 2, up, down)
    log = jnp.broadcast_to(log, (8, HC))
    for s in (s_p, s_m, s_2):
        s[NS:] = log


def from_rows(r_p, r_m, r_2, y):
    def on(yes):
        return jnp.where(yes, 1.0, 0.0).astype(F32)

    l_p, l_m, l_2 = (r[NS : NS + 1, :] for r in (r_p, r_m, r_2))
    v_p, v_m, v_2 = (r[:NS, :] for r in (r_p, r_m, r_2))
    up = v_p * on(y >= 1) + v_2 * (on(y >= 2) * jnp.exp(l_p)) + v_m * (on(y == 3) * jnp.exp(l_p + l_2))
    down = v_m * on(y <= 2) + v_2 * (on(y <= 1) * jnp.exp(l_m)) + v_p * (on(y == 0) * jnp.exp(l_m + l_2))
    return up, down


def row_scan(order, ends, cols, ci, x, pre, which):
    acc = jnp.zeros((NS, HC), F32)
    for p in order:
        k = place(p, x)
        pre[which, k] = acc
        acc = acc * jnp.exp(ci[k, SEG - 1 : SEG, :]) + ends[k, :, cols]
    return acc


def row_log(ci):
    return sum(ci[k, SEG - 1 : SEG, :] for k in range(NX))


FIRST, SECOND = slice(0, HC), slice(HC, 2 * HC)


def pack_kernel(tok, log, out):
    out[:SEG] = tok[...].astype(F32)
    for part in range(3):
        out[SEG:, SEG * part : SEG * part + SEG] = log[8 * part : 8 * part + 8]


def decays(x, toks, own, first, cirow, cerow, ci, ce, la):
    s = lax.broadcasted_iota(jnp.int32, (SEG, SEG), 0)
    t = lax.broadcasted_iota(jnp.int32, (SEG, SEG), 1)
    tri = jnp.where(s <= t, 1.0, 0.0).astype(F32)
    head = lax.broadcasted_iota(jnp.int32, (8, HC), 0) * HD
    lane = lax.broadcasted_iota(jnp.int32, (8, HC), 1)
    spread = jnp.where((lane >= head) & (lane < head + HD), 1.0, 0.0).astype(F32)
    la[...] = jnp.zeros((8, SEG), F32)
    for k, tok in enumerate(toks, first):
        for j in range(NH):
            mine = jnp.zeros((1, SEG), F32)
            for p in range(NX):
                h = NH * p + j
                if tok.shape[0] > SEG:
                    row, part = SEG + h % 8, h // 8
                    its = tok[row : row + 1, SEG * part : SEG * part + SEG]
                else:
                    its = own[h : h + 1]
                mine = jnp.where(x == p, its, mine)
            la[j : j + 1] = mine
        through = exact(la[...], tri, 1, 0)
        before = through - la[...]
        cirow[k] = through
        cerow[k] = before
        ci[k] = exact(through, spread, 0, 0)
        ce[k] = exact(before, spread, 0, 0)


def tok_part(at, toks, own, first, w_in, w_bc, cirow, cerow, ci, ce, tokt, xs, xfr, bc, ends, la, tokb):
    decays(at[0], toks, own, first, cirow, cerow, ci, ce, la)
    for k, t in enumerate(toks, first):
        v = t[:SEG].astype(BF16)
        tokb[k - first] = v
        tokt[:, SEG * k : SEG * k + SEG] = v.T

    def segment(i, _):
        k = first + i
        t = tokb[i]
        xv = dot(t, w_in[...], 1, 0).astype(BF16)
        bv = dot(t, w_bc[...], 1, 0).astype(BF16)
        xs[k] = xv
        bc[k] = bv
        xf = xv.astype(F32)
        last = ci[k, SEG - 1 : SEG, :]
        xfr[k, :, :HC] = (xf * jnp.exp(last - ci[k])).astype(BF16)
        xfr[k, :, HC:] = (xf * jnp.exp(ce[k])).astype(BF16)
        ends[k] = dot(bv[:, :NS], xfr[k], 0, 0)
        return 0

    lax.fori_loop(0, len(toks), segment, 0)


def tok_kernel_a(at, t0, own, t1, t3, w_in, w_bc, *refs):
    tok_part(at, (t0, t1, t3), own, 0, w_in, w_bc, *refs)


def tok_kernel_b(at, t2, w_in, w_bc, *refs):
    given, full, (pre, s_p, s_m, s_2, ends, la, tokb) = refs[:9], refs[9:17], refs[17:]
    full = (*full, ends)
    for a, b in zip(given, full, strict=True):
        if len(a.shape) == 2:
            b[:, : a.shape[1]] = a[...]
        else:
            b[: NX - 1] = a[...]
    tok_part(at, (t2,), None, NX - 1, w_in, w_bc, *full, la, tokb)
    x, y, ci = at[0], at[2], full[2]
    up = row_scan(range(NX), ends, FIRST, ci, x, pre, 0)
    down = row_scan(reversed(range(NX)), ends, SECOND, ci, x, pre, 1)
    send_rows(up, down, row_log(ci), y, s_p, s_m, s_2)


def decay_kernel(first, count, at, cirow, cerow, ci, ce, xs, bc, mat, mat_t, y):
    def segment(i, _):
        k = first + i
        b, c = bc[k, :, :NS], bc[k, :, NS:]
        t = lax.broadcasted_iota(jnp.int32, (SEG, SEG), 0)
        s = lax.broadcasted_iota(jnp.int32, (SEG, SEG), 1)
        low, same = t > s, t == s
        scores = dot(c, b, 1, 1)
        lane = lax.broadcasted_iota(jnp.int32, (SEG, 2 * HD), 1)
        for pair in range(NH // 2):
            cols = slice(pair * 2 * HD, (pair + 1) * 2 * HD)
            xp = xs[k, :, cols]
            rows = jnp.zeros((SEG, 2 * HD), F32)
            for j in range(2):
                h = 2 * pair + j
                at_t = slice(h * HD, h * HD + 1)
                diff = jnp.where(
                    low,
                    ci[k, :, at_t] - cirow[k, h : h + 1, :],
                    cerow[k, h : h + 1, :] - ce[k, :, at_t],
                )
                decay = jnp.where(same, 2.0, jnp.exp(diff))
                mat[i, h] = decay.astype(BF16)
                w = (decay * scores).astype(BF16)
                mat_t[i, h] = w.T
                xm = jnp.where((lane < HD) if j == 0 else (lane >= HD), xp, jnp.zeros_like(xp))
                rows = rows + dot(w, xm, 1, 0)
            y[i, :, cols] = rows
        return 0

    lax.fori_loop(0, count, segment, 0)


def cot_part(cots, first, w_out, ci, ce, bc, cotb, dy, dyfr, ends):
    for i, t in enumerate(cots):
        cotb[i] = t[...].astype(BF16)

    def segment(i, _):
        k = first + i
        d = dot(cotb[i], w_out[...], 1, 1)
        dy[i] = d.astype(BF16)
        last = ci[k, SEG - 1 : SEG, :]
        dyfr[i, :, :HC] = (d * jnp.exp(ci[k])).astype(BF16)
        dyfr[i, :, HC:] = (d * jnp.exp(last - ce[k])).astype(BF16)
        ends[k] = dot(bc[k, :, NS:], dyfr[i], 0, 0)
        return 0

    lax.fori_loop(0, len(cots), segment, 0)


def cot_kernel_a(at, c0, c1, w_out, ci, ce, bc, cotb, dy, dyfr, ends_a, ends):
    cot_part((c0, c1), 0, w_out, ci, ce, bc, cotb, dy, dyfr, ends)
    ends_a[...] = ends[:2]


def cot_kernel_b(
    at, c2, c3, w_out, ci, ce, bc, ends_a, cotb, dy, dyfr, pre, s_p, s_m, s_2, ends
):
    x, y = at[0], at[2]
    ends[:2] = ends_a[...]
    cot_part((c2, c3), 2, w_out, ci, ce, bc, cotb, dy, dyfr, ends)
    down = row_scan(reversed(range(NX)), ends, FIRST, ci, x, pre, 0)
    up = row_scan(range(NX), ends, SECOND, ci, x, pre, 1)
    send_rows(up, down, row_log(ci), y, s_p, s_m, s_2)


def enter(pre, which, q, ci, x, order, out, cols):
    log = jnp.zeros((1, HC), F32)
    for p in order:
        k = place(p, x)
        out[k, :, cols] = (pre[which, k] + q * jnp.exp(log)).astype(BF16)
        log = log + ci[k, SEG - 1 : SEG, :]


def blocks():
    rows = []
    for j in range(2 * NZ * NY):
        z, c, y = j // 8, j // 4 % 2, j % 4
        rows.append((j, c, 24 * (4 * y + z if c == 0 else 4 * z + y)))
    return rows


def inner_kernel(
    at, xs, bc, dy_a, dy_b, dyfr_a, dyfr_b, cotb_a, cotb_b, ci, ce, pre, r_p, r_m, r_2,
    mat_a, mat_t_a, y_a, mat_b, mat_t_b, y_b,
    g, dxi, dci, dbi, sr, yb,
):
    x, y_at = at[0], at[2]
    up, down = from_rows(r_p, r_m, r_2, y_at)
    enter(pre, 0, up, ci, x, range(NX), sr, pl.ds(0, HC))
    enter(pre, 1, down, ci, x, reversed(range(NX)), sr, pl.ds(HC, HC))

    def run(first, count, mat, mat_t, y_in, m0, dy, dyfr, d0):
        def segment(n, _):
            k, m, i = first + n, m0 + n, d0 + n
            b, c = bc[k, :, :NS], bc[k, :, NS:]
            lane = lax.broadcasted_iota(jnp.int32, (SEG, 2 * HD), 1)
            carry = dot(c, sr[k], 1, 0)
            total = jnp.zeros((SEG, SEG), F32)
            for pair in range(NH // 2):
                cols = slice(pair * 2 * HD, (pair + 1) * 2 * HD)
                xp, dp = xs[k, :, cols], dy[i, :, cols]
                dx = jnp.zeros((SEG, 2 * HD), F32)
                for j in range(2):
                    h = 2 * pair + j
                    dm = jnp.where((lane < HD) if j == 0 else (lane >= HD), dp, jnp.zeros_like(dp))
                    total = total + mat[m, h].astype(F32) * dot(dm, xp, 1, 1)
                    dx = dx + dot(mat_t[m, h], dm, 1, 0)
                last = ci[k, SEG - 1 : SEG, cols]
                y = y_in[m, :, cols] + carry[:, cols] * jnp.exp(ci[k, :, cols])
                y = y + carry[:, slice(HC + cols.start, HC + cols.stop)] * jnp.exp(last - ce[k, :, cols])
                yb[pl.ds(k * SEG, SEG), cols] = y.astype(BF16)
                dxi[k, :, cols] = dx
            total = total.astype(BF16)
            dci[k] = dot(total, b, 1, 0) + dot(dyfr[i], sr[k], 1, 1)
            dbi[k] = dot(total, c, 0, 0)
            return 0

        lax.fori_loop(0, count, segment, 0)

    run(0, 2, mat_a, mat_t_a, y_a, 0, dy_a, dyfr_a, 0)
    run(2, 1, mat_a, mat_t_a, y_a, 2, dy_b, dyfr_b, 0)
    run(3, 1, mat_b, mat_t_b, y_b, 0, dy_b, dyfr_b, 1)
    half = 2 * SEG
    raw = dot(yb[:half, :], cotb_a[...].reshape(half, DM), 0, 0)
    raw = raw + dot(yb[half:, :], cotb_b[...].reshape(half, DM), 0, 0)
    for j, c, row in blocks():
        g[c, row : row + 12, :] = raw[12 * j : 12 * j + 12, :HC]
        g[c, row + 12 : row + 24, :] = raw[12 * j : 12 * j + 12, HC:]


def outer_kernel(
    at, tokt, xfr, bc, ci, ce, pre, r_p, r_m, r_2, dxi, dci, dbi, g_out, keep, send, dz, ds, g
):
    x, core, y_at = at[0], at[1], at[2]
    up, down = from_rows(r_p, r_m, r_2, y_at)
    enter(pre, 0, down, ci, x, reversed(range(NX)), ds, pl.ds(0, HC))
    enter(pre, 1, up, ci, x, range(NX), ds, pl.ds(HC, HC))

    def segment(k, _):
        b = bc[k, :, :NS]
        last = ci[k, SEG - 1 : SEG, :]
        back = dot(b, ds[k], 1, 0)
        dx = dxi[k] + back[:, :HC] * jnp.exp(last - ci[k]) + back[:, HC:] * jnp.exp(ce[k])
        dz[k, :, :HC] = dx.astype(BF16)
        dz[k, :, HC : HC + NS] = (dbi[k] + dot(xfr[k], ds[k], 1, 1)).astype(BF16)
        dz[k, :, HC + NS :] = dci[k].astype(BF16)
        return 0

    lax.fori_loop(0, NX, segment, 0)
    raw = dot(tokt[...], dz[...].reshape(NX * SEG, WIDE), 1, 0)
    for j, c, row in blocks():
        g[c, row : row + 24, :] = raw[24 * j : 24 * j + 24, :]
    for out, c in ((keep, core), (send, 1 - core)):
        out[:, :WIDE] = g[c]
        out[:, WIDE:] = g_out[c]


def tokens_of(k, dz, w_in, w_bc):
    return dot(dz[k, :, :HC], w_in[...], 1, 1) + dot(dz[k, :, HC:], w_bc[...], 1, 1)


def far_kernel(at, dz, w_in, w_bc, d2a, d2b):
    d = tokens_of(3, dz, w_in, w_bc)
    d2a[...] = d[:HALF]
    d2b[...] = d[HALF:]


def tokens_kernel(at, dz, w_in, w_bc, d0, d1, d3):
    for k, d in enumerate((d0, d1, d3)):
        d[...] = tokens_of(k, dz, w_in, w_bc)


def pass_kernel(at, d1, d3, r_a, r_b, s1, s3):
    s1[:HALF] = d1[:HALF] + r_a[...]
    s1[HALF:] = d1[HALF:]
    s3[:HALF] = d3[:HALF]
    s3[HALF:] = d3[HALF:] + r_b[...]


def deal_kernel(which, at, *refs):
    terms, outs, total = refs[:-5], refs[-5:-1], refs[-1]
    acc = terms[0][...]
    for term in terms[1:]:
        acc = acc + term[...]
    total[...] = acc.reshape(total.shape)
    for k, out in enumerate(outs):
        out[...] = total[lax.rem(at[which] + k, 4)]


def cut_kernel(at, a, b, c, d, p0, p1, p2, p3, rows_out):
    rows = a[...] + b[...] + c[...] + d[...]
    mine, of_out = rows[:, :HC], rows[:, WIDE:]
    rows_out[...] = of_out
    local = (jnp.sum(mine * mine) + jnp.sum(of_out * of_out)).reshape(1, 1)
    for k, out in enumerate((p0, p1, p2, p3)):
        to = lax.rem(at[0] + k, NX)
        part = mine[:6]
        for p in range(1, NX):
            part = jnp.where(to == p, mine[6 * p : 6 * p + 6], part)
        out[:6] = part
        out[6:8] = jnp.zeros((2, HC), F32)
        out[8:32, : 2 * NS] = rows[:, HC:WIDE]
        out[8:32, 2 * NS :] = jnp.zeros((24, HC - 2 * NS), F32)
        out[32:] = jnp.broadcast_to(local, (8, HC))


def square_kernel(at, a, b, c, d, square):
    refs = (a, b, c, d)
    bc = sum(r[8:32, : 2 * NS] for r in refs)
    total = sum(r[32:, :128] for r in refs)
    square[...] = total + jnp.sum(bc * bc).reshape(1, 1)


def last_kernel(at, a, b, c, d, rows_out, square, all_in, all_bc, all_out, parts):
    x = at[0]
    entries = DM * 1536 + DM * 256 + 1536 * DM
    factor = jnp.minimum(1.0, 1.0 / jnp.sqrt(square[:1, :1] / entries + 1e-06))
    for k, r in enumerate((a, b, c, d)):
        parts[k] = r[...]
    for p in range(NX):
        all_in[:, HC * p : HC * p + HC] = factor * parts[lax.rem(x - p + NX, NX), :6, :]
    rows = sum(r[8:32, : 2 * NS] for r in (a, b, c, d))
    mine = rows[:6]
    for p in range(1, NX):
        mine = jnp.where(x == p, rows[6 * p : 6 * p + 6], mine)
    all_bc[...] = factor * mine
    all_out[:, :HC] = factor * rows_out[:12]
    all_out[:, HC:] = factor * rows_out[12:]


def call(kernel, outs, scratch, args, flops=0):
    moved = sum(a.size * a.dtype.itemsize for a in args)
    return pl.pallas_call(
        kernel,
        out_shape=[jax.ShapeDtypeStruct(*o) for o in outs],
        in_specs=[SMEM] + vm(len(args) - 1),
        out_specs=vm(len(outs)),
        scratch_shapes=[pltpu.VMEM(*s) for s in scratch],
        compiler_params=PARAMS,
        cost_estimate=pl.CostEstimate(flops=flops, bytes_accessed=moved, transcendentals=0),
    )(*args)


def rows_exchange(s_p, s_m, s_2):
    r_2 = move(s_2, "y", 2)
    return [move(s_p, "y", 1), move(s_m, "y", -1), r_2]


def deal(at, which, terms, rows, cols):
    p0, p1, p2, p3 = call(
        functools.partial(deal_kernel, which), [((rows, cols), F32)] * 4, [((4, rows, cols), F32)], [at, *terms]
    )

    def send(value, step):
        lanes, pairs = NX * NY, []
        for r in range(2 * NZ):
            for i in range(lanes):
                if (r % 2 == 0) == (which == 4):
                    to = r * lanes + (i + step * NX) % lanes
                else:
                    to = (r + 2 * step) % (2 * NZ) * lanes + i
                pairs.append((r * lanes + i, to))
        return lax.ppermute(value, ("rec", "seq"), pairs)

    r_2 = send(p2, 2)
    return [p0, send(p1, 1), r_2, send(p3, 3)]


def body(tokens, cotangent, log_decay, w_in, w_bc, w_out):
    seq, rec = lax.axis_index("seq"), lax.axis_index("rec")
    x = seq % NX
    core, y, z = rec % 2, seq // NX, rec // 2
    at = jnp.stack([x, core, y, z, jnp.where(core == 0, y, z), jnp.where(core == 0, z, y)]).astype(jnp.int32)
    tie = lax.optimization_barrier

    (t0,) = pl.pallas_call(
        pack_kernel,
        out_shape=[jax.ShapeDtypeStruct((SEG + 8, DM), F32)],
        in_specs=vm(2),
        out_specs=vm(1),
        compiler_params=PARAMS,
    )(tokens[0], log_decay[0])
    c0 = cotangent[0].astype(F32)
    wi = lax.dynamic_slice(w_in, (0, x * HC), (DM, HC))
    wo = lax.dynamic_slice(w_out, (x * HC, 0), (HC, DM))
    t3, t1 = move(t0, "x", 1), move(t0, "x", -1)
    t3, c0 = tie((t3, c0))
    t2 = move(t3, "x", 1)
    c0, t1 = tie((c0, t1))
    c1, c3 = move(c0, "x", -1), move(c0, "x", 1)
    t1, wi, wo = tie((t1, wi, wo))

    tall = ((TALL, HC), F32)
    edges = ((2, NX, NS, HC), F32)

    def of_tokens(n):
        return [
            ((n, 8, SEG), F32), ((n, 8, SEG), F32), ((n, SEG, HC), F32), ((n, SEG, HC), F32),
            ((DM, n * SEG), BF16), ((n, SEG, HC), BF16), ((n, SEG, 2 * HC), BF16), ((n, SEG, 2 * NS), BF16),
        ]

    def ends(n):
        return ((n, NS, 2 * HC), F32)

    flops = 2 * SEG * (DM * (HC + 2 * NS) + NS * 2 * HC)
    row = ((8, SEG), F32)
    three = call(
        tok_kernel_a, [*of_tokens(3), ends(3)], [row, ((3, SEG, DM), BF16)], [at, tokens[0], log_decay[0], t1, t3, wi, w_bc], 3 * flops
    )
    def mats(n):
        return [((n, NH, SEG, SEG), BF16), ((n, NH, SEG, SEG), BF16), ((n, SEG, HC), F32)]

    within = 2 * SEG * SEG * 2 * HC
    mats_a = call(
        functools.partial(decay_kernel, 0, 3), mats(3), [], [at, *three[:4], three[5], three[7]], 3 * within
    )
    t2, c1, *both = tie((t2, c1, *three, *mats_a))
    three, mats_a = both[:9], both[9:]
    c2 = move(c1, "x", -1)
    cirow, cerow, ci, ce, tokt, xs, xfr, bc, pre_s, *s_rows = call(
        tok_kernel_b, [*of_tokens(4), edges, tall, tall, tall], [ends(4), row, ((1, SEG, DM), BF16)], [at, t2, wi, w_bc, *three], flops
    )
    q_rows = rows_exchange(*s_rows)
    two = [((2, SEG, DM), BF16), ((2, SEG, HC), BF16), ((2, SEG, 2 * HC), BF16)]
    flops = 1024 * (DM * HC + NS * 2 * HC)
    cotb_a, dy_a, dyfr_a, ends_a = call(
        cot_kernel_a, [*two, ends(2)], [ends(4)], [at, cotangent[0], c1, wo, ci, ce, bc], flops
    )
    mats_b = call(functools.partial(decay_kernel, 3, 1), mats(1), [], [at, cirow, cerow, ci, ce, xs, bc], within)
    c3, c2, ends_a, *mats_b = tie((c3, c2, ends_a, *mats_b))
    cotb_b, dy_b, dyfr_b, pre_d, *s_rows = call(
        cot_kernel_b, [*two, edges, tall, tall, tall], [ends(4)], [at, c3, c2, wo, ci, ce, bc, ends_a], flops
    )
    p_rows = rows_exchange(*s_rows)
    g_out, dxi, dci, dbi = call(
        inner_kernel,
        [((2, ROWS, HC), F32), ((NX, SEG, HC), F32), ((NX, SEG, NS), F32), ((NX, SEG, NS), F32)],
        [((NX, NS, 2 * HC), BF16), ((NX * SEG, HC), BF16)],
        [at, xs, bc, dy_a, dy_b, dyfr_a, dyfr_b, cotb_a, cotb_b, ci, ce, pre_s, *q_rows, *mats_a, *mats_b],
        2 * 1024 * (HC * DM + 5 * SEG * HC + 6 * NS * HC),
    )
    keep, send, dz = call(
        outer_kernel,
        [((ROWS, ALL), F32), ((ROWS, ALL), F32), ((NX, SEG, WIDE), BF16)],
        [((NX, NS, 2 * HC), BF16), ((2, ROWS, WIDE), F32)],
        [at, tokt, xfr, bc, ci, ce, pre_d, *p_rows, dxi, dci, dbi, g_out],
        2 * 1024 * (WIDE * DM + 4 * NS * HC),
    )
    got = move(send, "c", 1)
    terms = deal(at, 4, [keep, got], 96, ALL)
    whole, half = ((SEG, DM), F32), ((HALF, DM), F32)
    flops = 2 * SEG * WIDE * DM
    d2a, d2b = call(far_kernel, [half, half], [], [at, dz, wi, w_bc], flops)
    terms[0], dz_later = tie((terms[0], dz))
    d0, d1, d3 = call(tokens_kernel, [whole] * 3, [], [at, dz_later, wi, w_bc], 3 * flops)
    r_a, r_b = move(d2a, "x", 1), move(d2b, "x", -1)
    s1, s3 = call(pass_kernel, [whole, whole], [], [at, d1, d3, r_a, r_b])
    m1, m3 = move(s1, "x", 1), move(s3, "x", -1)
    terms = deal(at, 5, terms, 24, ALL)
    p0, p1, p2, p3, rows_out = call(
        cut_kernel, [((40, HC), F32)] * 4 + [((24, HC), F32)], [], [at, *terms]
    )
    pieces = [p0, move(p1, "x", 1), move(p2, "x", 2), move(p3, "x", 3)]
    lanes = NX * NY
    pairs = [(r * lanes + i, 2 * NZ * NY * (i % NX) + r * NY + i // NX) for r in range(2 * NZ) for i in range(lanes)]
    rows_out = lax.ppermute(rows_out, ("rec", "seq"), pairs)
    (square,) = call(square_kernel, [((8, 128), F32)], [], [at, *pieces])
    for axis in ("y", "z"):
        square = square + (move(square, axis, 1) + move(square, axis, 3) + move(square, axis, 2))
        square, rows_out = tie((square, rows_out))
    square, m1, m3, d0 = tie((square, m1, m3, d0))
    d_tok = (d0 + m1 + m3).astype(BF16)
    square = square + move(square, "c", 1)
    square, d_tok = tie((square, d_tok))
    all_in, all_bc, all_out = call(
        last_kernel,
        [((6, NX * HC), F32), ((6, 2 * NS), F32), ((12, DM), F32)],
        [((NX, 40, HC), F32)],
        [at, *pieces, rows_out, square],
    )
    return d_tok[None], all_in, all_bc, all_out


def solution(mesh):
    in_specs = (P("rec", "seq", None), P("rec", "seq", None), P("rec", None, "seq"), P(), P(), P())
    out_specs = (
        P("rec", "seq", None),
        P(("rec", "seq"), None),
        P(("rec", "seq"), None),
        P(("rec", "seq"), None),
    )
    return jax.shard_map(body, mesh=mesh, in_specs=in_specs, out_specs=out_specs, check_vma=False)
```
